256 devices in a mesh: dp: 8 (over z), seq: 32 (over y, x, core).
Axes of the slice: x: 4, y: 4, z: 8, core: 2. Of those that a mesh axis runs over, the one named last changes fastest.
Arguments:
- query_rows: bfloat16 [8, 4096, 512], P('dp', 'seq'), may hold values from -6 to 6
- key_rows: bfloat16 [8, 4096, 512], P('dp', 'seq'), may hold values from -6 to 6
- value_rows: bfloat16 [8, 4096, 512], P('dp', 'seq'), may hold values from -6 to 6
- inputs: bfloat16 [8, 4096, 1024], P('dp', 'seq'), may hold values from -6 to 6
- lengths: int32 [8], P('dp'), may hold values from 1024 to 4096, as said below
- out_weight: bfloat16 [512, 1024], replicated, may hold values from -0.25 to 0.25
- kernel: float32 [31, 1024], replicated, may hold values from -1 to 1
- norm_gain: float32 [1024], replicated, may hold values from 0.5 to 1.5
- norm_shift: float32 [1024], replicated, may hold values from -1 to 1
- cotangent: bfloat16 [8, 4096, 1024], P('dp', 'seq'), may hold values from -6 to 6
Outputs:
- output: bfloat16 [8, 4096, 1024], P('dp', 'seq')
- grad_inputs: bfloat16 [8, 4096, 1024], P('dp', 'seq')
- grad_query: bfloat16 [8, 4096, 512], P('dp', 'seq')
- grad_key: bfloat16 [8, 4096, 512], P('dp', 'seq')
- grad_value: bfloat16 [8, 4096, 512], P('dp', 'seq')
- grad_out_weight: float32 [512, 1024], replicated
- grad_kernel: float32 [31, 1024], replicated
- grad_gain: float32 [1024], replicated
- grad_shift: float32 [1024], replicated
The draws below stay inside these ranges and needn't reach their ends.
Inputs may be any that keep to these rules, and one draw needn't show every extreme that they name: `lengths`: the longest recording has exactly 4096 valid frames.
All inputs are finite; a program needn't handle non-finite values.
Results may differ from the reference program's by a relative error of at most 0.028.
Values may be sent and summed in bfloat16 or wider, within the bound.
A program may use at most 128 MiB of HBM per device.

```python
import math
import jax
import jax.numpy as jnp
from jax import lax

D = 1024
HEADS = 8
HEAD_DIM = 64
KERNEL = 31
SEQ_LEN = 4096
RECORDINGS = 8
ATT = 512


def draw_lengths(key, part):
    drawn_lengths = jax.random.randint(jax.random.fold_in(key, 1), (RECORDINGS,), SEQ_LEN // 4, SEQ_LEN + 1, dtype=jnp.int32)
    longest = jax.random.randint(jax.random.fold_in(key, 2), (), 0, RECORDINGS, dtype=jnp.int32)
    return jnp.where(jnp.arange(RECORDINGS, dtype=jnp.int32) == longest, SEQ_LEN, drawn_lengths).astype(jnp.int32)


def base_rows(key, stream_id):
    gaussian = jax.random.normal(jax.random.fold_in(key, stream_id), (RECORDINGS, SEQ_LEN, HEADS, HEAD_DIM), jnp.float32)
    return jnp.clip(1.75 * gaussian, -6.0, 6.0)


def draw_query_rows(key, part):
    values = base_rows(key, 31)
    return values.reshape(RECORDINGS, SEQ_LEN, ATT).astype(jnp.bfloat16)


def draw_key_rows(key, part):
    values = base_rows(key, 32)
    return values.reshape(RECORDINGS, SEQ_LEN, ATT).astype(jnp.bfloat16)


def draw_inputs(key, part):
    gaussian = jnp.clip(jax.random.normal(jax.random.fold_in(key, 11), (RECORDINGS, SEQ_LEN, D), jnp.float32), -4.0, 4.0)
    region_count = (SEQ_LEN + 31) // 32
    region_scale = jnp.exp(jax.random.uniform(jax.random.fold_in(key, 12), (RECORDINGS, region_count, 1), jnp.float32, math.log(0.04), math.log(0.6)))
    row_scale = jnp.repeat(region_scale, 32, axis=1)[:, :SEQ_LEN]
    column_scale = jnp.exp(jax.random.uniform(jax.random.fold_in(key, 13), (1, 1, D), jnp.float32, math.log(0.5), math.log(2.0)))
    values = gaussian * row_scale * column_scale
    return values.astype(jnp.bfloat16)


def draw_cotangent(key, part):
    key = jax.random.fold_in(key, 40)
    shape = (RECORDINGS, SEQ_LEN, D)
    noise = jnp.clip(jax.random.normal(jax.random.fold_in(key, 1), shape, jnp.float32), -4.0, 4.0)
    common = jax.random.uniform(jax.random.fold_in(key, 2), (1, 1, D), jnp.float32, -1.5, 1.5)
    return (noise + common).astype(jnp.bfloat16)


def level_of(key, extent, cuts, least, largest):
    gain, own = 1.0, jax.random.fold_in(key, 6)
    for position, parts in cuts:
        heights = jnp.exp(jax.random.uniform(jax.random.fold_in(own, position), (parts,), jnp.float32, least / len(cuts), largest / len(cuts)))
        gain = gain * jnp.repeat(heights, extent[position] // parts).reshape([-1 if axis == position else 1 for axis in range(len(extent))])
    return gain


def bell_draw(stream_key, shape, spread, most, cuts=(), kind=jnp.bfloat16):
    level = level_of(stream_key, shape, cuts, -0.22, 0.18) if cuts else 1.0
    drawn = jax.random.normal(stream_key, shape, jnp.float32) * spread * level
    return jnp.minimum(jnp.maximum(drawn, -most), most).astype(kind)


def setup_inputs(seed: int = 0) -> dict:
    splits = jax.random.split(jax.random.key(seed), 11)
    return {
        "query_rows": draw_query_rows(jax.random.fold_in(splits[10], 71), 0),
        "key_rows": draw_key_rows(jax.random.fold_in(splits[10], 71), 0),
        "value_rows": bell_draw(splits[2], (RECORDINGS, SEQ_LEN, ATT), 1.0, 6.0, ((0, 8), (1, 32))),
        "inputs": draw_inputs(jax.random.fold_in(splits[10], 71), 0),
        "lengths": draw_lengths(jax.random.fold_in(splits[10], 71), 0),
        "out_weight": bell_draw(splits[5], (ATT, D), ATT ** -0.5, 0.25),
        "kernel": bell_draw(splits[6], (KERNEL, D), KERNEL ** -0.5, 1.0, (), jnp.float32),
        "norm_gain": jnp.clip(1.0 + 0.1 * jax.random.normal(splits[7], (D,), jnp.float32), 0.5, 1.5),
        "norm_shift": jnp.clip(jax.random.uniform(splits[8], (D,), jnp.float32, -1.0, 1.0), -1.0, 1.0),
        "cotangent": draw_cotangent(jax.random.fold_in(splits[10], 71), 0),
    }


NEGATIVE = -1e+30
EPSILON = 1e-05

def split_heads(matrix):
    return matrix.astype(jnp.float32).reshape(matrix.shape[0], HEADS, HEAD_DIM)

def head_scores(query_block, key_block):
    return jnp.einsum('qhd,khd->hqk', split_heads(query_block), split_heads(key_block)) * HEAD_DIM ** (-0.5)

def attend_forward(packed):
    query_rows, key_rows, value_rows, length = packed
    key_live = jnp.arange(SEQ_LEN, dtype=jnp.int32) < length
    block_rows = math.gcd(SEQ_LEN, 512)

    def one_block(query_block):
        scores = jnp.where(key_live[None, None, :], head_scores(query_block, key_rows), NEGATIVE)
        highest = lax.optimization_barrier(jnp.max(scores, axis=-1))
        log_total = highest + jnp.log(lax.optimization_barrier(jnp.sum(jnp.exp(scores - highest[:, :, None]), axis=-1)))
        weights = jnp.where(key_live[None, None, :], jnp.exp(scores - log_total[:, :, None]), 0.0).astype(jnp.bfloat16)
        context = jnp.einsum('hqk,khd->qhd', weights.astype(jnp.float32), split_heads(value_rows))
        return (context.reshape(block_rows, ATT).astype(jnp.bfloat16), log_total)
    blocks = query_rows.reshape(SEQ_LEN // block_rows, block_rows, ATT)
    context, log_total = lax.map(one_block, blocks)
    return (context.reshape(SEQ_LEN, ATT), jnp.transpose(log_total, (1, 0, 2)).reshape(HEADS, SEQ_LEN))

def attend_backward(packed):
    query_rows, key_rows, value_rows, log_total, context, grad_context, length = packed
    key_live = jnp.arange(SEQ_LEN, dtype=jnp.int32) < length
    block_rows = math.gcd(SEQ_LEN, 512)
    score_scale = HEAD_DIM ** (-0.5)
    row_delta = jnp.transpose(lax.optimization_barrier(jnp.sum(split_heads(context) * split_heads(grad_context), axis=-1)))
    block_ids = jnp.arange(SEQ_LEN // block_rows, dtype=jnp.int32)

    def query_block(block_index):
        block_start = (block_index * block_rows).astype(jnp.int32)
        query_part = lax.dynamic_slice_in_dim(query_rows, block_start, block_rows, 0)
        grad_part = lax.dynamic_slice_in_dim(grad_context, block_start, block_rows, 0)
        total_part = lax.dynamic_slice_in_dim(log_total, block_start, block_rows, 1)
        delta_part = lax.dynamic_slice_in_dim(row_delta, block_start, block_rows, 1)
        weights = jnp.where(key_live[None, None, :], jnp.exp(head_scores(query_part, key_rows) - total_part[:, :, None]), 0.0)
        grad_weights = jnp.einsum('qhd,khd->hqk', split_heads(grad_part), split_heads(value_rows))
        grad_scores = (weights * (grad_weights - delta_part[:, :, None])).astype(jnp.bfloat16)
        grad_query = jnp.einsum('hqk,khd->qhd', grad_scores.astype(jnp.float32), split_heads(key_rows)) * score_scale
        return grad_query.reshape(block_rows, ATT).astype(jnp.bfloat16)

    def key_block(block_index):
        block_start = (block_index * block_rows).astype(jnp.int32)
        key_part = lax.dynamic_slice_in_dim(key_rows, block_start, block_rows, 0)
        value_part = lax.dynamic_slice_in_dim(value_rows, block_start, block_rows, 0)
        live_part = lax.dynamic_slice_in_dim(key_live, block_start, block_rows, 0)
        weights = jnp.where(live_part[None, None, :], jnp.exp(head_scores(query_rows, key_part) - log_total[:, :, None]), 0.0)
        grad_value = jnp.einsum('hqk,qhd->khd', weights.astype(jnp.bfloat16).astype(jnp.float32), split_heads(grad_context))
        grad_weights = jnp.einsum('qhd,khd->hqk', split_heads(grad_context), split_heads(value_part))
        grad_scores = (weights * (grad_weights - row_delta[:, :, None])).astype(jnp.bfloat16)
        grad_key = jnp.einsum('hqk,qhd->khd', grad_scores.astype(jnp.float32), split_heads(query_rows)) * score_scale
        return (grad_key.reshape(block_rows, ATT).astype(jnp.bfloat16), grad_value.reshape(block_rows, ATT).astype(jnp.bfloat16))
    grad_query = lax.map(query_block, block_ids).reshape(SEQ_LEN, ATT)
    grad_key, grad_value = lax.map(key_block, block_ids)
    return (grad_query, grad_key.reshape(SEQ_LEN, ATT), grad_value.reshape(SEQ_LEN, ATT))

def reference(query_rows, key_rows, value_rows, inputs, lengths, out_weight, kernel, norm_gain, norm_shift, cotangent):
    context, log_total = lax.map(attend_forward, (query_rows, key_rows, value_rows, lengths))
    frame_mask = (jnp.arange(SEQ_LEN, dtype=jnp.int32)[None, :] < lengths[:, None]).astype(jnp.float32)[:, :, None]
    projected = jnp.einsum('bta,ad->btd', context.astype(jnp.float32), out_weight.astype(jnp.float32))
    hidden = (frame_mask * (inputs.astype(jnp.float32) + projected)).astype(jnp.bfloat16)
    half_width = KERNEL // 2
    padded = jnp.pad(hidden.astype(jnp.float32), ((0, 0), (half_width, half_width), (0, 0)))
    conv_out = jnp.zeros((RECORDINGS, SEQ_LEN, D), jnp.float32)
    for offset in range(KERNEL):
        conv_out = conv_out + kernel[offset] * padded[:, offset:offset + SEQ_LEN]
    valid_count = jnp.sum(lengths).astype(jnp.float32)
    moment_mean = lax.optimization_barrier(jnp.sum(frame_mask * conv_out, axis=(0, 1))) / valid_count
    centered = conv_out - moment_mean
    variance = lax.optimization_barrier(jnp.sum(frame_mask * centered * centered, axis=(0, 1))) / valid_count
    inverse = lax.rsqrt(variance + EPSILON)
    normed = centered * inverse
    act_in = normed * norm_gain + norm_shift
    gate_part = jax.nn.sigmoid(act_in)
    output = (frame_mask * (hidden.astype(jnp.float32) + act_in * gate_part)).astype(jnp.bfloat16)
    grad_out = frame_mask * cotangent.astype(jnp.float32)
    grad_act = grad_out * gate_part * (1.0 + act_in * (1.0 - gate_part))
    grad_gain = lax.optimization_barrier(jnp.sum(grad_act * normed, axis=(0, 1)))
    grad_shift = lax.optimization_barrier(jnp.sum(grad_act, axis=(0, 1)))
    grad_conv = frame_mask * inverse * norm_gain * (grad_act - (grad_shift + normed * grad_gain) / valid_count)
    grad_kernel = jnp.stack([lax.optimization_barrier(jnp.sum(grad_conv * padded[:, offset:offset + SEQ_LEN], axis=(0, 1))) for offset in range(KERNEL)])
    grad_padded = jnp.pad(grad_conv, ((0, 0), (half_width, half_width), (0, 0)))
    grad_hidden = grad_out
    for offset in range(KERNEL):
        grad_hidden = grad_hidden + kernel[offset] * grad_padded[:, 2 * half_width - offset:2 * half_width - offset + SEQ_LEN]
    grad_inputs = (frame_mask * grad_hidden).astype(jnp.bfloat16)
    grad_out_weight = jnp.einsum('bta,btd->ad', context.astype(jnp.float32), grad_inputs.astype(jnp.float32))
    grad_context = jnp.einsum('btd,ad->bta', grad_inputs.astype(jnp.float32), out_weight.astype(jnp.float32)).astype(jnp.bfloat16)
    grad_query, grad_key, grad_value = lax.map(attend_backward, (query_rows, key_rows, value_rows, log_total, context, grad_context, lengths))
    return (output, grad_inputs, grad_query, grad_key, grad_value, grad_out_weight, grad_kernel, grad_gain, grad_shift)
```

```python
import functools

import jax
import jax.numpy as jnp
from jax import lax
from jax.experimental import pallas as pl
from jax.experimental.pallas import tpu as pltpu
from jax.sharding import PartitionSpec as P

KERNEL = 31
HALF = 15
HEAD_DIM = 64
ROWS = 128
HALO = 32
NEGATIVE = -1e30
EPSILON = 1e-05
KEY_BLOCK = 512
QUERY_BLOCK = 256
MESH = pl.DeviceIdType.MESH
F32 = jnp.float32
BF16 = jnp.bfloat16


def roll64(x):
    return pltpu.roll(x, 64, 1)


def low_lanes(shape):
    return lax.broadcasted_iota(jnp.int32, shape, 1) < 64


def split_units(x):
    rows = x.shape[0]
    units = x.reshape(rows // 32, 2, 16, 128)
    return units[:, 0].reshape(rows // 2, 128), units[:, 1].reshape(rows // 2, 128)


def join_units(first, second):
    rows = first.shape[0]
    first = first.reshape(rows // 16, 1, 16, 128)
    second = second.reshape(rows // 16, 1, 16, 128)
    return jnp.concatenate([first, second], axis=1).reshape(2 * rows, 128)


def pack_pair(x):
    first, second = split_units(x)
    low = low_lanes(first.shape)
    even = jnp.where(low, first, roll64(second))
    odd = jnp.where(low, roll64(first), second)
    return even, odd


def unpack_pair(even, odd):
    low = low_lanes(even.shape)
    return join_units(jnp.where(low, even, roll64(odd)), jnp.where(low, roll64(even), odd))


def unpack_low(packed):
    low = low_lanes(packed.shape)
    return join_units(jnp.where(low, packed, 0.0), jnp.where(low, roll64(packed), 0.0))


def unpack_high(packed):
    low = low_lanes(packed.shape)
    return join_units(jnp.where(low, 0.0, roll64(packed)), jnp.where(low, 0.0, packed))


def pack_low(x):
    first, second = split_units(x)
    return jnp.where(low_lanes(first.shape), first, roll64(second))


def pack_high(x):
    first, second = split_units(x)
    return jnp.where(low_lanes(first.shape), roll64(first), second)


def dot(a, b, dims=((1,), (0,))):
    return lax.dot_general(a, b, (dims, ((), ())), preferred_element_type=F32)


def shifted(x, amount):
    return x if amount == 0 else pltpu.roll(x, x.shape[0] - amount, 0)


def kernel(
    heads,
    seq,
    depth,
    length_ref,
    q_ref,
    k_ref,
    v_ref,
    x_hbm,
    cot_hbm,
    w_hbm,
    taps_hbm,
    gain_ref,
    shift_ref,
    out_ref,
    ginp_ref,
    gq_ref,
    gk_ref,
    gv_ref,
    gfin_ref,
    sums_ref,
    kv_send,
    q_send,
    kvbuf,
    qpk,
    k1,
    v1,
    kt,
    v1t,
    qaug,
    qcl,
    sbuf,
    pt,
    ctxh,
    linv,
    ctx_send,
    ctx_recv,
    x_ext,
    cot_ext,
    w_ref,
    taps_ref,
    ctx_ref,
    hid_ref,
    conv_ref,
    ga_ref,
    stat_a,
    stat_b,
    recv_a,
    recv_b,
    stat_c,
    recv_c,
    stat_d,
    recv_d,
    tot_ref,
    do_send,
    do_recv,
    doaug,
    docl,
    rbuf,
    dqt,
    dsend,
    precv,
    osend,
    kvrecv,
    dq_send,
    dq_recv,
    wsend,
    g0,
    gs1,
    g1,
    gs2,
    g2,
    load_sem,
    send,
    recv,
    ctx_sem,
    dq_sem,
    part_send,
    part_recv,
    own_sem,
):
    chips = seq // 2
    width = q_ref.shape[1]
    channels = out_ref.shape[1]
    chunks = channels // 128
    queries = ROWS * heads
    half_keys = chips * ROWS
    half_blocks = half_keys // KEY_BLOCK
    query_blocks = queries // QUERY_BLOCK
    padded = channels + 128
    ext = ROWS + 2 * HALO
    mid = ROWS + 32

    z = lax.axis_index("dp")
    me = lax.axis_index("seq")
    chip = me // 2
    core = me % 2
    other = 1 - core
    partner = (z, chip * 2 + other)
    group = (chip // heads) * 2 + core
    my_group = me // heads
    length = length_ref[0]

    def remote(src, dst, send_sem, recv_sem, device):
        return pltpu.make_async_remote_copy(
            src_ref=src, dst_ref=dst, send_sem=send_sem, recv_sem=recv_sem, device_id=device, device_id_type=MESH
        )

    def drain(ref, sem):
        pltpu.make_async_copy(ref, ref, sem).wait()

    barrier = pltpu.get_barrier_semaphore()

    @pl.loop(1, seq)
    def _(d):
        pl.semaphore_signal(barrier, inc=1, device_id=(z, (me + d) % seq), device_id_type=MESH)

    @pl.loop(1, depth)
    def _(d):
        for c in range(2):
            pl.semaphore_signal(
                barrier, inc=1, device_id=((z + d) % depth, chip * 2 + c), device_id_type=MESH
            )

    own_x = pltpu.make_async_copy(x_hbm, x_ext.at[pl.ds(HALO, ROWS)], load_sem.at[0])
    own_cot = pltpu.make_async_copy(cot_hbm, cot_ext.at[pl.ds(16, ROWS)], load_sem.at[1])
    load_w = pltpu.make_async_copy(w_hbm, w_ref, load_sem.at[2])
    load_taps = pltpu.make_async_copy(taps_hbm, taps_ref, load_sem.at[3])
    own_x.start()
    own_cot.start()
    load_w.start()
    load_taps.start()

    for pair in range(heads // 2):
        columns = slice(128 * pair, 128 * pair + 128)
        kp = k_ref[:, columns].astype(F32)
        vp = v_ref[:, columns].astype(F32)
        low = low_lanes(kp.shape)
        kv_send[2 * pair] = jnp.where(low, kp, roll64(vp)).astype(BF16)
        kv_send[2 * pair + 1] = jnp.where(low, roll64(kp), vp).astype(BF16)
        even, odd = pack_pair(q_ref[:, columns].astype(F32))
        q_send[2 * pair] = even.astype(BF16)
        q_send[2 * pair + 1] = odd.astype(BF16)

    pl.semaphore_wait(barrier, seq - 1 + 2 * (depth - 1))

    kv_slot = pl.ds(core * half_keys + chip * ROWS, ROWS)
    pltpu.make_async_copy(kv_send.at[chip % heads], kvbuf.at[kv_slot], recv.at[0]).start()

    @pl.loop(1, chips)
    def _(d):
        peer = (chip + d) % chips
        remote(
            kv_send.at[peer % heads], kvbuf.at[kv_slot], send.at[0], recv.at[0], (z, peer * 2 + core)
        ).start()

    def head_device(head):
        return ((my_group // 2) * heads + head) * 2 + my_group % 2

    def to_heads(source, target, index, self_index):
        head = chip % heads
        slot = me % heads
        mine = head_device(head) == me

        @pl.when(mine)
        def _():
            pltpu.make_async_copy(source.at[head], target.at[slot], recv.at[index]).start()

        @pl.when(jnp.logical_not(mine))
        def _():
            remote(
                source.at[head], target.at[slot], send.at[self_index], recv.at[index], (z, head_device(head))
            ).start()

        @pl.loop(1, heads)
        def _(d):
            to = (chip + d) % heads
            remote(
                source.at[to], target.at[slot], send.at[index], recv.at[index], (z, head_device(to))
            ).start()

    def to_heads_done(target, index, self_index):
        drain(target.at[pl.ds(0, heads - 1)], send.at[index])

        @pl.when(head_device(chip % heads) != me)
        def _():
            drain(target.at[0], send.at[self_index])

    to_heads(q_send, qpk, 1, 2)

    after = (z, (me + 1) % seq)
    before = (z, (me + seq - 1) % seq)
    own_x.wait()
    own_cot.wait()
    halo_copies = (
        remote(x_ext.at[pl.ds(ROWS, HALO)], x_ext.at[pl.ds(0, HALO)], send.at[3], recv.at[3], after),
        remote(x_ext.at[pl.ds(HALO, HALO)], x_ext.at[pl.ds(HALO + ROWS, HALO)], send.at[4], recv.at[4], before),
        remote(cot_ext.at[pl.ds(ROWS, 16)], cot_ext.at[pl.ds(0, 16)], send.at[5], recv.at[5], after),
        remote(cot_ext.at[pl.ds(16, 16)], cot_ext.at[pl.ds(16 + ROWS, 16)], send.at[6], recv.at[6], before),
    )
    for copy in halo_copies:
        copy.start()

    mine_half = kvbuf.at[pl.ds(core * half_keys, half_keys)]
    drain(mine_half, recv.at[0])
    forward = remote(mine_half, mine_half, send.at[7], recv.at[7], partner)
    forward.start()

    def prepare_keys(half):
        @pl.loop(0, half_blocks)
        def _(block):
            start = pl.multiple_of(half * half_keys + block * KEY_BLOCK, KEY_BLOCK)
            rows = pl.ds(start, KEY_BLOCK)
            kv = kvbuf[rows].astype(F32)
            lane = lax.broadcasted_iota(jnp.int32, kv.shape, 1)
            row = lax.broadcasted_iota(jnp.int32, kv.shape, 0) + block * KEY_BLOCK
            frame = ((row >> 7) * 2 + half) * ROWS + (row & 127)
            bias = jnp.where(jnp.logical_and(lane == 64, frame >= length), NEGATIVE, 0.0)
            keyed = jnp.where(lane < 64, kv, bias)
            valued = jnp.where(lane < 64, 1.0, kv)
            k1[rows] = keyed.astype(BF16)
            v1[rows] = valued.astype(BF16)
            kt[:, rows] = jnp.transpose(kv)[:64].astype(BF16) * BF16(0.125)
            v1t[:, rows] = jnp.transpose(valued).astype(BF16)

    prepare_keys(core)

    drain(qpk, recv.at[1])
    for index in range(heads):
        rows = slice(ROWS * index, ROWS * index + ROWS)
        part = unpack_low(qpk[index].astype(F32))
        lane = lax.broadcasted_iota(jnp.int32, part.shape, 1)
        qcl[rows] = (part * 0.125).astype(BF16)
        qaug[rows] = jnp.where(lane == 64, 1.0, part).astype(BF16)

    forward.wait_recv()
    prepare_keys(other)

    key_blocks = 2 * half_blocks
    factor = 0.125 * 1.4426950408889634

    def scores_step(query_block, block, highest):
        rows = pl.ds(pl.multiple_of(block * KEY_BLOCK, KEY_BLOCK), KEY_BLOCK)
        scores = dot(
            k1[rows], qaug[query_block * QUERY_BLOCK : (query_block + 1) * QUERY_BLOCK], ((1,), (1,))
        )
        sbuf[query_block % 2, rows] = scores
        return jnp.maximum(highest, jnp.max(scores.reshape(KEY_BLOCK // 8, 8, QUERY_BLOCK), axis=0))

    def weights_step(query_block, block, highest, total):
        rows = pl.ds(pl.multiple_of(block * KEY_BLOCK, KEY_BLOCK), KEY_BLOCK)
        weights = jnp.exp2((sbuf[query_block % 2, rows] - highest) * factor).astype(BF16)
        pt[rows, query_block * QUERY_BLOCK : (query_block + 1) * QUERY_BLOCK] = weights
        return total + dot(v1t[:, rows], weights)

    def context_finish(query_block, total):
        turned = jnp.transpose(total)
        low = low_lanes(turned.shape)
        inverse = 1.0 / jnp.where(low, 1.0, roll64(turned))
        context = jnp.where(low, 0.0, turned * inverse).astype(BF16).astype(F32)
        rows = slice(query_block * QUERY_BLOCK, (query_block + 1) * QUERY_BLOCK)
        linv[rows] = inverse
        ctxh[rows] = context
        half_rows = slice(query_block * QUERY_BLOCK // 2, (query_block + 1) * QUERY_BLOCK // 2)
        ctx_send[half_rows] = pack_high(context).astype(BF16)

    start_high = jnp.full((8, QUERY_BLOCK), NEGATIVE, F32)
    start_total = jnp.zeros((128, QUERY_BLOCK), F32)
    high = lax.fori_loop(0, key_blocks, lambda b, h: scores_step(0, b, h), start_high)
    for block in range(query_blocks):
        highest = jnp.max(high, axis=0, keepdims=True)
        if block + 1 < query_blocks:

            def both(b, carried, block=block, highest=highest):
                h, t = carried
                return scores_step(block + 1, b, h), weights_step(block, b, highest, t)

            high, total = lax.fori_loop(0, key_blocks, both, (start_high, start_total))
        else:
            total = lax.fori_loop(
                0,
                key_blocks,
                lambda b, t, block=block, highest=highest: weights_step(block, b, highest, t),
                start_total,
            )
        context_finish(block, total)

    my_head = chip % heads
    moves = [(-1, 0, 16, 80), (0, 0, 80, 16)]
    moves += [(i, 64 * i - 16, 96, 0) for i in range(1, heads - 1)]
    moves += [(heads - 1, 64 * (heads - 1) - 16, 80, 0), (heads, 64 * heads - 16, 16, 0)]

    def owner_of(i):
        return (group * heads + i + seq) % seq

    for index, (i, start, count, to) in enumerate(moves):
        source = ctx_send.at[pl.ds(start, count)]
        target = ctx_recv.at[my_head, pl.ds(to, count)]

        @pl.when(owner_of(i) == me)
        def _(source=source, target=target):
            pltpu.make_async_copy(source, target, recv.at[8]).start()

        @pl.when(owner_of(i) != me)
        def _(source=source, target=target, i=i, index=index):
            remote(source, target, ctx_sem.at[index], recv.at[8], (z, owner_of(i))).start()

    load_w.wait()
    load_taps.wait()
    for copy in halo_copies:
        copy.wait_recv()
    drain(ctx_recv, recv.at[8])

    for pair in range(heads // 2):
        ctx_ref[:, 128 * pair : 128 * pair + 128] = unpack_pair(
            ctx_recv[2 * pair].astype(F32), ctx_recv[2 * pair + 1].astype(F32)
        ).astype(BF16)

    def live(rows, first):
        frame = me * ROWS + first + lax.broadcasted_iota(jnp.int32, (rows, 128), 0)
        return jnp.logical_and(frame >= 0, frame < length)

    def column(chunk):
        return pl.ds(pl.multiple_of(chunk * 128, 128), 128)

    counted = jnp.clip(length - me * ROWS, 0, ROWS).astype(F32)

    @pl.loop(0, channels // 256)
    def _(chunk):
        columns = pl.ds(pl.multiple_of(chunk * 256, 256), 256)
        hidden = x_ext[:, columns].astype(F32) + dot(ctx_ref[...], w_ref[:, columns])
        mask = live(ext, -HALO)
        mask = jnp.concatenate([mask, mask], axis=1)
        hid_ref[:, columns] = jnp.where(mask, hidden, 0.0).astype(BF16).astype(F32)

    @pl.loop(0, chunks)
    def _(chunk):
        columns = column(chunk)
        hidden = hid_ref[:, columns]
        total = jnp.zeros((mid, 128), F32)
        for low in range(8):
            moved = shifted(hidden, low)
            for high_part in range(4):
                tap = 8 * high_part + low - 1
                if 0 <= tap < KERNEL:
                    total = total + taps_ref[tap : tap + 1, columns] * moved[8 * high_part : 8 * high_part + mid]
        conv_ref[:, columns] = total
        own = total[16 : 16 + ROWS]
        mask = live(ROWS, 0)
        summed = jnp.sum(jnp.where(mask, own, 0.0), axis=0, keepdims=True)
        mean = summed / jnp.maximum(counted, 1.0)
        spread = own - mean
        squares = jnp.sum(jnp.where(mask, spread * spread, 0.0), axis=0, keepdims=True)
        stat_a[pl.ds(chunk, 1)] = summed
        stat_a[pl.ds(chunks + chunk, 1)] = squares

    stat_a[2 * chunks :] = jnp.full((chunks, 128), counted, F32)

    def gather_first(source, target, index):
        slot = z * 2 + core
        target[slot] = source[...]
        remote(source, target.at[slot], send.at[index], recv.at[index], partner).start()

        @pl.loop(1, depth)
        def _(d):
            for c in range(2):
                remote(
                    source, target.at[slot], send.at[index], recv.at[index], ((z + d) % depth, chip * 2 + c)
                ).start()

        drain(target.at[pl.ds(0, 2 * depth - 1)], recv.at[index])

    def gather_second(source, target, index):
        target[chip] = source[...]

        @pl.loop(1, chips)
        def _(d):
            remote(
                source, target.at[chip], send.at[index], recv.at[index], (z, ((chip + d) % chips) * 2 + core)
            ).start()

        drain(target.at[pl.ds(0, chips - 1)], recv.at[index])

    def merged(gathered):
        sums = gathered[:, :chunks]
        squares = gathered[:, chunks : 2 * chunks]
        counts = gathered[:, 2 * chunks :]
        count = jnp.sum(counts, axis=0)
        total = jnp.sum(sums, axis=0)
        mean = total / jnp.maximum(count, 1.0)
        shift = sums / jnp.maximum(counts, 1.0) - mean[None]
        return total, jnp.sum(squares, axis=0) + jnp.sum(counts * shift * shift, axis=0), count, mean

    gather_first(stat_a, recv_a, 9)
    total, squares, count, mean = merged(recv_a[...])
    stat_b[:chunks] = total
    stat_b[chunks : 2 * chunks] = squares
    stat_b[2 * chunks :] = count
    gather_second(stat_b, recv_b, 10)
    total, squares, count, mean = merged(recv_b[...])
    tot_ref[:chunks] = mean
    tot_ref[chunks : 2 * chunks] = lax.rsqrt(squares / count + EPSILON)
    tot_ref[2 * chunks : 3 * chunks] = 1.0 / count

    @pl.loop(0, chunks)
    def _(chunk):
        columns = column(chunk)
        mean = tot_ref[pl.ds(chunk, 1)]
        inverse = tot_ref[pl.ds(chunks + chunk, 1)]
        normed = (conv_ref[:, columns] - mean) * inverse
        conv_ref[:, columns] = normed
        act = normed * gain_ref[:, columns] + shift_ref[:, columns]
        gate = 1.0 / (1.0 + jnp.exp(-act))
        grad_out = jnp.where(live(mid, -16), cot_ext[:, columns].astype(F32), 0.0)
        grad_act = grad_out * gate * (1.0 + act * (1.0 - gate))
        ga_ref[:, columns] = grad_act
        own = grad_act[16 : 16 + ROWS]
        stat_c[pl.ds(chunk, 1)] = jnp.sum(own * normed[16 : 16 + ROWS], axis=0, keepdims=True)
        stat_c[pl.ds(chunks + chunk, 1)] = jnp.sum(own, axis=0, keepdims=True)
        gated = (act * gate)[16 : 16 + ROWS]
        hidden = hid_ref[HALO : HALO + ROWS, columns]
        out_ref[:, columns] = jnp.where(live(ROWS, 0), hidden + gated, 0.0).astype(BF16)

    gather_first(stat_c, recv_c, 11)
    stat_d[...] = jnp.sum(recv_c[...], axis=0)
    gather_second(stat_d, recv_d, 12)
    sums_ref[...] = jnp.sum(recv_d[...], axis=0)

    @pl.loop(0, chunks)
    def _(chunk):
        columns = column(chunk)
        inverse = tot_ref[pl.ds(chunks + chunk, 1)]
        per_count = tot_ref[pl.ds(2 * chunks + chunk, 1)]
        gain_sum = sums_ref[pl.ds(chunk, 1)] * per_count
        shift_sum = sums_ref[pl.ds(chunks + chunk, 1)] * per_count
        grad_act = ga_ref[:, columns]
        grad_conv = (inverse * gain_ref[:, columns]) * (grad_act - (shift_sum + conv_ref[:, columns] * gain_sum))
        grad_conv = jnp.where(live(mid, -16), grad_conv, 0.0)
        ga_ref[:, columns] = grad_conv
        total = cot_ext[16 : 16 + ROWS, columns].astype(F32)
        for low in range(8):
            moved = shifted(grad_conv, low)
            for high_part in range(4):
                tap = 31 - (8 * high_part + low)
                if 0 <= tap < KERNEL:
                    total = total + taps_ref[tap : tap + 1, columns] * moved[8 * high_part : 8 * high_part + ROWS]
        ginp_ref[:, columns] = jnp.where(live(ROWS, 0), total, 0.0).astype(BF16)

    @pl.loop(0, heads // 2)
    def _(pair):
        rows = pl.ds(pl.multiple_of(pair * 128, 128), 128)
        grad_context = dot(ginp_ref[...], w_ref[rows], ((1,), (1,))).astype(BF16).astype(F32)
        even, odd = pack_pair(grad_context)
        do_send[2 * pair] = even.astype(BF16)
        do_send[2 * pair + 1] = odd.astype(BF16)

    to_heads(do_send, do_recv, 13, 14)

    own_context = jnp.transpose(ctx_ref[HALO : HALO + ROWS].astype(F32)).astype(BF16)

    @pl.loop(0, channels // 256)
    def _(chunk):
        columns = pl.ds(pl.multiple_of(chunk * 256, 256), 256)
        terms = dot(own_context, ginp_ref[:, columns]).astype(BF16)
        wsend[:, :, :, columns] = terms.reshape(2, chips, 16, 256)

    wsend[:, :, :, channels:] = jnp.zeros((2, chips, 16, 128), BF16)

    @pl.loop(0, chunks)
    def _(chunk):
        columns = column(chunk)
        grad_conv = ga_ref[16 : 16 + ROWS, columns]
        hidden = hid_ref[16:, columns]
        found = [None] * 32
        for low in range(8):
            moved = shifted(hidden, low)
            for high_part in range(4):
                tap = 8 * high_part + low - 1
                if 0 <= tap < KERNEL:
                    terms = grad_conv * moved[8 * high_part : 8 * high_part + ROWS]
                    found[tap] = jnp.sum(terms, axis=0, keepdims=True)
        found[31] = jnp.zeros((1, 128), F32)
        stacked = jnp.concatenate(found, axis=0).astype(BF16)
        wsend[0, pl.ds(chunk, 1), :, channels:] = stacked[:16].reshape(1, 16, 128)
        wsend[1, pl.ds(chunk, 1), :, channels:] = stacked[16:].reshape(1, 16, 128)

    stage0 = remote(wsend.at[other], g0, send.at[15], recv.at[15], partner)
    stage0.start()

    drain(do_recv, recv.at[13])
    for index in range(heads):
        rows = slice(ROWS * index, ROWS * index + ROWS)
        scaled = (unpack_high(do_recv[index].astype(F32)) * linv[rows]).astype(BF16)
        docl[rows] = scaled
        scaled = scaled.astype(F32)
        delta = jnp.sum(ctxh[rows] * scaled, axis=1, keepdims=True)
        first = delta.astype(BF16).astype(F32)
        rest = delta - first
        lane = lax.broadcasted_iota(jnp.int32, scaled.shape, 1)
        doaug[rows] = jnp.where(lane == 0, -first, jnp.where(lane == 1, -rest, scaled)).astype(BF16)

    dqt[...] = jnp.zeros_like(dqt)

    def part_copy(turn):
        rows = pl.ds(pl.multiple_of(turn * KEY_BLOCK, KEY_BLOCK), KEY_BLOCK)
        return remote(dsend.at[rows], precv.at[rows], part_send.at[turn], part_recv.at[turn], partner)

    def stage1():
        stage0.wait_recv()

        @pl.loop(0, chips)
        def _(i):
            gs1[i] = (wsend[core, i].astype(F32) + g0[i].astype(F32)).astype(BF16)

        g1[chip] = gs1[chip]

        @pl.loop(1, chips)
        def _(d):
            peer = (chip + d) % chips
            remote(gs1.at[peer], g1.at[chip], send.at[16], recv.at[16], (z, peer * 2 + core)).start()

    def stage2():
        drain(g1.at[pl.ds(0, chips - 1)], recv.at[16])
        total = g1[0].astype(F32)
        for i in range(1, chips):
            total = total + g1[i].astype(F32)
        total = total.astype(BF16)
        gs2[...] = total
        g2[z] = total

        @pl.loop(1, depth)
        def _(d):
            remote(gs2, g2.at[z], send.at[17], recv.at[17], ((z + d) % depth, me)).start()

    def stage3():
        drain(g2.at[pl.ds(0, depth - 1)], recv.at[17])
        total = g2[0].astype(F32)
        for i in range(1, depth):
            total = total + g2[i].astype(F32)
        gfin_ref[core, chip] = total.astype(BF16)

        @pl.loop(1, chips)
        def _(d):
            peer = (chip + d) % chips
            piece = gfin_ref.at[core, chip]
            remote(piece, piece, send.at[18], recv.at[18], (z, peer * 2 + core)).start()

    def stage4_copy():
        piece = gfin_ref.at[core]
        return remote(piece, piece, send.at[19], recv.at[19], partner)

    def stage4():
        drain(gfin_ref.at[core, pl.ds(0, chips - 1)], recv.at[18])
        stage4_copy().start()

    steps = 2 * half_blocks

    @pl.loop(0, steps)
    def _(step):
        half = jnp.where(step < half_blocks, other, core)
        turn = step % half_blocks
        start = pl.multiple_of(half * half_keys + turn * KEY_BLOCK, KEY_BLOCK)
        rows = pl.ds(start, KEY_BLOCK)
        turn_rows = pl.ds(pl.multiple_of(turn * KEY_BLOCK, KEY_BLOCK), KEY_BLOCK)
        terms = jnp.zeros((KEY_BLOCK, 128), F32)
        for block in range(query_blocks):
            part = slice(block * QUERY_BLOCK, (block + 1) * QUERY_BLOCK)
            weights = pt[rows, part]
            grads = dot(v1[rows], doaug[part], ((1,), (1,))).astype(BF16)
            scores = weights * grads
            terms = terms + dot(scores, qcl[part]) + dot(weights, docl[part])
            dqt[:, part] += dot(kt[:, rows], scores)
        rbuf[...] = terms

        @pl.when(step < half_blocks)
        def _():
            dsend[turn_rows] = rbuf[...].astype(BF16)
            part_copy(turn).start()

        @pl.when(step >= half_blocks)
        def _():
            part_copy(turn).wait_recv()
            osend[turn_rows] = (rbuf[...] + precv[turn_rows].astype(F32)).astype(BF16)
            for i in range(KEY_BLOCK // ROWS):
                to = turn * (KEY_BLOCK // ROWS) + i
                source = osend.at[pl.ds(pl.multiple_of(to * ROWS, ROWS), ROWS)]

                @pl.when(to == chip)
                def _():
                    pltpu.make_async_copy(source, kvrecv.at[chip], recv.at[20]).start()

                @pl.when(to != chip)
                def _():
                    remote(source, kvrecv.at[chip], own_sem, recv.at[20], (z, to * 2 + core)).start()

        for number, stage in enumerate((stage1, stage2, stage3)):

            @pl.when(step == (number * steps) // 4 + max(steps // 4 - 1, 0))
            def _(stage=stage):
                stage()

    @pl.loop(0, query_blocks)
    def _(block):
        part = pl.ds(pl.multiple_of(block * QUERY_BLOCK, QUERY_BLOCK), QUERY_BLOCK)
        turned = dqt[:, part]
        turned = jnp.transpose(jnp.concatenate([turned, jnp.zeros_like(turned)], axis=0))
        half_part = pl.ds(pl.multiple_of(block * QUERY_BLOCK // 2, QUERY_BLOCK // 2), QUERY_BLOCK // 2)
        dq_send[half_part] = pack_low(turned).astype(BF16)

    for i in range(heads):
        source = dq_send.at[pl.ds(64 * i, 64)]
        target = dq_recv.at[my_head]

        @pl.when(owner_of(i) == me)
        def _(source=source, target=target):
            pltpu.make_async_copy(source, target, recv.at[21]).start()

        @pl.when(owner_of(i) != me)
        def _(source=source, target=target, i=i):
            remote(source, target, dq_sem.at[i], recv.at[21], (z, owner_of(i))).start()

    stage4()

    drain(kvrecv, recv.at[20])
    for pair in range(heads // 2):
        columns = slice(128 * pair, 128 * pair + 128)
        even = kvrecv[2 * pair].astype(F32) + kvrecv[2 * pair + heads].astype(F32)
        odd = kvrecv[2 * pair + 1].astype(F32) + kvrecv[2 * pair + 1 + heads].astype(F32)
        low = low_lanes(even.shape)
        gk_ref[:, columns] = jnp.where(low, even, roll64(odd)).astype(BF16)
        gv_ref[:, columns] = jnp.where(low, roll64(even), odd).astype(BF16)

    drain(dq_recv, recv.at[21])
    for pair in range(heads // 2):
        gq_ref[:, 128 * pair : 128 * pair + 128] = unpack_pair(
            dq_recv[2 * pair].astype(F32), dq_recv[2 * pair + 1].astype(F32)
        ).astype(BF16)

    drain(kvbuf.at[pl.ds(0, (chips - 1) * ROWS)], send.at[0])
    to_heads_done(qpk, 1, 2)
    for copy in halo_copies:
        copy.wait_send()
    forward.wait_send()
    for index, (i, start, count, to) in enumerate(moves):

        @pl.when(owner_of(i) != me)
        def _(index=index, start=start, count=count):
            drain(ctx_send.at[pl.ds(start, count)], ctx_sem.at[index])

    drain(recv_a.at[pl.ds(0, 2 * depth - 1)], send.at[9])
    drain(recv_b.at[pl.ds(0, chips - 1)], send.at[10])
    drain(recv_c.at[pl.ds(0, 2 * depth - 1)], send.at[11])
    drain(recv_d.at[pl.ds(0, chips - 1)], send.at[12])
    to_heads_done(do_recv, 13, 14)
    stage0.wait_send()
    drain(g1.at[pl.ds(0, chips - 1)], send.at[16])
    drain(g2.at[pl.ds(0, depth - 1)], send.at[17])
    drain(gfin_ref.at[core, pl.ds(0, chips - 1)], send.at[18])

    @pl.loop(0, half_blocks)
    def _(turn):
        part_copy(turn).wait_send()

    drain(kvrecv.at[pl.ds(0, chips - 1)], own_sem)
    for i in range(heads):

        @pl.when(owner_of(i) != me)
        def _(i=i):
            drain(dq_send.at[pl.ds(64 * i, 64)], dq_sem.at[i])

    last = stage4_copy()
    last.wait_send()
    rest = gfin_ref.at[other]
    drain(rest, recv.at[19])


def shards(
    depth,
    query_rows,
    key_rows,
    value_rows,
    inputs,
    lengths,
    out_weight,
    taps,
    norm_gain,
    norm_shift,
    cotangent,
):
    seq = lax.axis_size("seq")
    heads = seq // 4
    chips = seq // 2
    width = query_rows.shape[2]
    channels = inputs.shape[2]
    chunks = channels // 128
    queries = ROWS * heads
    keys = seq * ROWS
    ext = ROWS + 2 * HALO
    mid = ROWS + 32
    padded = channels + 128
    vmem = pltpu.VMEM
    scratch = [
        vmem((heads, ROWS, 128), BF16),
        vmem((heads, 64, 128), BF16),
        vmem((keys, 128), BF16),
        vmem((heads, 64, 128), BF16),
        vmem((keys, 128), BF16),
        vmem((keys, 128), BF16),
        vmem((64, keys), BF16),
        vmem((128, keys), BF16),
        vmem((queries, 128), BF16),
        vmem((queries, 128), BF16),
        vmem((2, keys, QUERY_BLOCK), F32),
        vmem((keys, queries), BF16),
        vmem((queries, 128), F32),
        vmem((queries, 128), F32),
        vmem((queries // 2, 128), BF16),
        vmem((heads, ext // 2, 128), BF16),
        vmem((ext, channels), BF16),
        vmem((mid, channels), BF16),
        vmem((width, channels), BF16),
        vmem((KERNEL, channels), F32),
        vmem((ext, width), BF16),
        vmem((ext, channels), F32),
        vmem((mid, channels), F32),
        vmem((mid, channels), F32),
        vmem((3 * chunks, 128), F32),
        vmem((3 * chunks, 128), F32),
        vmem((2 * depth, 3 * chunks, 128), F32),
        vmem((chips, 3 * chunks, 128), F32),
        vmem((2 * chunks, 128), F32),
        vmem((2 * depth, 2 * chunks, 128), F32),
        vmem((2 * chunks, 128), F32),
        vmem((chips, 2 * chunks, 128), F32),
        vmem((3 * chunks, 128), F32),
        vmem((heads, 64, 128), BF16),
        vmem((heads, 64, 128), BF16),
        vmem((queries, 128), BF16),
        vmem((queries, 128), BF16),
        vmem((KEY_BLOCK, 128), F32),
        vmem((64, queries), F32),
        vmem((keys // 2, 128), BF16),
        vmem((keys // 2, 128), BF16),
        vmem((keys // 2, 128), BF16),
        vmem((chips, ROWS, 128), BF16),
        vmem((queries // 2, 128), BF16),
        vmem((heads, 64, 128), BF16),
        vmem((2, chips, 16, padded), BF16),
        vmem((chips, 16, padded), BF16),
        vmem((chips, 16, padded), BF16),
        vmem((chips, 16, padded), BF16),
        vmem((16, padded), BF16),
        vmem((depth, 16, padded), BF16),
        pltpu.SemaphoreType.DMA((4,)),
        pltpu.SemaphoreType.DMA((22,)),
        pltpu.SemaphoreType.DMA((22,)),
        pltpu.SemaphoreType.DMA((heads + 2,)),
        pltpu.SemaphoreType.DMA((heads,)),
        pltpu.SemaphoreType.DMA((keys // 2 // KEY_BLOCK,)),
        pltpu.SemaphoreType.DMA((keys // 2 // KEY_BLOCK,)),
        pltpu.SemaphoreType.DMA,
    ]
    in_vmem = pl.BlockSpec(memory_space=pltpu.VMEM)
    anywhere = pl.BlockSpec(memory_space=pl.ANY)
    output, grad_inputs, grad_query, grad_key, grad_value, packed, sums = pl.pallas_call(
        functools.partial(kernel, heads, seq, depth),
        out_shape=(
            jax.ShapeDtypeStruct((ROWS, channels), BF16),
            jax.ShapeDtypeStruct((ROWS, channels), BF16),
            jax.ShapeDtypeStruct((ROWS, width), BF16),
            jax.ShapeDtypeStruct((ROWS, width), BF16),
            jax.ShapeDtypeStruct((ROWS, width), BF16),
            jax.ShapeDtypeStruct((2, chips, 16, padded), BF16),
            jax.ShapeDtypeStruct((2 * chunks, 128), F32),
        ),
        in_specs=[pl.BlockSpec(memory_space=pltpu.SMEM), in_vmem, in_vmem, in_vmem]
        + [anywhere] * 4
        + [in_vmem] * 2,
        out_specs=(in_vmem,) * 7,
        scratch_shapes=scratch,
        compiler_params=pltpu.CompilerParams(
            collective_id=0, has_side_effects=True, vmem_limit_bytes=60 * 1024 * 1024
        ),
    )(
        lengths,
        query_rows[0],
        key_rows[0],
        value_rows[0],
        inputs[0],
        cotangent[0],
        out_weight,
        taps,
        norm_gain[None],
        norm_shift[None],
    )
    grad_out_weight = packed[..., :channels].reshape(width, channels).astype(F32)
    tap_terms = packed[:, :chunks, :, channels:].astype(F32)
    grad_kernel = jnp.transpose(tap_terms, (0, 2, 1, 3)).reshape(32, channels)[:KERNEL]
    return (
        output[None],
        grad_inputs[None],
        grad_query[None],
        grad_key[None],
        grad_value[None],
        grad_out_weight,
        grad_kernel,
        sums[:chunks].reshape(channels),
        sums[chunks:].reshape(channels),
    )


def solution(mesh):
    rows = P("dp", "seq", None)
    return jax.shard_map(
        functools.partial(shards, mesh.shape["dp"]),
        mesh=mesh,
        in_specs=(rows, rows, rows, rows, P("dp"), P(), P(), P(), P(), rows),
        out_specs=(rows, rows, rows, rows, rows, P(), P(), P(), P()),
        check_vma=False,
    )
```

```python
import functools

import jax
import jax.numpy as jnp
from jax import lax
from jax.experimental import pallas as pl
from jax.experimental.pallas import tpu as pltpu
from jax.sharding import PartitionSpec as P

KERNEL = 31
HALF = 15
HEAD_DIM = 64
ROWS = 128
HALO = 32
NEGATIVE = -1e30
EPSILON = 1e-05
PIECES = 3
MESH = pl.DeviceIdType.MESH
F32 = jnp.float32
BF16 = jnp.bfloat16


def roll64(x):
    return pltpu.roll(x, 64, 1)


def low_lanes(shape):
    return lax.broadcasted_iota(jnp.int32, shape, 1) < 64


def split_units(x):
    rows = x.shape[0]
    units = x.reshape(rows // 32, 2, 16, 128)
    return units[:, 0].reshape(rows // 2, 128), units[:, 1].reshape(rows // 2, 128)


def join_units(first, second):
    rows = first.shape[0]
    first = first.reshape(rows // 16, 1, 16, 128)
    second = second.reshape(rows // 16, 1, 16, 128)
    return jnp.concatenate([first, second], axis=1).reshape(2 * rows, 128)


def pack_pair(x):
    first, second = split_units(x)
    low = low_lanes(first.shape)
    even = jnp.where(low, first, roll64(second))
    odd = jnp.where(low, roll64(first), second)
    return even, odd


def unpack_pair(even, odd):
    low = low_lanes(even.shape)
    return join_units(jnp.where(low, even, roll64(odd)), jnp.where(low, roll64(even), odd))


def unpack_low(packed):
    low = low_lanes(packed.shape)
    return join_units(jnp.where(low, packed, 0.0), jnp.where(low, roll64(packed), 0.0))


def unpack_high(packed):
    low = low_lanes(packed.shape)
    return join_units(jnp.where(low, 0.0, roll64(packed)), jnp.where(low, 0.0, packed))


def pack_low(x):
    first, second = split_units(x)
    return jnp.where(low_lanes(first.shape), first, roll64(second))


def pack_high(x):
    first, second = split_units(x)
    return jnp.where(low_lanes(first.shape), roll64(first), second)


def dot(a, b, dims=((1,), (0,))):
    return lax.dot_general(a, b, (dims, ((), ())), preferred_element_type=F32)


def shifted(x, amount):
    return x if amount == 0 else pltpu.roll(x, x.shape[0] - amount, 0)


def kernel(
    heads,
    seq,
    depth,
    length_ref,
    q_hbm,
    k_hbm,
    v_hbm,
    x_hbm,
    cot_hbm,
    w_hbm,
    taps_hbm,
    gain_hbm,
    shift_hbm,
    out_hbm,
    ginp_hbm,
    gq_hbm,
    gk_hbm,
    gv_hbm,
    gfin_ref,
    sums_ref,
    q_ref,
    k_ref,
    v_ref,
    gain_ref,
    shift_ref,
    out_ref,
    ginp_ref,
    gq_ref,
    gk_ref,
    gv_ref,
    len_send,
    len_recv,
    cmask_ref,
    cgrad_ref,
    cnorm_ref,
    kv_send,
    q_send,
    kvbuf,
    qpk,
    k1,
    v1,
    kt,
    v1t,
    qaug,
    qcl,
    sbuf,
    pt,
    ctxh,
    linv,
    ctx_send,
    ctx_recv,
    x_ext,
    cot_ext,
    w_ref,
    taps_ref,
    ctx_ref,
    hid_ref,
    conv_ref,
    ga_ref,
    stat_a,
    stat_b,
    recv_a,
    recv_b,
    stat_c,
    recv_c,
    stat_d,
    recv_d,
    tot_ref,
    do_send,
    do_recv,
    doaug,
    docl,
    rbuf,
    dqt,
    dsend,
    precv,
    osend,
    kvrecv,
    dq_send,
    dq_recv,
    wsend,
    g0,
    gs1,
    g1,
    gs2,
    g2,
    load_sem,
    send,
    recv,
    ctx_sem,
    dq_sem,
    part_send,
    part_recv,
    own_sem,
    piece_send,
    piece_recv,
    write_sem,
):
    chips = seq // 2
    width = q_ref.shape[1]
    channels = out_ref.shape[1]
    chunks = channels // 128
    queries = ROWS * heads
    half_keys = chips * ROWS
    forward_block = half_keys // 2
    backward_block = half_keys // 4
    query_block = min(queries, 512)
    query_blocks = queries // query_block
    padded = channels + 128
    piece_width = padded // PIECES
    ext = ROWS + 2 * HALO
    mid = ROWS + 32

    z = lax.axis_index("dp")
    me = lax.axis_index("seq")
    chip = me // 2
    core = me % 2
    other = 1 - core
    partner = (z, chip * 2 + other)
    group = (chip // heads) * 2 + core
    my_group = me // heads
    length = length_ref[0]

    def remote(src, dst, send_sem, recv_sem, device):
        return pltpu.make_async_remote_copy(
            src_ref=src, dst_ref=dst, send_sem=send_sem, recv_sem=recv_sem, device_id=device, device_id_type=MESH
        )

    def drain(ref, sem):
        pltpu.make_async_copy(ref, ref, sem).wait()

    pending = {}

    def later(name, ref, sem):
        pending[name] = lambda: drain(ref, sem)

    def settle(*names):
        for name in names or tuple(pending):
            pending.pop(name)()

    barrier = pltpu.get_barrier_semaphore()

    @pl.loop(1, seq)
    def _(d):
        pl.semaphore_signal(barrier, inc=1, device_id=(z, (me + d) % seq), device_id_type=MESH)

    @pl.loop(1, depth)
    def _(d):
        for c in range(2):
            pl.semaphore_signal(
                barrier, inc=1, device_id=((z + d) % depth, chip * 2 + c), device_id_type=MESH
            )

    loads = (
        ("k", k_hbm, k_ref),
        ("v", v_hbm, v_ref),
        ("q", q_hbm, q_ref),
        ("x", x_hbm, x_ext.at[pl.ds(HALO, ROWS)]),
        ("cot", cot_hbm, cot_ext.at[pl.ds(16, ROWS)]),
        ("w", w_hbm, w_ref),
        ("taps", taps_hbm, taps_ref),
        ("gain", gain_hbm, gain_ref),
        ("shift", shift_hbm, shift_ref),
    )
    for index, (name, source, target) in enumerate(loads):
        copy = pltpu.make_async_copy(source, target, load_sem.at[index])
        copy.start()
        pending[name] = copy.wait

    len_send[...] = jnp.full((8, 128), length.astype(F32), F32)
    settle("k", "v", "q")
    for pair in range(heads // 2):
        columns = slice(128 * pair, 128 * pair + 128)
        kp = k_ref[:, columns].astype(F32)
        vp = v_ref[:, columns].astype(F32)
        low = low_lanes(kp.shape)
        kv_send[2 * pair] = jnp.where(low, kp, roll64(vp)).astype(BF16)
        kv_send[2 * pair + 1] = jnp.where(low, roll64(kp), vp).astype(BF16)
        even, odd = pack_pair(q_ref[:, columns].astype(F32))
        q_send[2 * pair] = even.astype(BF16)
        q_send[2 * pair + 1] = odd.astype(BF16)

    pl.semaphore_wait(barrier, seq - 1 + 2 * (depth - 1))

    def kv_slot(d):
        return kvbuf.at[pl.ds(pl.multiple_of(core * half_keys + d * ROWS, ROWS), ROWS)]

    def send_keys(first, last, index):
        @pl.loop(first, last)
        def _(d):
            peer = (chip + d) % chips
            remote(kv_send.at[peer % heads], kv_slot(d), send.at[index], recv.at[index], (z, peer * 2 + core)).start()

    def quarter(half, index):
        return kvbuf.at[
            pl.ds(pl.multiple_of(half * half_keys + index * forward_block, forward_block), forward_block)
        ]

    some = chips // 2
    pltpu.make_async_copy(kv_send.at[chip % heads], kv_slot(0), recv.at[0]).start()
    send_keys(1, some, 0)
    later("keys 0 in", quarter(core, 0), recv.at[0])
    later("keys 0 out", kvbuf.at[pl.ds(0, (some - 1) * ROWS)], send.at[0])

    def head_device(head):
        return ((my_group // 2) * heads + head) * 2 + my_group % 2

    def to_heads(source, target, index, self_index):
        head = chip % heads
        slot = me % heads
        mine = head_device(head) == me

        @pl.when(mine)
        def _():
            pltpu.make_async_copy(source.at[head], target.at[slot], recv.at[index]).start()

        @pl.when(jnp.logical_not(mine))
        def _():
            remote(
                source.at[head], target.at[slot], send.at[self_index], recv.at[index], (z, head_device(head))
            ).start()

        @pl.loop(1, heads)
        def _(d):
            to = (chip + d) % heads
            remote(
                source.at[to], target.at[slot], send.at[index], recv.at[index], (z, head_device(to))
            ).start()

        def own_done():
            @pl.when(jnp.logical_not(mine))
            def _():
                drain(target.at[0], send.at[self_index])

        later(f"heads {index} in", target, recv.at[index])
        later(f"heads {index} out", target.at[pl.ds(0, heads - 1)], send.at[index])
        pending[f"heads {index} own"] = own_done

    to_heads(q_send, qpk, 1, 2)

    send_keys(some, chips, 22)
    later("keys 1 in", quarter(core, 1), recv.at[22])
    later("keys 1 out", kvbuf.at[pl.ds(0, some * ROWS)], send.at[22])

    len_recv[z] = len_send[...]

    @pl.loop(1, depth)
    def _(d):
        remote(len_send, len_recv.at[z], send.at[23], recv.at[23], ((z + d) % depth, me)).start()

    later("lengths in", len_recv.at[pl.ds(0, depth - 1)], recv.at[23])
    later("lengths out", len_recv.at[pl.ds(0, depth - 1)], send.at[23])

    after = (z, (me + 1) % seq)
    before = (z, (me + seq - 1) % seq)
    settle("x", "cot")
    halo_copies = (
        remote(x_ext.at[pl.ds(ROWS, HALO)], x_ext.at[pl.ds(0, HALO)], send.at[3], recv.at[3], after),
        remote(x_ext.at[pl.ds(HALO, HALO)], x_ext.at[pl.ds(HALO + ROWS, HALO)], send.at[4], recv.at[4], before),
        remote(cot_ext.at[pl.ds(ROWS, 16)], cot_ext.at[pl.ds(0, 16)], send.at[5], recv.at[5], after),
        remote(cot_ext.at[pl.ds(16, 16)], cot_ext.at[pl.ds(16 + ROWS, 16)], send.at[6], recv.at[6], before),
    )
    for index, copy in enumerate(halo_copies):
        copy.start()
        pending[f"halo {index} in"] = copy.wait_recv
        pending[f"halo {index} out"] = copy.wait_send

    def prepare_keys(half, index):
        rows_at_once = min(forward_block, 512)

        @pl.loop(0, forward_block // rows_at_once)
        def _(part):
            first = index * forward_block + part * rows_at_once
            rows = pl.ds(pl.multiple_of(half * half_keys + first, rows_at_once), rows_at_once)
            kv = kvbuf[rows].astype(F32)
            lane = lax.broadcasted_iota(jnp.int32, kv.shape, 1)
            row = lax.broadcasted_iota(jnp.int32, kv.shape, 0) + first
            source = chip - (row >> 7)
            source = jnp.where(source < 0, source + chips, source)
            frame = (source * 2 + half) * ROWS + (row & 127)
            bias = jnp.where(jnp.logical_and(lane == 64, frame >= length), NEGATIVE, 0.0)
            keyed = jnp.where(lane < 64, kv, bias)
            valued = jnp.where(lane < 64, 1.0, kv)
            k1[rows] = keyed.astype(BF16)
            v1[rows] = valued.astype(BF16)
            kt[:, rows] = jnp.transpose(kv)[:64].astype(BF16) * BF16(0.125)
            v1t[:, rows] = jnp.transpose(valued).astype(BF16)

    factor = 0.125 * 1.4426950408889634

    def block_rows(block):
        return pl.ds(pl.multiple_of(block * forward_block, forward_block), forward_block)

    def scores_step(part, block, highest):
        scores = dot(
            k1[block_rows(block)], qaug[part * query_block : (part + 1) * query_block], ((1,), (1,))
        )
        sbuf[part % 2, block_rows(block)] = scores
        return jnp.maximum(highest, jnp.max(scores.reshape(forward_block // 8, 8, query_block), axis=0))

    def weights_step(part, block, highest, total):
        rows = block_rows(block)
        weights = jnp.exp2((sbuf[part % 2, rows] - highest) * factor).astype(BF16)
        pt[rows, part * query_block : (part + 1) * query_block] = weights
        return total + dot(v1t[:, rows], weights)

    def context_finish(part, total):
        turned = jnp.transpose(total)
        low = low_lanes(turned.shape)
        inverse = 1.0 / jnp.where(low, 1.0, roll64(turned))
        context = jnp.where(low, 0.0, turned * inverse).astype(BF16).astype(F32)
        rows = slice(part * query_block, (part + 1) * query_block)
        linv[rows] = inverse
        ctxh[rows] = context
        half_rows = slice(part * query_block // 2, (part + 1) * query_block // 2)
        ctx_send[half_rows] = pack_high(context).astype(BF16)

    high = jnp.full((8, query_block), NEGATIVE, F32)
    for index in range(2):
        settle(f"keys {index} in")
        forward = remote(
            quarter(core, index), quarter(core, index), send.at[7 + 17 * index], recv.at[7 + 17 * index], partner
        )
        forward.start()
        later(f"forward {index} in", quarter(other, index), recv.at[7 + 17 * index])
        pending[f"forward {index} out"] = forward.wait_send
        prepare_keys(core, index)
        if index == 0:
            settle("heads 1 in")
            for slot in range(heads):
                rows = slice(ROWS * slot, ROWS * slot + ROWS)
                part = unpack_low(qpk[slot].astype(F32))
                lane = lax.broadcasted_iota(jnp.int32, part.shape, 1)
                qcl[rows] = (part * 0.125).astype(BF16)
                qaug[rows] = jnp.where(lane == 64, 1.0, part).astype(BF16)
        high = scores_step(0, core * 2 + index, high)
    for index in range(2):
        settle(f"forward {index} in")
        prepare_keys(other, index)
        high = scores_step(0, other * 2 + index, high)

    start_high = jnp.full((8, query_block), NEGATIVE, F32)
    start_total = jnp.zeros((128, query_block), F32)
    for part in range(query_blocks):
        highest = jnp.max(high, axis=0, keepdims=True)
        if part + 1 < query_blocks:

            def both(b, carried, part=part, highest=highest):
                h, t = carried
                return scores_step(part + 1, b, h), weights_step(part, b, highest, t)

            high, total = lax.fori_loop(0, 4, both, (start_high, start_total))
        else:
            total = lax.fori_loop(
                0, 4, lambda b, t, part=part, highest=highest: weights_step(part, b, highest, t), start_total
            )
        context_finish(part, total)

    my_head = chip % heads
    moves = [(-1, 0, 16, 80), (0, 0, 80, 16)]
    moves += [(i, 64 * i - 16, 96, 0) for i in range(1, heads - 1)]
    moves += [(heads - 1, 64 * (heads - 1) - 16, 80, 0), (heads, 64 * heads - 16, 16, 0)]

    def owner_of(i):
        return (group * heads + i + seq) % seq

    for index, (i, start, count, to) in enumerate(moves):
        source = ctx_send.at[pl.ds(start, count)]
        target = ctx_recv.at[my_head, pl.ds(to, count)]

        @pl.when(owner_of(i) == me)
        def _(source=source, target=target):
            pltpu.make_async_copy(source, target, recv.at[8]).start()

        @pl.when(owner_of(i) != me)
        def _(source=source, target=target, i=i, index=index):
            remote(source, target, ctx_sem.at[index], recv.at[8], (z, owner_of(i))).start()

        def sent(source=source, i=i, index=index):
            @pl.when(owner_of(i) != me)
            def _():
                drain(source, ctx_sem.at[index])

        pending[f"context {index}"] = sent

    def live(rows, first):
        frame = me * ROWS + first + lax.broadcasted_iota(jnp.int32, (rows, 128), 0)
        return jnp.logical_and(frame >= 0, frame < length)

    def column(chunk):
        return pl.ds(pl.multiple_of(chunk * 128, 128), 128)

    def turned_convolution(rows, columns):
        total = jnp.zeros((ROWS, 128), F32)
        for low in range(8):
            moved = shifted(rows, low)
            for high_part in range(4):
                tap = 31 - (8 * high_part + low)
                if 0 <= tap < KERNEL:
                    total = total + taps_ref[tap : tap + 1, columns] * moved[8 * high_part : 8 * high_part + ROWS]
        return total

    settle("w", "taps", "gain", "shift")

    @pl.loop(0, chunks)
    def _(chunk):
        columns = column(chunk)
        cmask_ref[:, columns] = turned_convolution(jnp.where(live(mid, -16), 1.0, 0.0), columns)

    settle(*(f"halo {index} in" for index in range(4)))
    drain(ctx_recv, recv.at[8])

    for pair in range(heads // 2):
        ctx_ref[:, 128 * pair : 128 * pair + 128] = unpack_pair(
            ctx_recv[2 * pair].astype(F32), ctx_recv[2 * pair + 1].astype(F32)
        ).astype(BF16)

    counted = jnp.clip(length - me * ROWS, 0, ROWS).astype(F32)

    @pl.loop(0, channels // 256)
    def _(chunk):
        columns = pl.ds(pl.multiple_of(chunk * 256, 256), 256)
        hidden = x_ext[:, columns].astype(F32) + dot(ctx_ref[...], w_ref[:, columns])
        mask = live(ext, -HALO)
        mask = jnp.concatenate([mask, mask], axis=1)
        hid_ref[:, columns] = jnp.where(mask, hidden, 0.0).astype(BF16).astype(F32)

    @pl.loop(0, chunks)
    def _(chunk):
        columns = column(chunk)
        hidden = hid_ref[:, columns]
        total = jnp.zeros((mid, 128), F32)
        for low in range(8):
            moved = shifted(hidden, low)
            for high_part in range(4):
                tap = 8 * high_part + low - 1
                if 0 <= tap < KERNEL:
                    total = total + taps_ref[tap : tap + 1, columns] * moved[8 * high_part : 8 * high_part + mid]
        conv_ref[:, columns] = total
        own = total[16 : 16 + ROWS]
        mask = live(ROWS, 0)
        summed = jnp.sum(jnp.where(mask, own, 0.0), axis=0, keepdims=True)
        mean = summed / jnp.maximum(counted, 1.0)
        spread = own - mean
        squares = jnp.sum(jnp.where(mask, spread * spread, 0.0), axis=0, keepdims=True)
        stat_a[pl.ds(chunk, 1)] = summed
        stat_a[pl.ds(chunks + chunk, 1)] = squares

    settle("lengths in")
    lengths = len_recv[:, :1]


    def write(source, target, index):
        copy = pltpu.make_async_copy(source, target, write_sem.at[index])
        copy.start()
        pending[f"write {index}"] = copy.wait

    def gather_first(source, target, index, beside=None):
        slot = z * 2 + core
        target[slot] = source[...]
        remote(source, target.at[slot], send.at[index], recv.at[index], partner).start()

        @pl.loop(1, depth)
        def _(d):
            for c in range(2):
                remote(
                    source, target.at[slot], send.at[index], recv.at[index], ((z + d) % depth, chip * 2 + c)
                ).start()

        later(f"first {index}", target.at[pl.ds(0, 2 * depth - 1)], send.at[index])
        if beside is not None:
            beside()
        drain(target.at[pl.ds(0, 2 * depth - 1)], recv.at[index])

    def gather_second(source, target, index):
        target[chip] = source[...]

        @pl.loop(1, chips)
        def _(d):
            remote(
                source, target.at[chip], send.at[index], recv.at[index], (z, ((chip + d) % chips) * 2 + core)
            ).start()

        later(f"second {index}", target.at[pl.ds(0, chips - 1)], send.at[index])
        drain(target.at[pl.ds(0, chips - 1)], recv.at[index])

    def frames_of(index):
        return jnp.clip(lengths - (index * ROWS).astype(F32), 0.0, float(ROWS))

    def merged(gathered, counts):
        sums = gathered[:, :chunks]
        squares = gathered[:, chunks:]
        count = jnp.sum(counts, axis=0)
        total = jnp.sum(sums, axis=0)
        mean = total / jnp.maximum(count, 1.0)
        shift = sums / jnp.maximum(counts, 1.0) - mean[None]
        return total, jnp.sum(squares, axis=0) + jnp.sum(counts * shift * shift, axis=0), count, mean

    def first_counts():
        both_cores = [frames_of(chip * 2 + c) for c in range(2)]
        return jnp.concatenate([lax.slice_in_dim(both_cores[i % 2], i // 2, i // 2 + 1) for i in range(2 * depth)], axis=0)

    def second_counts():
        per_chip = []
        for i in range(chips):
            first = jnp.clip(lengths - float(2 * i * ROWS), 0.0, float(2 * ROWS))
            per_chip.append(jnp.sum(first, axis=0, keepdims=True))
        return jnp.concatenate(per_chip, axis=0)

    gather_first(stat_a, recv_a, 9)
    total, squares, count, mean = merged(recv_a[...], first_counts())
    stat_b[:chunks] = total
    stat_b[chunks:] = squares
    gather_second(stat_b, recv_b, 10)
    total, squares, count, mean = merged(recv_b[...], second_counts())
    tot_ref[:chunks] = mean
    tot_ref[chunks : 2 * chunks] = lax.rsqrt(squares / count + EPSILON)
    tot_ref[2 * chunks : 3 * chunks] = jnp.broadcast_to(1.0 / count, (chunks, 128))

    @pl.loop(0, chunks)
    def _(chunk):
        columns = column(chunk)
        mean = tot_ref[pl.ds(chunk, 1)]
        inverse = tot_ref[pl.ds(chunks + chunk, 1)]
        normed = (conv_ref[:, columns] - mean) * inverse
        conv_ref[:, columns] = normed
        act = normed * gain_ref[:, columns] + shift_ref[:, columns]
        gate = 1.0 / (1.0 + jnp.exp(-act))
        grad_out = jnp.where(live(mid, -16), cot_ext[:, columns].astype(F32), 0.0)
        grad_act = grad_out * gate * (1.0 + act * (1.0 - gate))
        ga_ref[:, columns] = grad_act
        own = grad_act[16 : 16 + ROWS]
        stat_c[pl.ds(chunk, 1)] = jnp.sum(own * normed[16 : 16 + ROWS], axis=0, keepdims=True)
        stat_c[pl.ds(chunks + chunk, 1)] = jnp.sum(own, axis=0, keepdims=True)
        gated = (act * gate)[16 : 16 + ROWS]
        hidden = hid_ref[HALO : HALO + ROWS, columns]
        out_ref[:, columns] = jnp.where(live(ROWS, 0), hidden + gated, 0.0).astype(BF16)

    def beside():
        write(out_ref, out_hbm, 0)

        @pl.loop(0, chunks)
        def _(chunk):
            columns = column(chunk)
            cgrad_ref[:, columns] = turned_convolution(ga_ref[:, columns], columns)
            cnorm_ref[:, columns] = turned_convolution(
                jnp.where(live(mid, -16), conv_ref[:, columns], 0.0), columns
            )

    gather_first(stat_c, recv_c, 11, beside)
    stat_d[...] = jnp.sum(recv_c[...], axis=0)
    gather_second(stat_d, recv_d, 12)
    sums_ref[...] = jnp.sum(recv_d[...], axis=0)

    @pl.loop(0, chunks)
    def _(chunk):
        columns = column(chunk)
        inverse = tot_ref[pl.ds(chunks + chunk, 1)]
        per_count = tot_ref[pl.ds(2 * chunks + chunk, 1)]
        gain_sum = sums_ref[pl.ds(chunk, 1)] * per_count
        shift_sum = sums_ref[pl.ds(chunks + chunk, 1)] * per_count
        scale = inverse * gain_ref[:, columns]
        turned = cgrad_ref[:, columns] - shift_sum * cmask_ref[:, columns] - gain_sum * cnorm_ref[:, columns]
        total = cot_ext[16 : 16 + ROWS, columns].astype(F32) + scale * turned
        ginp_ref[:, columns] = jnp.where(live(ROWS, 0), total, 0.0).astype(BF16)

    write(ginp_ref, ginp_hbm, 1)

    @pl.loop(0, heads // 2)
    def _(pair):
        rows = pl.ds(pl.multiple_of(pair * 128, 128), 128)
        grad_context = dot(ginp_ref[...], w_ref[rows], ((1,), (1,))).astype(BF16).astype(F32)
        even, odd = pack_pair(grad_context)
        do_send[2 * pair] = even.astype(BF16)
        do_send[2 * pair + 1] = odd.astype(BF16)

    to_heads(do_send, do_recv, 13, 14)

    own_context = jnp.transpose(ctx_ref[HALO : HALO + ROWS].astype(F32)).astype(BF16)

    def stage0(piece):
        copy = remote(
            wsend.at[piece].at[other], g0.at[piece], piece_send.at[5 * piece + 0], piece_recv.at[5 * piece + 0], partner
        )
        copy.start()
        pending[f"stage 0 in {piece}"] = copy.wait_recv
        pending[f"stage 0 out {piece}"] = copy.wait_send

    for piece in range(PIECES):
        first = piece * piece_width
        size = min(piece_width, channels - first)
        if size > 0:
            terms = dot(own_context, ginp_ref[:, first : first + size]).astype(BF16)
            wsend.at[piece][:, :, :, :size] = terms.reshape(2, chips, 16, size)
        if piece < PIECES - 1:
            stage0(piece)

    tap_lanes = slice(piece_width - 128, piece_width)
    wsend[PIECES - 1, :, :, :, tap_lanes] = jnp.zeros((2, chips, 16, 128), BF16)

    @pl.loop(0, chunks)
    def _(chunk):
        columns = column(chunk)
        per_count = tot_ref[pl.ds(2 * chunks + chunk, 1)]
        gain_sum = sums_ref[pl.ds(chunk, 1)] * per_count
        shift_sum = sums_ref[pl.ds(chunks + chunk, 1)] * per_count
        scale = tot_ref[pl.ds(chunks + chunk, 1)] * gain_ref[:, columns]
        own = slice(16, 16 + ROWS)
        grad_conv = scale * (ga_ref[own, columns] - (shift_sum + conv_ref[own, columns] * gain_sum))
        grad_conv = jnp.where(live(ROWS, 0), grad_conv, 0.0)
        hidden = hid_ref[16:, columns]
        found = [None] * 32
        for low in range(8):
            moved = shifted(hidden, low)
            for high_part in range(4):
                tap = 8 * high_part + low - 1
                if 0 <= tap < KERNEL:
                    terms = grad_conv * moved[8 * high_part : 8 * high_part + ROWS]
                    found[tap] = jnp.sum(terms, axis=0, keepdims=True)
        found[31] = jnp.zeros((1, 128), F32)
        stacked = jnp.concatenate(found, axis=0).astype(BF16)
        wsend.at[PIECES - 1].at[0][pl.ds(chunk, 1), :, tap_lanes] = stacked[:16].reshape(1, 16, 128)
        wsend.at[PIECES - 1].at[1][pl.ds(chunk, 1), :, tap_lanes] = stacked[16:].reshape(1, 16, 128)

    stage0(PIECES - 1)

    def stage1(piece):
        settle(f"stage 0 in {piece}")

        @pl.loop(0, chips)
        def _(i):
            total = wsend.at[piece].at[core, i][...].astype(F32) + g0.at[piece].at[i][...].astype(F32)
            gs1.at[piece].at[i][...] = total.astype(BF16)

        g1.at[piece].at[chip][...] = gs1.at[piece].at[chip][...]

        @pl.loop(1, chips)
        def _(d):
            peer = (chip + d) % chips
            remote(
                gs1.at[piece].at[peer],
                g1.at[piece].at[chip],
                piece_send.at[5 * piece + 1],
                piece_recv.at[5 * piece + 1],
                (z, peer * 2 + core),
            ).start()

        later(f"stage 1 in {piece}", g1.at[piece].at[pl.ds(0, chips - 1)], piece_recv.at[5 * piece + 1])
        later(f"stage 1 out {piece}", g1.at[piece].at[pl.ds(0, chips - 1)], piece_send.at[5 * piece + 1])

    def stage2(piece):
        settle(f"stage 1 in {piece}")
        total = g1.at[piece][0].astype(F32)
        for i in range(1, chips):
            total = total + g1.at[piece][i].astype(F32)
        total = total.astype(BF16)
        gs2[piece] = total
        g2.at[piece].at[z][...] = total

        @pl.loop(1, depth)
        def _(d):
            remote(
                gs2.at[piece],
                g2.at[piece].at[z],
                piece_send.at[5 * piece + 2],
                piece_recv.at[5 * piece + 2],
                ((z + d) % depth, me),
            ).start()

        pending[f"stage 2 in {piece}"] = lambda: drain(
            g2.at[piece].at[pl.ds(0, depth - 1)], piece_recv.at[5 * piece + 2]
        )
        pending[f"stage 2 out {piece}"] = lambda: drain(
            g2.at[piece].at[pl.ds(0, depth - 1)], piece_send.at[5 * piece + 2]
        )

    def stage3(piece):
        settle(f"stage 2 in {piece}")
        total = g2.at[piece][0].astype(F32)
        for i in range(1, depth):
            total = total + g2.at[piece][i].astype(F32)
        gfin_ref.at[piece].at[core, chip][...] = total.astype(BF16)
        final = gfin_ref.at[piece].at[core, chip]

        @pl.loop(1, chips)
        def _(d):
            peer = (chip + d) % chips
            remote(
                final, final, piece_send.at[5 * piece + 3], piece_recv.at[5 * piece + 3], (z, peer * 2 + core)
            ).start()

        size = gfin_ref.at[piece].at[core, pl.ds(0, chips - 1)]
        later(f"stage 3 in {piece}", size, piece_recv.at[5 * piece + 3])
        later(f"stage 3 out {piece}", size, piece_send.at[5 * piece + 3])

    def stage4(piece):
        settle(f"stage 3 in {piece}")
        finals = gfin_ref.at[piece].at[core]
        copy = remote(finals, finals, piece_send.at[5 * piece + 4], piece_recv.at[5 * piece + 4], partner)
        copy.start()
        later(f"stage 4 in {piece}", gfin_ref.at[piece].at[other], piece_recv.at[5 * piece + 4])
        pending[f"stage 4 out {piece}"] = copy.wait_send

    for piece in range(PIECES):
        stage1(piece)

    settle("heads 13 in")
    for index in range(heads):
        rows = slice(ROWS * index, ROWS * index + ROWS)
        scaled = (unpack_high(do_recv[index].astype(F32)) * linv[rows]).astype(BF16)
        docl[rows] = scaled
        scaled = scaled.astype(F32)
        delta = jnp.sum(ctxh[rows] * scaled, axis=1, keepdims=True)
        first = delta.astype(BF16).astype(F32)
        rest = delta - first
        lane = lax.broadcasted_iota(jnp.int32, scaled.shape, 1)
        doaug[rows] = jnp.where(lane == 0, -first, jnp.where(lane == 1, -rest, scaled)).astype(BF16)

    dqt[...] = jnp.zeros_like(dqt)

    def part_copy(turn):
        rows = pl.ds(pl.multiple_of(turn * backward_block, backward_block), backward_block)
        return remote(dsend.at[rows], precv.at[rows], part_send.at[turn], part_recv.at[turn], partner)

    turns = 4
    slots = backward_block // ROWS

    @pl.loop(0, 2 * turns)
    def _(step):
        half = jnp.where(step < turns, other, core)
        turn = step % turns
        rows = pl.ds(
            pl.multiple_of(half * half_keys + turn * backward_block, backward_block), backward_block
        )
        turn_rows = pl.ds(pl.multiple_of(turn * backward_block, backward_block), backward_block)
        weights = pt[rows]
        grads = dot(v1[rows], doaug[...], ((1,), (1,))).astype(BF16)
        scores = weights * grads
        dqt[...] += dot(kt[:, rows], scores)
        rbuf[...] = dot(scores, qcl[...]) + dot(weights, docl[...])

        @pl.when(step < turns)
        def _():
            dsend[turn_rows] = rbuf[...].astype(BF16)
            part_copy(turn).start()

        @pl.when(step >= turns)
        def _():
            part_copy(turn).wait_recv()
            osend[turn_rows] = (rbuf[...] + precv[turn_rows].astype(F32)).astype(BF16)
            for i in range(slots):
                slot = turn * slots + i
                owner = (chip + chips - slot) % chips
                source = osend.at[pl.ds(pl.multiple_of(slot * ROWS, ROWS), ROWS)]

                def give(source=source, owner=owner):
                    remote(source, kvrecv.at[chip], own_sem, recv.at[20], (z, owner * 2 + core)).start()

                if i == 0:

                    @pl.when(turn == 0)
                    def _(source=source):
                        pltpu.make_async_copy(source, kvrecv.at[chip], recv.at[20]).start()

                    pl.when(turn > 0)(give)
                else:
                    give()

        for piece in range(PIECES):

            @pl.when(step == 3 + piece)
            def _(piece=piece):
                stage2(piece)

    def parts_sent():
        @pl.loop(0, turns)
        def _(turn):
            part_copy(turn).wait_send()

    pending["parts"] = parts_sent
    later("owned in", kvrecv, recv.at[20])
    later("owned out", kvrecv.at[pl.ds(0, chips - 1)], own_sem)

    @pl.loop(0, query_blocks)
    def _(block):
        part = pl.ds(pl.multiple_of(block * query_block, query_block), query_block)
        turned = dqt[:, part]
        turned = jnp.transpose(jnp.concatenate([turned, jnp.zeros_like(turned)], axis=0))
        half_part = pl.ds(pl.multiple_of(block * query_block // 2, query_block // 2), query_block // 2)
        dq_send[half_part] = pack_low(turned).astype(BF16)

    for i in range(heads):
        source = dq_send.at[pl.ds(64 * i, 64)]
        target = dq_recv.at[my_head]

        @pl.when(owner_of(i) == me)
        def _(source=source, target=target):
            pltpu.make_async_copy(source, target, recv.at[21]).start()

        @pl.when(owner_of(i) != me)
        def _(source=source, target=target, i=i):
            remote(source, target, dq_sem.at[i], recv.at[21], (z, owner_of(i))).start()

        def sent(source=source, i=i):
            @pl.when(owner_of(i) != me)
            def _():
                drain(source, dq_sem.at[i])

        pending[f"grad query {i}"] = sent

    for piece in range(PIECES):
        stage3(piece)

    settle("owned in")
    for pair in range(heads // 2):
        columns = slice(128 * pair, 128 * pair + 128)
        even = kvrecv[2 * pair].astype(F32) + kvrecv[2 * pair + heads].astype(F32)
        odd = kvrecv[2 * pair + 1].astype(F32) + kvrecv[2 * pair + 1 + heads].astype(F32)
        low = low_lanes(even.shape)
        gk_ref[:, columns] = jnp.where(low, even, roll64(odd)).astype(BF16)
        gv_ref[:, columns] = jnp.where(low, roll64(even), odd).astype(BF16)
    write(gk_ref, gk_hbm, 3)
    write(gv_ref, gv_hbm, 4)

    drain(dq_recv, recv.at[21])
    for pair in range(heads // 2):
        gq_ref[:, 128 * pair : 128 * pair + 128] = unpack_pair(
            dq_recv[2 * pair].astype(F32), dq_recv[2 * pair + 1].astype(F32)
        ).astype(BF16)

    write(gq_ref, gq_hbm, 2)
    for piece in range(PIECES):
        stage4(piece)
    settle()


def finish(width, chunks, *refs):
    out, ginp, gq, gk, gv, packed, sums = refs[:7]
    outs = refs[7:16]
    weights, taps, sem = refs[16:]
    channels = weights.shape[1]
    copies = [
        pltpu.make_async_copy(source, target, sem.at[index])
        for index, (source, target) in enumerate(
            (
                (out, outs[0]),
                (ginp, outs[1]),
                (gq, outs[2]),
                (gk, outs[3]),
                (gv, outs[4]),
                (weights, outs[5]),
                (taps, outs[6]),
                (sums.at[pl.ds(0, chunks)], outs[7]),
                (sums.at[pl.ds(chunks, chunks)], outs[8]),
            )
        )
    ]
    for index in (0, 1, 2, 3, 4, 7, 8):
        copies[index].start()
    piece_width = packed.shape[-1]
    for piece in range(PIECES):
        first = piece * piece_width
        size = min(piece_width, channels - first)
        for half in range(2 if size > 0 else 0):
            rows = slice(half * width // 2, (half + 1) * width // 2)
            terms = packed[piece, half, :, :, :size].astype(F32)
            weights[rows, first : first + size] = terms.reshape(width // 2, size)
    for chunk in range(chunks):
        lanes = slice(piece_width - 128, piece_width)
        columns = slice(128 * chunk, 128 * chunk + 128)
        taps[:16, columns] = packed[PIECES - 1, 0, chunk, :, lanes].astype(F32)
        taps[16:, columns] = packed[PIECES - 1, 1, chunk, :15, lanes].astype(F32)
    copies[5].start()
    copies[6].start()
    for copy in copies:
        copy.wait()


def shards(
    depth,
    query_rows,
    key_rows,
    value_rows,
    inputs,
    lengths,
    out_weight,
    taps,
    norm_gain,
    norm_shift,
    cotangent,
):
    seq = lax.axis_size("seq")
    heads = seq // 4
    chips = seq // 2
    width = query_rows.shape[2]
    channels = inputs.shape[2]
    chunks = channels // 128
    queries = ROWS * heads
    keys = seq * ROWS
    ext = ROWS + 2 * HALO
    mid = ROWS + 32
    padded = channels + 128
    piece_width = padded // PIECES
    query_block = min(queries, 512)
    vmem = pltpu.VMEM
    scratch = [
        vmem((ROWS, width), BF16),
        vmem((ROWS, width), BF16),
        vmem((ROWS, width), BF16),
        vmem((1, channels), F32),
        vmem((1, channels), F32),
        vmem((ROWS, channels), BF16),
        vmem((ROWS, channels), BF16),
        vmem((ROWS, width), BF16),
        vmem((ROWS, width), BF16),
        vmem((ROWS, width), BF16),
        vmem((8, 128), F32),
        vmem((depth, 8, 128), F32),
        vmem((ROWS, channels), F32),
        vmem((ROWS, channels), F32),
        vmem((ROWS, channels), F32),
        vmem((heads, ROWS, 128), BF16),
        vmem((heads, 64, 128), BF16),
        vmem((keys, 128), BF16),
        vmem((heads, 64, 128), BF16),
        vmem((keys, 128), BF16),
        vmem((keys, 128), BF16),
        vmem((64, keys), BF16),
        vmem((128, keys), BF16),
        vmem((queries, 128), BF16),
        vmem((queries, 128), BF16),
        vmem((2, keys, query_block), F32),
        vmem((keys, queries), BF16),
        vmem((queries, 128), F32),
        vmem((queries, 128), F32),
        vmem((queries // 2, 128), BF16),
        vmem((heads, ext // 2, 128), BF16),
        vmem((ext, channels), BF16),
        vmem((mid, channels), BF16),
        vmem((width, channels), BF16),
        vmem((KERNEL, channels), F32),
        vmem((ext, width), BF16),
        vmem((ext, channels), F32),
        vmem((mid, channels), F32),
        vmem((mid, channels), F32),
        vmem((2 * chunks, 128), F32),
        vmem((2 * chunks, 128), F32),
        vmem((2 * depth, 2 * chunks, 128), F32),
        vmem((chips, 2 * chunks, 128), F32),
        vmem((2 * chunks, 128), F32),
        vmem((2 * depth, 2 * chunks, 128), F32),
        vmem((2 * chunks, 128), F32),
        vmem((chips, 2 * chunks, 128), F32),
        vmem((3 * chunks, 128), F32),
        vmem((heads, 64, 128), BF16),
        vmem((heads, 64, 128), BF16),
        vmem((queries, 128), BF16),
        vmem((queries, 128), BF16),
        vmem((keys // 8, 128), F32),
        vmem((64, queries), F32),
        vmem((keys // 2, 128), BF16),
        vmem((keys // 2, 128), BF16),
        vmem((keys // 2, 128), BF16),
        vmem((chips, ROWS, 128), BF16),
        vmem((queries // 2, 128), BF16),
        vmem((heads, 64, 128), BF16),
        vmem((PIECES, 2, chips, 16, piece_width), BF16),
        vmem((PIECES, chips, 16, piece_width), BF16),
        vmem((PIECES, chips, 16, piece_width), BF16),
        vmem((PIECES, chips, 16, piece_width), BF16),
        vmem((PIECES, 16, piece_width), BF16),
        vmem((PIECES, depth, 16, piece_width), BF16),
        pltpu.SemaphoreType.DMA((9,)),
        pltpu.SemaphoreType.DMA((25,)),
        pltpu.SemaphoreType.DMA((25,)),
        pltpu.SemaphoreType.DMA((heads + 2,)),
        pltpu.SemaphoreType.DMA((heads,)),
        pltpu.SemaphoreType.DMA((4,)),
        pltpu.SemaphoreType.DMA((4,)),
        pltpu.SemaphoreType.DMA,
        pltpu.SemaphoreType.DMA((5 * PIECES,)),
        pltpu.SemaphoreType.DMA((5 * PIECES,)),
        pltpu.SemaphoreType.DMA((5,)),
    ]
    in_vmem = pl.BlockSpec(memory_space=pltpu.VMEM)
    anywhere = pl.BlockSpec(memory_space=pl.ANY)
    plain = (
        jax.ShapeDtypeStruct((ROWS, channels), BF16),
        jax.ShapeDtypeStruct((ROWS, channels), BF16),
        jax.ShapeDtypeStruct((ROWS, width), BF16),
        jax.ShapeDtypeStruct((ROWS, width), BF16),
        jax.ShapeDtypeStruct((ROWS, width), BF16),
    )
    results = pl.pallas_call(
        functools.partial(kernel, heads, seq, depth),
        out_shape=plain
        + (
            jax.ShapeDtypeStruct((PIECES, 2, chips, 16, piece_width), BF16),
            jax.ShapeDtypeStruct((2 * chunks, 128), F32),
        ),
        in_specs=[pl.BlockSpec(memory_space=pltpu.SMEM)] + [anywhere] * 9,
        out_specs=(anywhere,) * 5 + (in_vmem,) * 2,
        scratch_shapes=scratch,
        compiler_params=pltpu.CompilerParams(
            collective_id=0, has_side_effects=True, vmem_limit_bytes=60 * 1024 * 1024
        ),
    )(
        lengths,
        query_rows[0],
        key_rows[0],
        value_rows[0],
        inputs[0],
        cotangent[0],
        out_weight,
        taps,
        norm_gain[None],
        norm_shift[None],
    )
    final = pl.pallas_call(
        functools.partial(finish, width, chunks),
        out_shape=plain
        + (
            jax.ShapeDtypeStruct((width, channels), F32),
            jax.ShapeDtypeStruct((KERNEL, channels), F32),
            jax.ShapeDtypeStruct((chunks, 128), F32),
            jax.ShapeDtypeStruct((chunks, 128), F32),
        ),
        in_specs=[anywhere] * 5 + [in_vmem] * 2,
        out_specs=(anywhere,) * 9,
        scratch_shapes=[
            vmem((width, channels), F32),
            vmem((KERNEL, channels), F32),
            pltpu.SemaphoreType.DMA((9,)),
        ],
        compiler_params=pltpu.CompilerParams(vmem_limit_bytes=16 * 1024 * 1024),
    )(*results)
    return (
        *(array[None] for array in final[:5]),
        final[5],
        final[6],
        final[7].reshape(channels),
        final[8].reshape(channels),
    )


def solution(mesh):
    rows = P("dp", "seq", None)
    return jax.shard_map(
        functools.partial(shards, mesh.shape["dp"]),
        mesh=mesh,
        in_specs=(rows, rows, rows, rows, P("dp"), P(), P(), P(), P(), rows),
        out_specs=(rows, rows, rows, rows, rows, P(), P(), P(), P()),
        check_vma=False,
    )
```

```python
import functools

import jax
import jax.numpy as jnp
from jax import lax
from jax.experimental import pallas as pl
from jax.experimental.pallas import tpu as pltpu
from jax.sharding import PartitionSpec as P

KERNEL = 31
HALF = 15
HEAD_DIM = 64
ROWS = 128
HALO = 32
NEGATIVE = -1e30
EPSILON = 1e-05
PIECES = 3
MESH = pl.DeviceIdType.MESH
F32 = jnp.float32
BF16 = jnp.bfloat16


def roll64(x):
    return pltpu.roll(x, 64, 1)


def low_lanes(shape):
    return lax.broadcasted_iota(jnp.int32, shape, 1) < 64


def split_units(x):
    rows = x.shape[0]
    units = x.reshape(rows // 32, 2, 16, 128)
    return units[:, 0].reshape(rows // 2, 128), units[:, 1].reshape(rows // 2, 128)


def join_units(first, second):
    rows = first.shape[0]
    first = first.reshape(rows // 16, 1, 16, 128)
    second = second.reshape(rows // 16, 1, 16, 128)
    return jnp.concatenate([first, second], axis=1).reshape(2 * rows, 128)


def pack_pair(x):
    first, second = split_units(x)
    low = low_lanes(first.shape)
    even = jnp.where(low, first, roll64(second))
    odd = jnp.where(low, roll64(first), second)
    return even, odd


def unpack_pair(even, odd):
    low = low_lanes(even.shape)
    return join_units(jnp.where(low, even, roll64(odd)), jnp.where(low, roll64(even), odd))


def unpack_low(packed):
    low = low_lanes(packed.shape)
    return join_units(jnp.where(low, packed, 0.0), jnp.where(low, roll64(packed), 0.0))


def unpack_high(packed):
    low = low_lanes(packed.shape)
    return join_units(jnp.where(low, 0.0, roll64(packed)), jnp.where(low, 0.0, packed))


def pack_low(x):
    first, second = split_units(x)
    return jnp.where(low_lanes(first.shape), first, roll64(second))


def pack_high(x):
    first, second = split_units(x)
    return jnp.where(low_lanes(first.shape), roll64(first), second)


def dot(a, b, dims=((1,), (0,))):
    return lax.dot_general(a, b, (dims, ((), ())), preferred_element_type=F32)


def shifted(x, amount):
    return x if amount == 0 else pltpu.roll(x, x.shape[0] - amount, 0)


def kernel(
    heads,
    seq,
    depth,
    length_ref,
    q_hbm,
    k_hbm,
    v_hbm,
    x_hbm,
    cot_hbm,
    w_hbm,
    taps_hbm,
    gain_hbm,
    shift_hbm,
    out_hbm,
    ginp_hbm,
    gq_hbm,
    gk_hbm,
    gv_hbm,
    gfin_ref,
    sums_ref,
    q_ref,
    k_ref,
    v_ref,
    gain_ref,
    shift_ref,
    out_ref,
    ginp_ref,
    gq_ref,
    gk_ref,
    gv_ref,
    len_send,
    len_recv,
    cmask_ref,
    cgrad_ref,
    cnorm_ref,
    tmask_ref,
    tgrad_ref,
    tnorm_ref,
    count_a,
    count_b,
    kv_send,
    q_send,
    kvbuf,
    qpk,
    k1,
    v1,
    kt,
    v1t,
    qaug,
    qcl,
    sbuf,
    pt,
    ctxh,
    linv,
    ctx_send,
    ctx_recv,
    x_ext,
    cot_ext,
    w_ref,
    taps_ref,
    ctx_ref,
    hid_ref,
    conv_ref,
    ga_ref,
    stat_a,
    stat_b,
    recv_a,
    recv_b,
    stat_c,
    recv_c,
    stat_d,
    recv_d,
    tot_ref,
    do_send,
    do_recv,
    doaug,
    docl,
    rbuf,
    dqt,
    dsend,
    precv,
    osend,
    kvrecv,
    dq_send,
    dq_recv,
    wsend,
    g0,
    gs1,
    g1,
    gs2,
    g2,
    load_sem,
    send,
    recv,
    ctx_sem,
    dq_sem,
    part_send,
    part_recv,
    own_sem,
    piece_send,
    piece_recv,
    write_sem,
):
    chips = seq // 2
    width = q_ref.shape[1]
    channels = out_ref.shape[1]
    chunks = channels // 128
    queries = ROWS * heads
    half_keys = chips * ROWS
    forward_block = half_keys // 2
    backward_block = half_keys // 4
    query_block = min(queries, 512)
    query_blocks = queries // query_block
    padded = channels + 128
    piece_width = padded // PIECES
    ext = ROWS + 2 * HALO
    mid = ROWS + 32

    z = lax.axis_index("dp")
    me = lax.axis_index("seq")
    chip = me // 2
    core = me % 2
    other = 1 - core
    partner = (z, chip * 2 + other)
    group = (chip // heads) * 2 + core
    my_group = me // heads
    length = length_ref[0]

    def remote(src, dst, send_sem, recv_sem, device):
        return pltpu.make_async_remote_copy(
            src_ref=src, dst_ref=dst, send_sem=send_sem, recv_sem=recv_sem, device_id=device, device_id_type=MESH
        )

    def drain(ref, sem):
        pltpu.make_async_copy(ref, ref, sem).wait()

    pending = {}

    def later(name, ref, sem):
        pending[name] = lambda: drain(ref, sem)

    def settle(*names):
        for name in names or tuple(pending):
            pending.pop(name)()

    barrier = pltpu.get_barrier_semaphore()

    @pl.loop(1, seq)
    def _(d):
        pl.semaphore_signal(barrier, inc=1, device_id=(z, (me + d) % seq), device_id_type=MESH)

    @pl.loop(1, depth)
    def _(d):
        pl.semaphore_signal(barrier, inc=1, device_id=((z + d) % depth, me), device_id_type=MESH)

    loads = (
        ("k", k_hbm, k_ref),
        ("v", v_hbm, v_ref),
        ("q", q_hbm, q_ref),
        ("x", x_hbm, x_ext.at[pl.ds(HALO, ROWS)]),
        ("cot", cot_hbm, cot_ext.at[pl.ds(16, ROWS)]),
        ("w", w_hbm, w_ref),
        ("taps", taps_hbm, taps_ref),
        ("gain", gain_hbm, gain_ref),
        ("shift", shift_hbm, shift_ref),
    )
    for index, (name, source, target) in enumerate(loads):
        copy = pltpu.make_async_copy(source, target, load_sem.at[index])
        copy.start()
        pending[name] = copy.wait

    len_send[...] = jnp.full((8, 128), length.astype(F32), F32)
    settle("k", "v", "q")
    for pair in range(heads // 2):
        columns = slice(128 * pair, 128 * pair + 128)
        kp = k_ref[:, columns].astype(F32)
        vp = v_ref[:, columns].astype(F32)
        low = low_lanes(kp.shape)
        kv_send[2 * pair] = jnp.where(low, kp, roll64(vp)).astype(BF16)
        kv_send[2 * pair + 1] = jnp.where(low, roll64(kp), vp).astype(BF16)
        even, odd = pack_pair(q_ref[:, columns].astype(F32))
        q_send[2 * pair] = even.astype(BF16)
        q_send[2 * pair + 1] = odd.astype(BF16)

    pl.semaphore_wait(barrier, seq - 1 + depth - 1)

    def kv_slot(d):
        return kvbuf.at[pl.ds(pl.multiple_of(core * half_keys + d * ROWS, ROWS), ROWS)]

    def send_keys(first, last, index):
        @pl.loop(first, last)
        def _(d):
            peer = (chip + d) % chips
            remote(kv_send.at[peer % heads], kv_slot(d), send.at[index], recv.at[index], (z, peer * 2 + core)).start()

    def quarter(half, index):
        return kvbuf.at[
            pl.ds(pl.multiple_of(half * half_keys + index * forward_block, forward_block), forward_block)
        ]

    some = chips // 2
    pltpu.make_async_copy(kv_send.at[chip % heads], kv_slot(0), recv.at[0]).start()
    send_keys(1, some, 0)
    later("keys 0 in", quarter(core, 0), recv.at[0])
    later("keys 0 out", kvbuf.at[pl.ds(0, (some - 1) * ROWS)], send.at[0])

    def head_device(head):
        return ((my_group // 2) * heads + head) * 2 + my_group % 2

    def to_heads(source, target, index, self_index):
        head = chip % heads
        slot = me % heads
        mine = head_device(head) == me

        @pl.when(mine)
        def _():
            pltpu.make_async_copy(source.at[head], target.at[slot], recv.at[index]).start()

        @pl.when(jnp.logical_not(mine))
        def _():
            remote(
                source.at[head], target.at[slot], send.at[self_index], recv.at[index], (z, head_device(head))
            ).start()

        @pl.loop(1, heads)
        def _(d):
            to = (chip + d) % heads
            remote(
                source.at[to], target.at[slot], send.at[index], recv.at[index], (z, head_device(to))
            ).start()

        def own_done():
            @pl.when(jnp.logical_not(mine))
            def _():
                drain(target.at[0], send.at[self_index])

        later(f"heads {index} in", target, recv.at[index])
        later(f"heads {index} out", target.at[pl.ds(0, heads - 1)], send.at[index])
        pending[f"heads {index} own"] = own_done

    to_heads(q_send, qpk, 1, 2)

    send_keys(some, chips, 22)
    later("keys 1 in", quarter(core, 1), recv.at[22])
    later("keys 1 out", kvbuf.at[pl.ds(0, some * ROWS)], send.at[22])

    len_recv[z] = len_send[...]

    @pl.loop(1, depth)
    def _(d):
        remote(len_send, len_recv.at[z], send.at[23], recv.at[23], ((z + d) % depth, me)).start()

    later("lengths in", len_recv.at[pl.ds(0, depth - 1)], recv.at[23])
    later("lengths out", len_recv.at[pl.ds(0, depth - 1)], send.at[23])

    after = (z, (me + 1) % seq)
    before = (z, (me + seq - 1) % seq)
    settle("x", "cot")
    halo_copies = (
        remote(x_ext.at[pl.ds(ROWS, HALO)], x_ext.at[pl.ds(0, HALO)], send.at[3], recv.at[3], after),
        remote(x_ext.at[pl.ds(HALO, HALO)], x_ext.at[pl.ds(HALO + ROWS, HALO)], send.at[4], recv.at[4], before),
        remote(cot_ext.at[pl.ds(ROWS, 16)], cot_ext.at[pl.ds(0, 16)], send.at[5], recv.at[5], after),
        remote(cot_ext.at[pl.ds(16, 16)], cot_ext.at[pl.ds(16 + ROWS, 16)], send.at[6], recv.at[6], before),
    )
    for index, copy in enumerate(halo_copies):
        copy.start()
        pending[f"halo {index} in"] = copy.wait_recv
        pending[f"halo {index} out"] = copy.wait_send

    def prepare_keys(half, index):
        rows_at_once = min(forward_block, 512)

        @pl.loop(0, forward_block // rows_at_once)
        def _(part):
            first = index * forward_block + part * rows_at_once
            rows = pl.ds(pl.multiple_of(half * half_keys + first, rows_at_once), rows_at_once)
            kv = kvbuf[rows].astype(F32)
            lane = lax.broadcasted_iota(jnp.int32, kv.shape, 1)
            row = lax.broadcasted_iota(jnp.int32, kv.shape, 0) + first
            source = chip - (row >> 7)
            source = jnp.where(source < 0, source + chips, source)
            frame = (source * 2 + half) * ROWS + (row & 127)
            bias = jnp.where(jnp.logical_and(lane == 64, frame >= length), NEGATIVE, 0.0)
            keyed = jnp.where(lane < 64, kv, bias)
            valued = jnp.where(lane < 64, 1.0, kv)
            k1[rows] = keyed.astype(BF16)
            v1[rows] = valued.astype(BF16)
            kt[:, rows] = jnp.transpose(kv)[:64].astype(BF16) * BF16(0.125)
            v1t[:, rows] = jnp.transpose(valued).astype(BF16)

    factor = 0.125 * 1.4426950408889634

    def block_rows(block):
        return pl.ds(pl.multiple_of(block * forward_block, forward_block), forward_block)

    def scores_step(part, block, highest):
        scores = dot(
            k1[block_rows(block)], qaug[part * query_block : (part + 1) * query_block], ((1,), (1,))
        )
        sbuf[part % 2, block_rows(block)] = scores
        return jnp.maximum(highest, jnp.max(scores.reshape(forward_block // 8, 8, query_block), axis=0))

    def weights_step(part, block, highest, total):
        rows = block_rows(block)
        weights = jnp.exp2((sbuf[part % 2, rows] - highest) * factor).astype(BF16)
        pt[rows, part * query_block : (part + 1) * query_block] = weights
        return total + dot(v1t[:, rows], weights)

    def context_finish(part, total):
        turned = jnp.transpose(total)
        low = low_lanes(turned.shape)
        inverse = 1.0 / jnp.where(low, 1.0, roll64(turned))
        context = jnp.where(low, 0.0, turned * inverse).astype(BF16).astype(F32)
        rows = slice(part * query_block, (part + 1) * query_block)
        linv[rows] = inverse
        ctxh[rows] = context
        half_rows = slice(part * query_block // 2, (part + 1) * query_block // 2)
        ctx_send[half_rows] = pack_high(context).astype(BF16)

    high = jnp.full((8, query_block), NEGATIVE, F32)
    for index in range(2):
        settle(f"keys {index} in")
        forward = remote(
            quarter(core, index), quarter(core, index), send.at[7 + 17 * index], recv.at[7 + 17 * index], partner
        )
        forward.start()
        later(f"forward {index} in", quarter(other, index), recv.at[7 + 17 * index])
        pending[f"forward {index} out"] = forward.wait_send
        prepare_keys(core, index)
        if index == 0:
            settle("heads 1 in")
            for slot in range(heads):
                rows = slice(ROWS * slot, ROWS * slot + ROWS)
                part = unpack_low(qpk[slot].astype(F32))
                lane = lax.broadcasted_iota(jnp.int32, part.shape, 1)
                qcl[rows] = (part * 0.125).astype(BF16)
                qaug[rows] = jnp.where(lane == 64, 1.0, part).astype(BF16)
        high = scores_step(0, core * 2 + index, high)
    for index in range(2):
        settle(f"forward {index} in")
        prepare_keys(other, index)
        high = scores_step(0, other * 2 + index, high)

    start_high = jnp.full((8, query_block), NEGATIVE, F32)
    start_total = jnp.zeros((128, query_block), F32)
    for part in range(query_blocks):
        highest = jnp.max(high, axis=0, keepdims=True)
        if part + 1 < query_blocks:

            def both(b, carried, part=part, highest=highest):
                h, t = carried
                return scores_step(part + 1, b, h), weights_step(part, b, highest, t)

            high, total = lax.fori_loop(0, 4, both, (start_high, start_total))
        else:
            total = lax.fori_loop(
                0, 4, lambda b, t, part=part, highest=highest: weights_step(part, b, highest, t), start_total
            )
        context_finish(part, total)

    my_head = chip % heads
    moves = [(-1, 0, 16, 80), (0, 0, 80, 16)]
    moves += [(i, 64 * i - 16, 96, 0) for i in range(1, heads - 1)]
    moves += [(heads - 1, 64 * (heads - 1) - 16, 80, 0), (heads, 64 * heads - 16, 16, 0)]

    def owner_of(i):
        return (group * heads + i + seq) % seq

    for index, (i, start, count, to) in enumerate(moves):
        source = ctx_send.at[pl.ds(start, count)]
        target = ctx_recv.at[my_head, pl.ds(to, count)]

        @pl.when(owner_of(i) == me)
        def _(source=source, target=target):
            pltpu.make_async_copy(source, target, recv.at[8]).start()

        @pl.when(owner_of(i) != me)
        def _(source=source, target=target, i=i, index=index):
            remote(source, target, ctx_sem.at[index], recv.at[8], (z, owner_of(i))).start()

        def sent(source=source, i=i, index=index):
            @pl.when(owner_of(i) != me)
            def _():
                drain(source, ctx_sem.at[index])

        pending[f"context {index}"] = sent

    def live(rows, first):
        frame = me * ROWS + first + lax.broadcasted_iota(jnp.int32, (rows, 128), 0)
        return jnp.logical_and(frame >= 0, frame < length)

    def column(chunk):
        return pl.ds(pl.multiple_of(chunk * 128, 128), 128)

    def turned_convolution(rows, columns):
        total = jnp.zeros((ROWS, 128), F32)
        for low in range(8):
            moved = shifted(rows, low)
            for high_part in range(4):
                tap = 31 - (8 * high_part + low)
                if 0 <= tap < KERNEL:
                    total = total + taps_ref[tap : tap + 1, columns] * moved[8 * high_part : 8 * high_part + ROWS]
        return total

    settle("w", "taps", "gain", "shift")

    @pl.loop(0, chunks)
    def _(chunk):
        columns = column(chunk)
        cmask_ref[:, columns] = turned_convolution(jnp.where(live(mid, -16), 1.0, 0.0), columns)

    settle("lengths in")
    lengths = len_recv[:, :1]
    count_a[...] = jnp.clip(lengths - (me * ROWS).astype(F32), 0.0, float(ROWS))
    for i in range(seq):
        count_b[i] = jnp.sum(jnp.clip(lengths - float(i * ROWS), 0.0, float(ROWS)), axis=0)
    for target in (tmask_ref, tgrad_ref, tnorm_ref):
        target[KERNEL:] = jnp.zeros((1, channels), F32)

    settle(*(f"halo {index} in" for index in range(4)))
    drain(ctx_recv, recv.at[8])

    for pair in range(heads // 2):
        ctx_ref[:, 128 * pair : 128 * pair + 128] = unpack_pair(
            ctx_recv[2 * pair].astype(F32), ctx_recv[2 * pair + 1].astype(F32)
        ).astype(BF16)

    counted = jnp.clip(length - me * ROWS, 0, ROWS).astype(F32)

    @pl.loop(0, channels // 256)
    def _(chunk):
        columns = pl.ds(pl.multiple_of(chunk * 256, 256), 256)
        hidden = x_ext[:, columns].astype(F32) + dot(ctx_ref[...], w_ref[:, columns])
        mask = live(ext, -HALO)
        mask = jnp.concatenate([mask, mask], axis=1)
        hid_ref[:, columns] = jnp.where(mask, hidden, 0.0).astype(BF16).astype(F32)

    @pl.loop(0, chunks)
    def _(chunk):
        columns = column(chunk)
        hidden = hid_ref[:, columns]
        total = jnp.zeros((mid, 128), F32)
        for low in range(8):
            moved = shifted(hidden, low)
            for high_part in range(4):
                tap = 8 * high_part + low - 1
                if 0 <= tap < KERNEL:
                    total = total + taps_ref[tap : tap + 1, columns] * moved[8 * high_part : 8 * high_part + mid]
        conv_ref[:, columns] = total
        own = total[16 : 16 + ROWS]
        mask = live(ROWS, 0)
        summed = jnp.sum(jnp.where(mask, own, 0.0), axis=0, keepdims=True)
        mean = summed / jnp.maximum(counted, 1.0)
        spread = own - mean
        squares = jnp.sum(jnp.where(mask, spread * spread, 0.0), axis=0, keepdims=True)
        stat_a[pl.ds(chunk, 1)] = summed
        stat_a[pl.ds(chunks + chunk, 1)] = squares


    def write(source, target, index):
        copy = pltpu.make_async_copy(source, target, write_sem.at[index])
        copy.start()
        pending[f"write {index}"] = copy.wait

    def gather(source, target, index, slot, count, peer, beside):
        target[slot] = source[...]

        @pl.loop(1, count)
        def _(d):
            remote(source, target.at[slot], send.at[index], recv.at[index], peer(d)).start()

        later(f"sums {index}", target.at[pl.ds(0, count - 1)], send.at[index])
        if beside is not None:
            beside()
        drain(target.at[pl.ds(0, count - 1)], recv.at[index])

    def gather_first(source, target, index, beside=None):
        gather(source, target, index, z, depth, lambda d: ((z + d) % depth, me), beside)

    def gather_second(source, target, index, beside=None):
        gather(source, target, index, me, seq, lambda d: (z, (me + d) % seq), beside)

    def correlate(target, rows, columns):
        hidden = hid_ref[16:, columns]
        for low in range(8):
            moved = shifted(hidden, low)
            for high_part in range(4):
                tap = 8 * high_part + low - 1
                if 0 <= tap < KERNEL:
                    terms = rows * moved[8 * high_part : 8 * high_part + ROWS]
                    target[tap : tap + 1, columns] = jnp.sum(terms, axis=0, keepdims=True)

    def correlate_mask():
        @pl.loop(0, chunks)
        def _(chunk):
            correlate(tmask_ref, jnp.where(live(ROWS, 0), 1.0, 0.0), column(chunk))

    def correlate_rest():
        @pl.loop(0, chunks)
        def _(chunk):
            columns = column(chunk)
            own = slice(16, 16 + ROWS)
            correlate(tgrad_ref, ga_ref[own, columns], columns)
            correlate(tnorm_ref, jnp.where(live(ROWS, 0), conv_ref[own, columns], 0.0), columns)

    def merged(gathered, counts):
        sums = gathered[:, :chunks]
        squares = gathered[:, chunks:]
        count = jnp.sum(counts, axis=0)
        total = jnp.sum(sums, axis=0)
        mean = total / jnp.maximum(count, 1.0)
        shift = sums / jnp.maximum(counts, 1.0) - mean[None]
        return total, jnp.sum(squares, axis=0) + jnp.sum(counts * shift * shift, axis=0), count, mean

    gather_first(stat_a, recv_a, 9, correlate_mask)
    total, squares, count, mean = merged(recv_a[...], count_a[...])
    stat_b[:chunks] = total
    stat_b[chunks:] = squares
    gather_second(stat_b, recv_b, 10)
    total, squares, count, mean = merged(recv_b[...], count_b[...])
    tot_ref[:chunks] = mean
    tot_ref[chunks : 2 * chunks] = lax.rsqrt(squares / count + EPSILON)
    tot_ref[2 * chunks : 3 * chunks] = jnp.broadcast_to(1.0 / count, (chunks, 128))

    @pl.loop(0, chunks)
    def _(chunk):
        columns = column(chunk)
        mean = tot_ref[pl.ds(chunk, 1)]
        inverse = tot_ref[pl.ds(chunks + chunk, 1)]
        normed = (conv_ref[:, columns] - mean) * inverse
        conv_ref[:, columns] = normed
        act = normed * gain_ref[:, columns] + shift_ref[:, columns]
        gate = 1.0 / (1.0 + jnp.exp(-act))
        grad_out = jnp.where(live(mid, -16), cot_ext[:, columns].astype(F32), 0.0)
        grad_act = grad_out * gate * (1.0 + act * (1.0 - gate))
        ga_ref[:, columns] = grad_act
        own = grad_act[16 : 16 + ROWS]
        stat_c[pl.ds(chunk, 1)] = jnp.sum(own * normed[16 : 16 + ROWS], axis=0, keepdims=True)
        stat_c[pl.ds(chunks + chunk, 1)] = jnp.sum(own, axis=0, keepdims=True)
        gated = (act * gate)[16 : 16 + ROWS]
        hidden = hid_ref[HALO : HALO + ROWS, columns]
        out_ref[:, columns] = jnp.where(live(ROWS, 0), hidden + gated, 0.0).astype(BF16)

    def beside():
        write(out_ref, out_hbm, 0)

        @pl.loop(0, chunks)
        def _(chunk):
            columns = column(chunk)
            cgrad_ref[:, columns] = turned_convolution(ga_ref[:, columns], columns)
            cnorm_ref[:, columns] = turned_convolution(
                jnp.where(live(mid, -16), conv_ref[:, columns], 0.0), columns
            )

    gather_first(stat_c, recv_c, 11, beside)
    stat_d[...] = jnp.sum(recv_c[...], axis=0)
    gather_second(stat_d, recv_d, 12, correlate_rest)
    sums_ref[...] = jnp.sum(recv_d[...], axis=0)

    @pl.loop(0, chunks)
    def _(chunk):
        columns = column(chunk)
        inverse = tot_ref[pl.ds(chunks + chunk, 1)]
        per_count = tot_ref[pl.ds(2 * chunks + chunk, 1)]
        gain_sum = sums_ref[pl.ds(chunk, 1)] * per_count
        shift_sum = sums_ref[pl.ds(chunks + chunk, 1)] * per_count
        scale = inverse * gain_ref[:, columns]
        turned = cgrad_ref[:, columns] - shift_sum * cmask_ref[:, columns] - gain_sum * cnorm_ref[:, columns]
        total = cot_ext[16 : 16 + ROWS, columns].astype(F32) + scale * turned
        ginp_ref[:, columns] = jnp.where(live(ROWS, 0), total, 0.0).astype(BF16)

    write(ginp_ref, ginp_hbm, 1)

    @pl.loop(0, heads // 2)
    def _(pair):
        rows = pl.ds(pl.multiple_of(pair * 128, 128), 128)
        grad_context = dot(ginp_ref[...], w_ref[rows], ((1,), (1,))).astype(BF16).astype(F32)
        even, odd = pack_pair(grad_context)
        do_send[2 * pair] = even.astype(BF16)
        do_send[2 * pair + 1] = odd.astype(BF16)

    to_heads(do_send, do_recv, 13, 14)

    own_context = jnp.transpose(ctx_ref[HALO : HALO + ROWS].astype(F32)).astype(BF16)

    def stage0(piece):
        copy = remote(
            wsend.at[piece].at[other], g0.at[piece], piece_send.at[5 * piece + 0], piece_recv.at[5 * piece + 0], partner
        )
        copy.start()
        pending[f"stage 0 in {piece}"] = copy.wait_recv
        pending[f"stage 0 out {piece}"] = copy.wait_send

    for piece in range(PIECES):
        first = piece * piece_width
        size = min(piece_width, channels - first)
        if size > 0:
            terms = dot(own_context, ginp_ref[:, first : first + size]).astype(BF16)
            wsend.at[piece][:, :, :, :size] = terms.reshape(2, chips, 16, size)
        if piece < PIECES - 1:
            stage0(piece)

    tap_lanes = slice(piece_width - 128, piece_width)
    wsend[PIECES - 1, :, :, :, tap_lanes] = jnp.zeros((2, chips, 16, 128), BF16)

    @pl.loop(0, chunks)
    def _(chunk):
        columns = column(chunk)
        per_count = tot_ref[pl.ds(2 * chunks + chunk, 1)]
        gain_sum = sums_ref[pl.ds(chunk, 1)] * per_count
        shift_sum = sums_ref[pl.ds(chunks + chunk, 1)] * per_count
        scale = tot_ref[pl.ds(chunks + chunk, 1)] * gain_ref[:, columns]
        stacked = tgrad_ref[:, columns] - shift_sum * tmask_ref[:, columns] - gain_sum * tnorm_ref[:, columns]
        stacked = (scale * stacked).astype(BF16)
        wsend.at[PIECES - 1].at[0][pl.ds(chunk, 1), :, tap_lanes] = stacked[:16].reshape(1, 16, 128)
        wsend.at[PIECES - 1].at[1][pl.ds(chunk, 1), :, tap_lanes] = stacked[16:].reshape(1, 16, 128)

    stage0(PIECES - 1)

    def stage1(piece):
        settle(f"stage 0 in {piece}")

        total = wsend.at[piece].at[core][...].astype(F32) + g0[piece].astype(F32)
        gs1[piece] = total.astype(BF16)
        g1.at[piece].at[chip][...] = gs1.at[piece].at[chip][...]

        @pl.loop(1, chips)
        def _(d):
            peer = (chip + d) % chips
            remote(
                gs1.at[piece].at[peer],
                g1.at[piece].at[chip],
                piece_send.at[5 * piece + 1],
                piece_recv.at[5 * piece + 1],
                (z, peer * 2 + core),
            ).start()

        later(f"stage 1 in {piece}", g1.at[piece].at[pl.ds(0, chips - 1)], piece_recv.at[5 * piece + 1])
        later(f"stage 1 out {piece}", g1.at[piece].at[pl.ds(0, chips - 1)], piece_send.at[5 * piece + 1])

    def stage2(piece):
        settle(f"stage 1 in {piece}")
        total = g1.at[piece][0].astype(F32)
        for i in range(1, chips):
            total = total + g1.at[piece][i].astype(F32)
        total = total.astype(BF16)
        gs2[piece] = total
        g2.at[piece].at[z][...] = total

        @pl.loop(1, depth)
        def _(d):
            remote(
                gs2.at[piece],
                g2.at[piece].at[z],
                piece_send.at[5 * piece + 2],
                piece_recv.at[5 * piece + 2],
                ((z + d) % depth, me),
            ).start()

        pending[f"stage 2 in {piece}"] = lambda: drain(
            g2.at[piece].at[pl.ds(0, depth - 1)], piece_recv.at[5 * piece + 2]
        )
        pending[f"stage 2 out {piece}"] = lambda: drain(
            g2.at[piece].at[pl.ds(0, depth - 1)], piece_send.at[5 * piece + 2]
        )

    def stage3(piece):
        settle(f"stage 2 in {piece}")
        total = g2.at[piece][0].astype(F32)
        for i in range(1, depth):
            total = total + g2.at[piece][i].astype(F32)
        gfin_ref.at[piece].at[core, chip][...] = total.astype(BF16)
        final = gfin_ref.at[piece].at[core, chip]

        @pl.loop(1, chips)
        def _(d):
            peer = (chip + d) % chips
            remote(
                final, final, piece_send.at[5 * piece + 3], piece_recv.at[5 * piece + 3], (z, peer * 2 + core)
            ).start()

        size = gfin_ref.at[piece].at[core, pl.ds(0, chips - 1)]
        later(f"stage 3 in {piece}", size, piece_recv.at[5 * piece + 3])
        later(f"stage 3 out {piece}", size, piece_send.at[5 * piece + 3])

    def stage4(piece):
        settle(f"stage 3 in {piece}")
        finals = gfin_ref.at[piece].at[core]
        copy = remote(finals, finals, piece_send.at[5 * piece + 4], piece_recv.at[5 * piece + 4], partner)
        copy.start()
        later(f"stage 4 in {piece}", gfin_ref.at[piece].at[other], piece_recv.at[5 * piece + 4])
        pending[f"stage 4 out {piece}"] = copy.wait_send

    for piece in range(PIECES):
        stage1(piece)

    settle("heads 13 in")
    for index in range(heads):
        rows = slice(ROWS * index, ROWS * index + ROWS)
        scaled = (unpack_high(do_recv[index].astype(F32)) * linv[rows]).astype(BF16)
        docl[rows] = scaled
        scaled = scaled.astype(F32)
        delta = jnp.sum(ctxh[rows] * scaled, axis=1, keepdims=True)
        first = delta.astype(BF16).astype(F32)
        rest = delta - first
        lane = lax.broadcasted_iota(jnp.int32, scaled.shape, 1)
        doaug[rows] = jnp.where(lane == 0, -first, jnp.where(lane == 1, -rest, scaled)).astype(BF16)

    dqt[...] = jnp.zeros_like(dqt)

    def part_copy(turn):
        rows = pl.ds(pl.multiple_of(turn * backward_block, backward_block), backward_block)
        return remote(dsend.at[rows], precv.at[rows], part_send.at[turn], part_recv.at[turn], partner)

    turns = 4
    slots = backward_block // ROWS

    @pl.loop(0, 2 * turns)
    def _(step):
        half = jnp.where(step < turns, other, core)
        turn = step % turns
        rows = pl.ds(
            pl.multiple_of(half * half_keys + turn * backward_block, backward_block), backward_block
        )
        turn_rows = pl.ds(pl.multiple_of(turn * backward_block, backward_block), backward_block)
        weights = pt[rows]
        grads = dot(v1[rows], doaug[...], ((1,), (1,))).astype(BF16)
        scores = weights * grads
        dqt[...] += dot(kt[:, rows], scores)
        rbuf[...] = dot(scores, qcl[...]) + dot(weights, docl[...])

        @pl.when(step < turns)
        def _():
            dsend[turn_rows] = rbuf[...].astype(BF16)
            part_copy(turn).start()

        @pl.when(step >= turns)
        def _():
            part_copy(turn).wait_recv()
            osend[turn_rows] = (rbuf[...] + precv[turn_rows].astype(F32)).astype(BF16)
            for i in range(slots):
                slot = turn * slots + i
                owner = (chip + chips - slot) % chips
                source = osend.at[pl.ds(pl.multiple_of(slot * ROWS, ROWS), ROWS)]

                def give(source=source, owner=owner):
                    remote(source, kvrecv.at[chip], own_sem, recv.at[20], (z, owner * 2 + core)).start()

                if i == 0:

                    @pl.when(turn == 0)
                    def _(source=source):
                        pltpu.make_async_copy(source, kvrecv.at[chip], recv.at[20]).start()

                    pl.when(turn > 0)(give)
                else:
                    give()

        for piece in range(PIECES):

            @pl.when(step == 2 + piece)
            def _(piece=piece):
                stage2(piece)

    def parts_sent():
        @pl.loop(0, turns)
        def _(turn):
            part_copy(turn).wait_send()

    pending["parts"] = parts_sent
    later("owned in", kvrecv, recv.at[20])
    later("owned out", kvrecv.at[pl.ds(0, chips - 1)], own_sem)

    @pl.loop(0, query_blocks)
    def _(block):
        part = pl.ds(pl.multiple_of(block * query_block, query_block), query_block)
        turned = dqt[:, part]
        turned = jnp.transpose(jnp.concatenate([turned, jnp.zeros_like(turned)], axis=0))
        half_part = pl.ds(pl.multiple_of(block * query_block // 2, query_block // 2), query_block // 2)
        dq_send[half_part] = pack_low(turned).astype(BF16)

    for i in range(heads):
        source = dq_send.at[pl.ds(64 * i, 64)]
        target = dq_recv.at[my_head]

        @pl.when(owner_of(i) == me)
        def _(source=source, target=target):
            pltpu.make_async_copy(source, target, recv.at[21]).start()

        @pl.when(owner_of(i) != me)
        def _(source=source, target=target, i=i):
            remote(source, target, dq_sem.at[i], recv.at[21], (z, owner_of(i))).start()

        def sent(source=source, i=i):
            @pl.when(owner_of(i) != me)
            def _():
                drain(source, dq_sem.at[i])

        pending[f"grad query {i}"] = sent

    for piece in range(PIECES):
        stage3(piece)

    settle("owned in")
    for pair in range(heads // 2):
        columns = slice(128 * pair, 128 * pair + 128)
        even = kvrecv[2 * pair].astype(F32) + kvrecv[2 * pair + heads].astype(F32)
        odd = kvrecv[2 * pair + 1].astype(F32) + kvrecv[2 * pair + 1 + heads].astype(F32)
        low = low_lanes(even.shape)
        gk_ref[:, columns] = jnp.where(low, even, roll64(odd)).astype(BF16)
        gv_ref[:, columns] = jnp.where(low, roll64(even), odd).astype(BF16)
    write(gk_ref, gk_hbm, 3)
    write(gv_ref, gv_hbm, 4)

    drain(dq_recv, recv.at[21])
    for pair in range(heads // 2):
        gq_ref[:, 128 * pair : 128 * pair + 128] = unpack_pair(
            dq_recv[2 * pair].astype(F32), dq_recv[2 * pair + 1].astype(F32)
        ).astype(BF16)

    write(gq_ref, gq_hbm, 2)
    for piece in range(PIECES):
        stage4(piece)
    settle()


def finish(width, chunks, *refs):
    out, ginp, gq, gk, gv, packed, sums = refs[:7]
    outs = refs[7:16]
    weights, taps, sem = refs[16:]
    channels = weights.shape[1]
    copies = [
        pltpu.make_async_copy(source, target, sem.at[index])
        for index, (source, target) in enumerate(
            (
                (out, outs[0]),
                (ginp, outs[1]),
                (gq, outs[2]),
                (gk, outs[3]),
                (gv, outs[4]),
                (weights, outs[5]),
                (taps, outs[6]),
                (sums.at[pl.ds(0, chunks)], outs[7]),
                (sums.at[pl.ds(chunks, chunks)], outs[8]),
            )
        )
    ]
    for index in (0, 1, 2, 3, 4, 7, 8):
        copies[index].start()
    piece_width = packed.shape[-1]
    for piece in range(PIECES):
        first = piece * piece_width
        size = min(piece_width, channels - first)
        for half in range(2 if size > 0 else 0):
            rows = slice(half * width // 2, (half + 1) * width // 2)
            terms = packed[piece, half, :, :, :size].astype(F32)
            weights[rows, first : first + size] = terms.reshape(width // 2, size)
    for chunk in range(chunks):
        lanes = slice(piece_width - 128, piece_width)
        columns = slice(128 * chunk, 128 * chunk + 128)
        taps[:16, columns] = packed[PIECES - 1, 0, chunk, :, lanes].astype(F32)
        taps[16:, columns] = packed[PIECES - 1, 1, chunk, :15, lanes].astype(F32)
    copies[5].start()
    copies[6].start()
    for copy in copies:
        copy.wait()


def shards(
    depth,
    query_rows,
    key_rows,
    value_rows,
    inputs,
    lengths,
    out_weight,
    taps,
    norm_gain,
    norm_shift,
    cotangent,
):
    seq = lax.axis_size("seq")
    heads = seq // 4
    chips = seq // 2
    width = query_rows.shape[2]
    channels = inputs.shape[2]
    chunks = channels // 128
    queries = ROWS * heads
    keys = seq * ROWS
    ext = ROWS + 2 * HALO
    mid = ROWS + 32
    padded = channels + 128
    piece_width = padded // PIECES
    query_block = min(queries, 512)
    vmem = pltpu.VMEM
    scratch = [
        vmem((ROWS, width), BF16),
        vmem((ROWS, width), BF16),
        vmem((ROWS, width), BF16),
        vmem((1, channels), F32),
        vmem((1, channels), F32),
        vmem((ROWS, channels), BF16),
        vmem((ROWS, channels), BF16),
        vmem((ROWS, width), BF16),
        vmem((ROWS, width), BF16),
        vmem((ROWS, width), BF16),
        vmem((8, 128), F32),
        vmem((depth, 8, 128), F32),
        vmem((ROWS, channels), F32),
        vmem((ROWS, channels), F32),
        vmem((ROWS, channels), F32),
        vmem((KERNEL + 1, channels), F32),
        vmem((KERNEL + 1, channels), F32),
        vmem((KERNEL + 1, channels), F32),
        vmem((depth, 1, 128), F32),
        vmem((seq, 1, 128), F32),
        vmem((heads, ROWS, 128), BF16),
        vmem((heads, 64, 128), BF16),
        vmem((keys, 128), BF16),
        vmem((heads, 64, 128), BF16),
        vmem((keys, 128), BF16),
        vmem((keys, 128), BF16),
        vmem((64, keys), BF16),
        vmem((128, keys), BF16),
        vmem((queries, 128), BF16),
        vmem((queries, 128), BF16),
        vmem((2, keys, query_block), F32),
        vmem((keys, queries), BF16),
        vmem((queries, 128), F32),
        vmem((queries, 128), F32),
        vmem((queries // 2, 128), BF16),
        vmem((heads, ext // 2, 128), BF16),
        vmem((ext, channels), BF16),
        vmem((mid, channels), BF16),
        vmem((width, channels), BF16),
        vmem((KERNEL, channels), F32),
        vmem((ext, width), BF16),
        vmem((ext, channels), F32),
        vmem((mid, channels), F32),
        vmem((mid, channels), F32),
        vmem((2 * chunks, 128), F32),
        vmem((2 * chunks, 128), F32),
        vmem((depth, 2 * chunks, 128), F32),
        vmem((seq, 2 * chunks, 128), F32),
        vmem((2 * chunks, 128), F32),
        vmem((depth, 2 * chunks, 128), F32),
        vmem((2 * chunks, 128), F32),
        vmem((seq, 2 * chunks, 128), F32),
        vmem((3 * chunks, 128), F32),
        vmem((heads, 64, 128), BF16),
        vmem((heads, 64, 128), BF16),
        vmem((queries, 128), BF16),
        vmem((queries, 128), BF16),
        vmem((keys // 8, 128), F32),
        vmem((64, queries), F32),
        vmem((keys // 2, 128), BF16),
        vmem((keys // 2, 128), BF16),
        vmem((keys // 2, 128), BF16),
        vmem((chips, ROWS, 128), BF16),
        vmem((queries // 2, 128), BF16),
        vmem((heads, 64, 128), BF16),
        vmem((PIECES, 2, chips, 16, piece_width), BF16),
        vmem((PIECES, chips, 16, piece_width), BF16),
        vmem((PIECES, chips, 16, piece_width), BF16),
        vmem((PIECES, chips, 16, piece_width), BF16),
        vmem((PIECES, 16, piece_width), BF16),
        vmem((PIECES, depth, 16, piece_width), BF16),
        pltpu.SemaphoreType.DMA((9,)),
        pltpu.SemaphoreType.DMA((25,)),
        pltpu.SemaphoreType.DMA((25,)),
        pltpu.SemaphoreType.DMA((heads + 2,)),
        pltpu.SemaphoreType.DMA((heads,)),
        pltpu.SemaphoreType.DMA((4,)),
        pltpu.SemaphoreType.DMA((4,)),
        pltpu.SemaphoreType.DMA,
        pltpu.SemaphoreType.DMA((5 * PIECES,)),
        pltpu.SemaphoreType.DMA((5 * PIECES,)),
        pltpu.SemaphoreType.DMA((5,)),
    ]
    in_vmem = pl.BlockSpec(memory_space=pltpu.VMEM)
    anywhere = pl.BlockSpec(memory_space=pl.ANY)
    plain = (
        jax.ShapeDtypeStruct((ROWS, channels), BF16),
        jax.ShapeDtypeStruct((ROWS, channels), BF16),
        jax.ShapeDtypeStruct((ROWS, width), BF16),
        jax.ShapeDtypeStruct((ROWS, width), BF16),
        jax.ShapeDtypeStruct((ROWS, width), BF16),
    )
    results = pl.pallas_call(
        functools.partial(kernel, heads, seq, depth),
        out_shape=plain
        + (
            jax.ShapeDtypeStruct((PIECES, 2, chips, 16, piece_width), BF16),
            jax.ShapeDtypeStruct((2 * chunks, 128), F32),
        ),
        in_specs=[pl.BlockSpec(memory_space=pltpu.SMEM)] + [anywhere] * 9,
        out_specs=(anywhere,) * 5 + (in_vmem,) * 2,
        scratch_shapes=scratch,
        compiler_params=pltpu.CompilerParams(
            collective_id=0, has_side_effects=True, vmem_limit_bytes=60 * 1024 * 1024
        ),
    )(
        lengths,
        query_rows[0],
        key_rows[0],
        value_rows[0],
        inputs[0],
        cotangent[0],
        out_weight,
        taps,
        norm_gain[None],
        norm_shift[None],
    )
    final = pl.pallas_call(
        functools.partial(finish, width, chunks),
        out_shape=plain
        + (
            jax.ShapeDtypeStruct((width, channels), F32),
            jax.ShapeDtypeStruct((KERNEL, channels), F32),
            jax.ShapeDtypeStruct((chunks, 128), F32),
            jax.ShapeDtypeStruct((chunks, 128), F32),
        ),
        in_specs=[anywhere] * 5 + [in_vmem] * 2,
        out_specs=(anywhere,) * 9,
        scratch_shapes=[
            vmem((width, channels), F32),
            vmem((KERNEL, channels), F32),
            pltpu.SemaphoreType.DMA((9,)),
        ],
        compiler_params=pltpu.CompilerParams(vmem_limit_bytes=60 * 1024 * 1024),
    )(*results)
    return (
        *(array[None] for array in final[:5]),
        final[5],
        final[6],
        final[7].reshape(channels),
        final[8].reshape(channels),
    )


def solution(mesh):
    rows = P("dp", "seq", None)
    return jax.shard_map(
        functools.partial(shards, mesh.shape["dp"]),
        mesh=mesh,
        in_specs=(rows, rows, rows, rows, P("dp"), P(), P(), P(), P(), rows),
        out_specs=(rows, rows, rows, rows, rows, P(), P(), P(), P()),
        check_vma=False,
    )
```

```python
import functools

import jax
import jax.numpy as jnp
from jax import lax
from jax.experimental import pallas as pl
from jax.experimental.pallas import tpu as pltpu
from jax.sharding import PartitionSpec as P

KERNEL = 31
HALF = 15
HEAD_DIM = 64
ROWS = 128
HALO = 32
NEGATIVE = -1e30
EPSILON = 1e-05
PIECES = 3
MESH = pl.DeviceIdType.MESH
F32 = jnp.float32
BF16 = jnp.bfloat16


def roll64(x):
    return pltpu.roll(x, 64, 1)


def low_lanes(shape):
    return lax.broadcasted_iota(jnp.int32, shape, 1) < 64


def split_units(x):
    rows = x.shape[0]
    units = x.reshape(rows // 32, 2, 16, 128)
    return units[:, 0].reshape(rows // 2, 128), units[:, 1].reshape(rows // 2, 128)


def join_units(first, second):
    rows = first.shape[0]
    first = first.reshape(rows // 16, 1, 16, 128)
    second = second.reshape(rows // 16, 1, 16, 128)
    return jnp.concatenate([first, second], axis=1).reshape(2 * rows, 128)


def pack_pair(x):
    first, second = split_units(x)
    low = low_lanes(first.shape)
    even = jnp.where(low, first, roll64(second))
    odd = jnp.where(low, roll64(first), second)
    return even, odd


def unpack_pair(even, odd):
    low = low_lanes(even.shape)
    return join_units(jnp.where(low, even, roll64(odd)), jnp.where(low, roll64(even), odd))


def unpack_low(packed):
    low = low_lanes(packed.shape)
    return join_units(jnp.where(low, packed, 0.0), jnp.where(low, roll64(packed), 0.0))


def unpack_high(packed):
    low = low_lanes(packed.shape)
    return join_units(jnp.where(low, 0.0, roll64(packed)), jnp.where(low, 0.0, packed))


def pack_low(x):
    first, second = split_units(x)
    return jnp.where(low_lanes(first.shape), first, roll64(second))


def pack_high(x):
    first, second = split_units(x)
    return jnp.where(low_lanes(first.shape), roll64(first), second)


def dot(a, b, dims=((1,), (0,))):
    return lax.dot_general(a, b, (dims, ((), ())), preferred_element_type=F32)


def shifted(x, amount):
    return x if amount == 0 else pltpu.roll(x, x.shape[0] - amount, 0)


def kernel(
    heads,
    seq,
    depth,
    length_ref,
    q_hbm,
    k_hbm,
    v_hbm,
    x_hbm,
    cot_hbm,
    w_hbm,
    taps_hbm,
    gain_hbm,
    shift_hbm,
    out_hbm,
    ginp_hbm,
    gq_hbm,
    gk_hbm,
    gv_hbm,
    gfin_ref,
    sums_ref,
    q_ref,
    k_ref,
    v_ref,
    gain_ref,
    shift_ref,
    out_ref,
    ginp_ref,
    gq_ref,
    gk_ref,
    gv_ref,
    len_send,
    len_recv,
    cmask_ref,
    cgrad_ref,
    cnorm_ref,
    tmask_ref,
    tgrad_ref,
    tnorm_ref,
    count_a,
    count_b,
    kv_send,
    q_send,
    kvbuf,
    qpk,
    k1,
    v1,
    kt,
    v1t,
    qaug,
    qcl,
    sbuf,
    pt,
    ctxh,
    linv,
    ctx_send,
    ctx_recv,
    x_ext,
    cot_ext,
    w_ref,
    taps_ref,
    ctx_ref,
    hid_ref,
    conv_ref,
    ga_ref,
    stat_a,
    stat_b,
    recv_a,
    recv_b,
    stat_c,
    recv_c,
    stat_d,
    recv_d,
    tot_ref,
    do_send,
    do_recv,
    doaug,
    docl,
    rbuf,
    dqt,
    dsend,
    precv,
    osend,
    kvrecv,
    dq_send,
    dq_recv,
    wsend,
    g0,
    gs1,
    g1,
    gs2,
    g2,
    load_sem,
    send,
    recv,
    ctx_sem,
    dq_sem,
    part_send,
    part_recv,
    own_sem,
    piece_send,
    piece_recv,
    write_sem,
):
    chips = seq // 2
    width = q_ref.shape[1]
    channels = out_ref.shape[1]
    chunks = channels // 128
    queries = ROWS * heads
    half_keys = chips * ROWS
    forward_block = half_keys // 2
    backward_block = half_keys // 4
    query_block = min(queries, 512)
    query_blocks = queries // query_block
    padded = channels + 128
    piece_width = padded // PIECES
    ext = ROWS + 2 * HALO
    mid = ROWS + 32

    z = lax.axis_index("dp")
    me = lax.axis_index("seq")
    chip = me // 2
    core = me % 2
    other = 1 - core
    partner = (z, chip * 2 + other)
    group = (chip // heads) * 2 + core
    my_group = me // heads
    length = length_ref[0]

    def remote(src, dst, send_sem, recv_sem, device):
        return pltpu.make_async_remote_copy(
            src_ref=src, dst_ref=dst, send_sem=send_sem, recv_sem=recv_sem, device_id=device, device_id_type=MESH
        )

    def drain(ref, sem):
        pltpu.make_async_copy(ref, ref, sem).wait()

    pending = {}

    def later(name, ref, sem):
        pending[name] = lambda: drain(ref, sem)

    def settle(*names):
        for name in names or tuple(pending):
            pending.pop(name)()

    barrier = pltpu.get_barrier_semaphore()

    @pl.loop(1, seq)
    def _(d):
        pl.semaphore_signal(barrier, inc=1, device_id=(z, (me + d) % seq), device_id_type=MESH)

    @pl.loop(1, depth)
    def _(d):
        pl.semaphore_signal(barrier, inc=1, device_id=((z + d) % depth, me), device_id_type=MESH)

    loads = (
        ("k", k_hbm, k_ref),
        ("v", v_hbm, v_ref),
        ("q", q_hbm, q_ref),
        ("x", x_hbm, x_ext.at[pl.ds(HALO, ROWS)]),
        ("cot", cot_hbm, cot_ext.at[pl.ds(16, ROWS)]),
        ("w", w_hbm, w_ref),
        ("taps", taps_hbm, taps_ref),
        ("gain", gain_hbm, gain_ref),
        ("shift", shift_hbm, shift_ref),
    )
    for index, (name, source, target) in enumerate(loads):
        copy = pltpu.make_async_copy(source, target, load_sem.at[index])
        copy.start()
        pending[name] = copy.wait

    len_send[...] = jnp.full((8, 128), length.astype(F32), F32)
    settle("k", "v", "q")
    for pair in range(heads // 2):
        columns = slice(128 * pair, 128 * pair + 128)
        kp = k_ref[:, columns].astype(F32)
        vp = v_ref[:, columns].astype(F32)
        low = low_lanes(kp.shape)
        kv_send[2 * pair] = jnp.where(low, kp, roll64(vp)).astype(BF16)
        kv_send[2 * pair + 1] = jnp.where(low, roll64(kp), vp).astype(BF16)
        even, odd = pack_pair(q_ref[:, columns].astype(F32))
        q_send[2 * pair] = even.astype(BF16)
        q_send[2 * pair + 1] = odd.astype(BF16)

    pl.semaphore_wait(barrier, seq - 1 + depth - 1)

    def kv_slot(d):
        return kvbuf.at[pl.ds(pl.multiple_of(core * half_keys + d * ROWS, ROWS), ROWS)]

    def send_keys(first, last, index):
        @pl.loop(first, last)
        def _(d):
            peer = (chip + d) % chips
            remote(kv_send.at[peer % heads], kv_slot(d), send.at[index], recv.at[index], (z, peer * 2 + core)).start()

    def quarter(half, index):
        return kvbuf.at[
            pl.ds(pl.multiple_of(half * half_keys + index * forward_block, forward_block), forward_block)
        ]

    some = chips // 2
    pltpu.make_async_copy(kv_send.at[chip % heads], kv_slot(0), recv.at[0]).start()
    send_keys(1, some, 0)
    later("keys 0 in", quarter(core, 0), recv.at[0])
    later("keys 0 out", kvbuf.at[pl.ds(0, (some - 1) * ROWS)], send.at[0])

    def head_device(head):
        return ((my_group // 2) * heads + head) * 2 + my_group % 2

    def to_heads(source, target, index, self_index):
        head = chip % heads
        slot = me % heads
        mine = head_device(head) == me

        @pl.when(mine)
        def _():
            pltpu.make_async_copy(source.at[head], target.at[slot], recv.at[index]).start()

        @pl.when(jnp.logical_not(mine))
        def _():
            remote(
                source.at[head], target.at[slot], send.at[self_index], recv.at[index], (z, head_device(head))
            ).start()

        @pl.loop(1, heads)
        def _(d):
            to = (chip + d) % heads
            remote(
                source.at[to], target.at[slot], send.at[index], recv.at[index], (z, head_device(to))
            ).start()

        def own_done():
            @pl.when(jnp.logical_not(mine))
            def _():
                drain(target.at[0], send.at[self_index])

        later(f"heads {index} in", target, recv.at[index])
        later(f"heads {index} out", target.at[pl.ds(0, heads - 1)], send.at[index])
        pending[f"heads {index} own"] = own_done

    to_heads(q_send, qpk, 1, 2)

    send_keys(some, chips, 22)
    later("keys 1 in", quarter(core, 1), recv.at[22])
    later("keys 1 out", kvbuf.at[pl.ds(0, some * ROWS)], send.at[22])

    len_recv[z] = len_send[...]

    @pl.loop(1, depth)
    def _(d):
        remote(len_send, len_recv.at[z], send.at[23], recv.at[23], ((z + d) % depth, me)).start()

    later("lengths in", len_recv.at[pl.ds(0, depth - 1)], recv.at[23])
    later("lengths out", len_recv.at[pl.ds(0, depth - 1)], send.at[23])

    after = (z, (me + 1) % seq)
    before = (z, (me + seq - 1) % seq)
    settle("x", "cot")
    halo_copies = (
        remote(x_ext.at[pl.ds(ROWS, HALO)], x_ext.at[pl.ds(0, HALO)], send.at[3], recv.at[3], after),
        remote(x_ext.at[pl.ds(HALO, HALO)], x_ext.at[pl.ds(HALO + ROWS, HALO)], send.at[4], recv.at[4], before),
        remote(cot_ext.at[pl.ds(ROWS, 16)], cot_ext.at[pl.ds(0, 16)], send.at[5], recv.at[5], after),
        remote(cot_ext.at[pl.ds(16, 16)], cot_ext.at[pl.ds(16 + ROWS, 16)], send.at[6], recv.at[6], before),
    )
    for index, copy in enumerate(halo_copies):
        copy.start()
        pending[f"halo {index} in"] = copy.wait_recv
        pending[f"halo {index} out"] = copy.wait_send

    def prepare_keys(half, index):
        rows_at_once = min(forward_block, 512)

        @pl.loop(0, forward_block // rows_at_once)
        def _(part):
            first = index * forward_block + part * rows_at_once
            rows = pl.ds(pl.multiple_of(half * half_keys + first, rows_at_once), rows_at_once)
            kv = kvbuf[rows].astype(F32)
            lane = lax.broadcasted_iota(jnp.int32, kv.shape, 1)
            row = lax.broadcasted_iota(jnp.int32, kv.shape, 0) + first
            source = chip - (row >> 7)
            source = jnp.where(source < 0, source + chips, source)
            frame = (source * 2 + half) * ROWS + (row & 127)
            bias = jnp.where(jnp.logical_and(lane == 64, frame >= length), NEGATIVE, 0.0)
            keyed = jnp.where(lane < 64, kv, bias)
            valued = jnp.where(lane < 64, 1.0, kv)
            k1[rows] = keyed.astype(BF16)
            v1[rows] = valued.astype(BF16)
            kt[:, rows] = jnp.transpose(kv)[:64].astype(BF16) * BF16(0.125)
            v1t[:, rows] = jnp.transpose(valued).astype(BF16)

    factor = 0.125 * 1.4426950408889634

    def block_rows(block):
        return pl.ds(pl.multiple_of(block * forward_block, forward_block), forward_block)

    def scores_step(part, block, highest):
        scores = dot(
            k1[block_rows(block)], qaug[part * query_block : (part + 1) * query_block], ((1,), (1,))
        )
        sbuf[part % 2, block_rows(block)] = scores
        return jnp.maximum(highest, jnp.max(scores.reshape(forward_block // 8, 8, query_block), axis=0))

    def weights_step(part, block, highest, total):
        rows = block_rows(block)
        weights = jnp.exp2((sbuf[part % 2, rows] - highest) * factor).astype(BF16)
        pt[rows, part * query_block : (part + 1) * query_block] = weights
        return total + dot(v1t[:, rows], weights)

    def context_finish(part, total):
        turned = jnp.transpose(total)
        low = low_lanes(turned.shape)
        inverse = 1.0 / jnp.where(low, 1.0, roll64(turned))
        context = jnp.where(low, 0.0, turned * inverse).astype(BF16).astype(F32)
        rows = slice(part * query_block, (part + 1) * query_block)
        linv[rows] = inverse
        ctxh[rows] = context
        half_rows = slice(part * query_block // 2, (part + 1) * query_block // 2)
        ctx_send[half_rows] = pack_high(context).astype(BF16)

    high = jnp.full((8, query_block), NEGATIVE, F32)
    for index in range(2):
        settle(f"keys {index} in")
        forward = remote(
            quarter(core, index), quarter(core, index), send.at[7 + 17 * index], recv.at[7 + 17 * index], partner
        )
        forward.start()
        later(f"forward {index} in", quarter(other, index), recv.at[7 + 17 * index])
        pending[f"forward {index} out"] = forward.wait_send
        prepare_keys(core, index)
        if index == 0:
            settle("heads 1 in")
            for slot in range(heads):
                rows = slice(ROWS * slot, ROWS * slot + ROWS)
                part = unpack_low(qpk[slot].astype(F32))
                lane = lax.broadcasted_iota(jnp.int32, part.shape, 1)
                qcl[rows] = (part * 0.125).astype(BF16)
                qaug[rows] = jnp.where(lane == 64, 1.0, part).astype(BF16)
        high = scores_step(0, core * 2 + index, high)
    for index in range(2):
        settle(f"forward {index} in")
        prepare_keys(other, index)
        high = scores_step(0, other * 2 + index, high)

    start_high = jnp.full((8, query_block), NEGATIVE, F32)
    start_total = jnp.zeros((128, query_block), F32)
    for part in range(query_blocks):
        highest = jnp.max(high, axis=0, keepdims=True)
        if part + 1 < query_blocks:

            def both(b, carried, part=part, highest=highest):
                h, t = carried
                return scores_step(part + 1, b, h), weights_step(part, b, highest, t)

            high, total = lax.fori_loop(0, 4, both, (start_high, start_total))
        else:
            total = lax.fori_loop(
                0, 4, lambda b, t, part=part, highest=highest: weights_step(part, b, highest, t), start_total
            )
        context_finish(part, total)

    my_head = chip % heads
    moves = [(-1, 0, 16, 80), (0, 0, 80, 16)]
    moves += [(i, 64 * i - 16, 96, 0) for i in range(1, heads - 1)]
    moves += [(heads - 1, 64 * (heads - 1) - 16, 80, 0), (heads, 64 * heads - 16, 16, 0)]

    def owner_of(i):
        return (group * heads + i + seq) % seq

    for index, (i, start, count, to) in enumerate(moves):
        source = ctx_send.at[pl.ds(start, count)]
        target = ctx_recv.at[my_head, pl.ds(to, count)]

        @pl.when(owner_of(i) == me)
        def _(source=source, target=target):
            pltpu.make_async_copy(source, target, recv.at[8]).start()

        @pl.when(owner_of(i) != me)
        def _(source=source, target=target, i=i, index=index):
            remote(source, target, ctx_sem.at[index], recv.at[8], (z, owner_of(i))).start()

        def sent(source=source, i=i, index=index):
            @pl.when(owner_of(i) != me)
            def _():
                drain(source, ctx_sem.at[index])

        pending[f"context {index}"] = sent

    def live(rows, first):
        frame = me * ROWS + first + lax.broadcasted_iota(jnp.int32, (rows, 128), 0)
        return jnp.logical_and(frame >= 0, frame < length)

    def column(chunk):
        return pl.ds(pl.multiple_of(chunk * 128, 128), 128)

    def turned_convolution(rows, columns):
        total = jnp.zeros((ROWS, 128), F32)
        for low in range(8):
            moved = shifted(rows, low)
            for high_part in range(4):
                tap = 31 - (8 * high_part + low)
                if 0 <= tap < KERNEL:
                    total = total + taps_ref[tap : tap + 1, columns] * moved[8 * high_part : 8 * high_part + ROWS]
        return total

    settle("w", "taps", "gain", "shift")

    @pl.loop(0, chunks)
    def _(chunk):
        columns = column(chunk)
        cmask_ref[:, columns] = turned_convolution(jnp.where(live(mid, -16), 1.0, 0.0), columns)

    settle("lengths in")
    lengths = len_recv[:, :1]
    count_a[...] = jnp.clip(lengths - (me * ROWS).astype(F32), 0.0, float(ROWS))
    for i in range(seq):
        count_b[i] = jnp.sum(jnp.clip(lengths - float(i * ROWS), 0.0, float(ROWS)), axis=0)
    for target in (tmask_ref, tgrad_ref, tnorm_ref):
        target[KERNEL:] = jnp.zeros((1, channels), F32)

    settle(*(f"halo {index} in" for index in range(4)))
    drain(ctx_recv, recv.at[8])

    for pair in range(heads // 2):
        ctx_ref[:, 128 * pair : 128 * pair + 128] = unpack_pair(
            ctx_recv[2 * pair].astype(F32), ctx_recv[2 * pair + 1].astype(F32)
        ).astype(BF16)

    counted = jnp.clip(length - me * ROWS, 0, ROWS).astype(F32)

    @pl.loop(0, channels // 256)
    def _(chunk):
        columns = pl.ds(pl.multiple_of(chunk * 256, 256), 256)
        hidden = x_ext[:, columns].astype(F32) + dot(ctx_ref[...], w_ref[:, columns])
        mask = live(ext, -HALO)
        mask = jnp.concatenate([mask, mask], axis=1)
        hid_ref[:, columns] = jnp.where(mask, hidden, 0.0).astype(BF16).astype(F32)

    @pl.loop(0, chunks)
    def _(chunk):
        columns = column(chunk)
        hidden = hid_ref[:, columns]
        total = jnp.zeros((mid, 128), F32)
        for low in range(8):
            moved = shifted(hidden, low)
            for high_part in range(4):
                tap = 8 * high_part + low - 1
                if 0 <= tap < KERNEL:
                    total = total + taps_ref[tap : tap + 1, columns] * moved[8 * high_part : 8 * high_part + mid]
        conv_ref[:, columns] = total
        own = total[16 : 16 + ROWS]
        mask = live(ROWS, 0)
        summed = jnp.sum(jnp.where(mask, own, 0.0), axis=0, keepdims=True)
        mean = summed / jnp.maximum(counted, 1.0)
        spread = own - mean
        squares = jnp.sum(jnp.where(mask, spread * spread, 0.0), axis=0, keepdims=True)
        stat_a[pl.ds(chunk, 1)] = summed
        stat_a[pl.ds(chunks + chunk, 1)] = squares


    def write(source, target, index):
        copy = pltpu.make_async_copy(source, target, write_sem.at[index])
        copy.start()
        pending[f"write {index}"] = copy.wait

    def gather(source, target, index, slot, count, peer, beside):
        target[slot] = source[...]

        @pl.loop(1, count)
        def _(d):
            remote(source, target.at[slot], send.at[index], recv.at[index], peer(d)).start()

        later(f"sums {index}", target.at[pl.ds(0, count - 1)], send.at[index])
        if beside is not None:
            beside()
        drain(target.at[pl.ds(0, count - 1)], recv.at[index])

    def gather_first(source, target, index, beside=None):
        gather(source, target, index, z, depth, lambda d: ((z + d) % depth, me), beside)

    def gather_second(source, target, index, beside=None):
        gather(source, target, index, me, seq, lambda d: (z, (me + d) % seq), beside)

    def correlate(target, rows, columns):
        hidden = hid_ref[16:, columns]
        for low in range(8):
            moved = shifted(hidden, low)
            for high_part in range(4):
                tap = 8 * high_part + low - 1
                if 0 <= tap < KERNEL:
                    terms = rows * moved[8 * high_part : 8 * high_part + ROWS]
                    target[tap : tap + 1, columns] = jnp.sum(terms, axis=0, keepdims=True)

    def correlate_mask():
        @pl.loop(0, chunks)
        def _(chunk):
            correlate(tmask_ref, jnp.where(live(ROWS, 0), 1.0, 0.0), column(chunk))

    def correlate_rest():
        @pl.loop(0, chunks)
        def _(chunk):
            columns = column(chunk)
            own = slice(16, 16 + ROWS)
            correlate(tgrad_ref, ga_ref[own, columns], columns)
            correlate(tnorm_ref, jnp.where(live(ROWS, 0), conv_ref[own, columns], 0.0), columns)

    def merged(gathered, counts):
        sums = gathered[:, :chunks]
        squares = gathered[:, chunks:]
        count = jnp.sum(counts, axis=0)
        total = jnp.sum(sums, axis=0)
        mean = total / jnp.maximum(count, 1.0)
        shift = sums / jnp.maximum(counts, 1.0) - mean[None]
        return total, jnp.sum(squares, axis=0) + jnp.sum(counts * shift * shift, axis=0), count, mean

    gather_first(stat_a, recv_a, 9, correlate_mask)
    total, squares, count, mean = merged(recv_a[...], count_a[...])
    stat_b[:chunks] = total
    stat_b[chunks:] = squares
    gather_second(stat_b, recv_b, 10)
    total, squares, count, mean = merged(recv_b[...], count_b[...])
    tot_ref[:chunks] = mean
    tot_ref[chunks : 2 * chunks] = lax.rsqrt(squares / count + EPSILON)
    tot_ref[2 * chunks : 3 * chunks] = jnp.broadcast_to(1.0 / count, (chunks, 128))

    @pl.loop(0, chunks)
    def _(chunk):
        columns = column(chunk)
        mean = tot_ref[pl.ds(chunk, 1)]
        inverse = tot_ref[pl.ds(chunks + chunk, 1)]
        normed = (conv_ref[:, columns] - mean) * inverse
        conv_ref[:, columns] = normed
        act = normed * gain_ref[:, columns] + shift_ref[:, columns]
        gate = 1.0 / (1.0 + jnp.exp(-act))
        grad_out = jnp.where(live(mid, -16), cot_ext[:, columns].astype(F32), 0.0)
        grad_act = grad_out * gate * (1.0 + act * (1.0 - gate))
        ga_ref[:, columns] = grad_act
        own = grad_act[16 : 16 + ROWS]
        stat_c[pl.ds(chunk, 1)] = jnp.sum(own * normed[16 : 16 + ROWS], axis=0, keepdims=True)
        stat_c[pl.ds(chunks + chunk, 1)] = jnp.sum(own, axis=0, keepdims=True)
        gated = (act * gate)[16 : 16 + ROWS]
        hidden = hid_ref[HALO : HALO + ROWS, columns]
        out_ref[:, columns] = jnp.where(live(ROWS, 0), hidden + gated, 0.0).astype(BF16)

    def beside():
        write(out_ref, out_hbm, 0)

        @pl.loop(0, chunks)
        def _(chunk):
            columns = column(chunk)
            cgrad_ref[:, columns] = turned_convolution(ga_ref[:, columns], columns)
            cnorm_ref[:, columns] = turned_convolution(
                jnp.where(live(mid, -16), conv_ref[:, columns], 0.0), columns
            )

    gather_first(stat_c, recv_c, 11, beside)
    stat_d[...] = jnp.sum(recv_c[...], axis=0)
    gather_second(stat_d, recv_d, 12, correlate_rest)
    sums_ref[...] = jnp.sum(recv_d[...], axis=0)

    @pl.loop(0, chunks)
    def _(chunk):
        columns = column(chunk)
        inverse = tot_ref[pl.ds(chunks + chunk, 1)]
        per_count = tot_ref[pl.ds(2 * chunks + chunk, 1)]
        gain_sum = sums_ref[pl.ds(chunk, 1)] * per_count
        shift_sum = sums_ref[pl.ds(chunks + chunk, 1)] * per_count
        scale = inverse * gain_ref[:, columns]
        turned = cgrad_ref[:, columns] - shift_sum * cmask_ref[:, columns] - gain_sum * cnorm_ref[:, columns]
        total = cot_ext[16 : 16 + ROWS, columns].astype(F32) + scale * turned
        ginp_ref[:, columns] = jnp.where(live(ROWS, 0), total, 0.0).astype(BF16)

    write(ginp_ref, ginp_hbm, 1)

    @pl.loop(0, heads // 2)
    def _(pair):
        rows = pl.ds(pl.multiple_of(pair * 128, 128), 128)
        grad_context = dot(ginp_ref[...], w_ref[rows], ((1,), (1,))).astype(BF16).astype(F32)
        even, odd = pack_pair(grad_context)
        do_send[2 * pair] = even.astype(BF16)
        do_send[2 * pair + 1] = odd.astype(BF16)

    to_heads(do_send, do_recv, 13, 14)

    own_context = jnp.transpose(ctx_ref[HALO : HALO + ROWS].astype(F32)).astype(BF16)

    def stage0(piece):
        copy = remote(
            wsend.at[piece].at[other], g0.at[piece], piece_send.at[5 * piece + 0], piece_recv.at[5 * piece + 0], partner
        )
        copy.start()
        pending[f"stage 0 in {piece}"] = copy.wait_recv
        pending[f"stage 0 out {piece}"] = copy.wait_send

    for piece in range(PIECES):
        first = piece * piece_width
        size = min(piece_width, channels - first)
        if size > 0:
            terms = dot(own_context, ginp_ref[:, first : first + size]).astype(BF16)
            wsend.at[piece][:, :, :, :size] = terms.reshape(2, chips, 16, size)
        if piece < PIECES - 1:
            stage0(piece)

    tap_lanes = slice(piece_width - 128, piece_width)
    wsend[PIECES - 1, :, :, :, tap_lanes] = jnp.zeros((2, chips, 16, 128), BF16)

    @pl.loop(0, chunks)
    def _(chunk):
        columns = column(chunk)
        per_count = tot_ref[pl.ds(2 * chunks + chunk, 1)]
        gain_sum = sums_ref[pl.ds(chunk, 1)] * per_count
        shift_sum = sums_ref[pl.ds(chunks + chunk, 1)] * per_count
        scale = tot_ref[pl.ds(chunks + chunk, 1)] * gain_ref[:, columns]
        stacked = tgrad_ref[:, columns] - shift_sum * tmask_ref[:, columns] - gain_sum * tnorm_ref[:, columns]
        stacked = (scale * stacked).astype(BF16)
        wsend.at[PIECES - 1].at[0][pl.ds(chunk, 1), :, tap_lanes] = stacked[:16].reshape(1, 16, 128)
        wsend.at[PIECES - 1].at[1][pl.ds(chunk, 1), :, tap_lanes] = stacked[16:].reshape(1, 16, 128)

    stage0(PIECES - 1)

    def stage1(piece):
        settle(f"stage 0 in {piece}")

        total = wsend.at[piece].at[core][...].astype(F32) + g0[piece].astype(F32)
        gs1[piece] = total.astype(BF16)
        g1.at[piece].at[chip][...] = gs1.at[piece].at[chip][...]

        @pl.loop(1, chips)
        def _(d):
            peer = (chip + d) % chips
            remote(
                gs1.at[piece].at[peer],
                g1.at[piece].at[chip],
                piece_send.at[5 * piece + 1],
                piece_recv.at[5 * piece + 1],
                (z, peer * 2 + core),
            ).start()

        later(f"stage 1 in {piece}", g1.at[piece].at[pl.ds(0, chips - 1)], piece_recv.at[5 * piece + 1])
        later(f"stage 1 out {piece}", g1.at[piece].at[pl.ds(0, chips - 1)], piece_send.at[5 * piece + 1])

    def stage2(piece):
        settle(f"stage 1 in {piece}")
        total = g1.at[piece][0].astype(F32)
        for i in range(1, chips):
            total = total + g1.at[piece][i].astype(F32)
        total = total.astype(BF16)
        gs2[piece] = total
        g2.at[piece].at[z][...] = total

        @pl.loop(1, depth)
        def _(d):
            remote(
                gs2.at[piece],
                g2.at[piece].at[z],
                piece_send.at[5 * piece + 2],
                piece_recv.at[5 * piece + 2],
                ((z + d) % depth, me),
            ).start()

        pending[f"stage 2 in {piece}"] = lambda: drain(
            g2.at[piece].at[pl.ds(0, depth - 1)], piece_recv.at[5 * piece + 2]
        )
        pending[f"stage 2 out {piece}"] = lambda: drain(
            g2.at[piece].at[pl.ds(0, depth - 1)], piece_send.at[5 * piece + 2]
        )

    def stage3(piece):
        settle(f"stage 2 in {piece}")
        total = g2.at[piece][0].astype(F32)
        for i in range(1, depth):
            total = total + g2.at[piece][i].astype(F32)
        gfin_ref.at[piece].at[core, chip][...] = total.astype(BF16)
        final = gfin_ref.at[piece].at[core, chip]

        @pl.loop(1, chips)
        def _(d):
            peer = (chip + d) % chips
            remote(
                final, final, piece_send.at[5 * piece + 3], piece_recv.at[5 * piece + 3], (z, peer * 2 + core)
            ).start()

        size = gfin_ref.at[piece].at[core, pl.ds(0, chips - 1)]
        later(f"stage 3 in {piece}", size, piece_recv.at[5 * piece + 3])
        later(f"stage 3 out {piece}", size, piece_send.at[5 * piece + 3])

    def stage4(piece):
        settle(f"stage 3 in {piece}")
        finals = gfin_ref.at[piece].at[core]
        copy = remote(finals, finals, piece_send.at[5 * piece + 4], piece_recv.at[5 * piece + 4], partner)
        copy.start()
        later(f"stage 4 in {piece}", gfin_ref.at[piece].at[other], piece_recv.at[5 * piece + 4])
        pending[f"stage 4 out {piece}"] = copy.wait_send

    for piece in range(PIECES):
        stage1(piece)

    settle("heads 13 in")
    for index in range(heads):
        rows = slice(ROWS * index, ROWS * index + ROWS)
        scaled = (unpack_high(do_recv[index].astype(F32)) * linv[rows]).astype(BF16)
        docl[rows] = scaled
        scaled = scaled.astype(F32)
        delta = jnp.sum(ctxh[rows] * scaled, axis=1, keepdims=True)
        first = delta.astype(BF16).astype(F32)
        rest = delta - first
        lane = lax.broadcasted_iota(jnp.int32, scaled.shape, 1)
        doaug[rows] = jnp.where(lane == 0, -first, jnp.where(lane == 1, -rest, scaled)).astype(BF16)

    dqt[...] = jnp.zeros_like(dqt)

    def part_copy(turn):
        rows = pl.ds(pl.multiple_of(turn * backward_block, backward_block), backward_block)
        return remote(dsend.at[rows], precv.at[rows], part_send.at[turn], part_recv.at[turn], partner)

    turns = 4
    slots = backward_block // ROWS

    @pl.loop(0, 2 * turns)
    def _(step):
        half = jnp.where(step < turns, other, core)
        turn = step % turns
        rows = pl.ds(
            pl.multiple_of(half * half_keys + turn * backward_block, backward_block), backward_block
        )
        turn_rows = pl.ds(pl.multiple_of(turn * backward_block, backward_block), backward_block)
        weights = pt[rows]
        grads = dot(v1[rows], doaug[...], ((1,), (1,))).astype(BF16)
        scores = weights * grads
        dqt[...] += dot(kt[:, rows], scores)
        rbuf[...] = dot(scores, qcl[...]) + dot(weights, docl[...])

        @pl.when(step < turns)
        def _():
            dsend[turn_rows] = rbuf[...].astype(BF16)
            part_copy(turn).start()

        @pl.when(step >= turns)
        def _():
            part_copy(turn).wait_recv()
            osend[turn_rows] = (rbuf[...] + precv[turn_rows].astype(F32)).astype(BF16)
            for i in range(slots):
                slot = turn * slots + i
                owner = (chip + chips - slot) % chips
                source = osend.at[pl.ds(pl.multiple_of(slot * ROWS, ROWS), ROWS)]

                def give(source=source, owner=owner):
                    remote(source, kvrecv.at[chip], own_sem, recv.at[20], (z, owner * 2 + core)).start()

                if i == 0:

                    @pl.when(turn == 0)
                    def _(source=source):
                        pltpu.make_async_copy(source, kvrecv.at[chip], recv.at[20]).start()

                    pl.when(turn > 0)(give)
                else:
                    give()

        for piece in range(PIECES):

            @pl.when(step == 2 + piece)
            def _(piece=piece):
                stage2(piece)

    def parts_sent():
        @pl.loop(0, turns)
        def _(turn):
            part_copy(turn).wait_send()

    pending["parts"] = parts_sent
    later("owned in", kvrecv, recv.at[20])
    later("owned out", kvrecv.at[pl.ds(0, chips - 1)], own_sem)

    @pl.loop(0, query_blocks)
    def _(block):
        part = pl.ds(pl.multiple_of(block * query_block, query_block), query_block)
        turned = dqt[:, part]
        turned = jnp.transpose(jnp.concatenate([turned, jnp.zeros_like(turned)], axis=0))
        half_part = pl.ds(pl.multiple_of(block * query_block // 2, query_block // 2), query_block // 2)
        dq_send[half_part] = pack_low(turned).astype(BF16)

    for i in range(heads):
        source = dq_send.at[pl.ds(64 * i, 64)]
        target = dq_recv.at[my_head]

        @pl.when(owner_of(i) == me)
        def _(source=source, target=target):
            pltpu.make_async_copy(source, target, recv.at[21]).start()

        @pl.when(owner_of(i) != me)
        def _(source=source, target=target, i=i):
            remote(source, target, dq_sem.at[i], recv.at[21], (z, owner_of(i))).start()

        def sent(source=source, i=i):
            @pl.when(owner_of(i) != me)
            def _():
                drain(source, dq_sem.at[i])

        pending[f"grad query {i}"] = sent

    for piece in range(PIECES):
        stage3(piece)

    settle("owned in")
    for pair in range(heads // 2):
        columns = slice(128 * pair, 128 * pair + 128)
        even = kvrecv[2 * pair].astype(F32) + kvrecv[2 * pair + heads].astype(F32)
        odd = kvrecv[2 * pair + 1].astype(F32) + kvrecv[2 * pair + 1 + heads].astype(F32)
        low = low_lanes(even.shape)
        gk_ref[:, columns] = jnp.where(low, even, roll64(odd)).astype(BF16)
        gv_ref[:, columns] = jnp.where(low, roll64(even), odd).astype(BF16)
    write(gk_ref, gk_hbm, 3)
    write(gv_ref, gv_hbm, 4)

    drain(dq_recv, recv.at[21])
    for pair in range(heads // 2):
        gq_ref[:, 128 * pair : 128 * pair + 128] = unpack_pair(
            dq_recv[2 * pair].astype(F32), dq_recv[2 * pair + 1].astype(F32)
        ).astype(BF16)

    write(gq_ref, gq_hbm, 2)
    for piece in range(PIECES):
        stage4(piece)
    settle()


def finish(width, chunks, *refs):
    sources = refs[:7]
    outs = refs[7:16]
    out, ginp, gq, gk, gv, packed, sums = refs[16:23]
    weights, taps, load_sem, sem = refs[23:]
    channels = weights.shape[1]
    loads = [
        pltpu.make_async_copy(source, target, load_sem.at[index])
        for index, (source, target) in enumerate(zip(sources, refs[16:23]))
    ]
    for index in (5, 6, 0, 1, 2, 3, 4):
        loads[index].start()
    copies = [
        pltpu.make_async_copy(source, target, sem.at[index])
        for index, (source, target) in enumerate(
            (
                (out, outs[0]),
                (ginp, outs[1]),
                (gq, outs[2]),
                (gk, outs[3]),
                (gv, outs[4]),
                (weights, outs[5]),
                (taps, outs[6]),
                (sums.at[pl.ds(0, chunks)], outs[7]),
                (sums.at[pl.ds(chunks, chunks)], outs[8]),
            )
        )
    ]
    loads[5].wait()
    piece_width = packed.shape[-1]
    for piece in range(PIECES):
        first = piece * piece_width
        size = min(piece_width, channels - first)
        for half in range(2 if size > 0 else 0):
            rows = slice(half * width // 2, (half + 1) * width // 2)
            terms = packed[piece, half, :, :, :size].astype(F32)
            weights[rows, first : first + size] = terms.reshape(width // 2, size)
    for chunk in range(chunks):
        lanes = slice(piece_width - 128, piece_width)
        columns = slice(128 * chunk, 128 * chunk + 128)
        taps[:16, columns] = packed[PIECES - 1, 0, chunk, :, lanes].astype(F32)
        taps[16:, columns] = packed[PIECES - 1, 1, chunk, :15, lanes].astype(F32)
    copies[5].start()
    copies[6].start()
    loads[6].wait()
    copies[7].start()
    copies[8].start()
    for index in range(5):
        loads[index].wait()
        copies[index].start()
    for copy in copies:
        copy.wait()


def shards(
    depth,
    query_rows,
    key_rows,
    value_rows,
    inputs,
    lengths,
    out_weight,
    taps,
    norm_gain,
    norm_shift,
    cotangent,
):
    seq = lax.axis_size("seq")
    heads = seq // 4
    chips = seq // 2
    width = query_rows.shape[2]
    channels = inputs.shape[2]
    chunks = channels // 128
    queries = ROWS * heads
    keys = seq * ROWS
    ext = ROWS + 2 * HALO
    mid = ROWS + 32
    padded = channels + 128
    piece_width = padded // PIECES
    query_block = min(queries, 512)
    vmem = pltpu.VMEM
    scratch = [
        vmem((ROWS, width), BF16),
        vmem((ROWS, width), BF16),
        vmem((ROWS, width), BF16),
        vmem((1, channels), F32),
        vmem((1, channels), F32),
        vmem((ROWS, channels), BF16),
        vmem((ROWS, channels), BF16),
        vmem((ROWS, width), BF16),
        vmem((ROWS, width), BF16),
        vmem((ROWS, width), BF16),
        vmem((8, 128), F32),
        vmem((depth, 8, 128), F32),
        vmem((ROWS, channels), F32),
        vmem((ROWS, channels), F32),
        vmem((ROWS, channels), F32),
        vmem((KERNEL + 1, channels), F32),
        vmem((KERNEL + 1, channels), F32),
        vmem((KERNEL + 1, channels), F32),
        vmem((depth, 1, 128), F32),
        vmem((seq, 1, 128), F32),
        vmem((heads, ROWS, 128), BF16),
        vmem((heads, 64, 128), BF16),
        vmem((keys, 128), BF16),
        vmem((heads, 64, 128), BF16),
        vmem((keys, 128), BF16),
        vmem((keys, 128), BF16),
        vmem((64, keys), BF16),
        vmem((128, keys), BF16),
        vmem((queries, 128), BF16),
        vmem((queries, 128), BF16),
        vmem((2, keys, query_block), F32),
        vmem((keys, queries), BF16),
        vmem((queries, 128), F32),
        vmem((queries, 128), F32),
        vmem((queries // 2, 128), BF16),
        vmem((heads, ext // 2, 128), BF16),
        vmem((ext, channels), BF16),
        vmem((mid, channels), BF16),
        vmem((width, channels), BF16),
        vmem((KERNEL, channels), F32),
        vmem((ext, width), BF16),
        vmem((ext, channels), F32),
        vmem((mid, channels), F32),
        vmem((mid, channels), F32),
        vmem((2 * chunks, 128), F32),
        vmem((2 * chunks, 128), F32),
        vmem((depth, 2 * chunks, 128), F32),
        vmem((seq, 2 * chunks, 128), F32),
        vmem((2 * chunks, 128), F32),
        vmem((depth, 2 * chunks, 128), F32),
        vmem((2 * chunks, 128), F32),
        vmem((seq, 2 * chunks, 128), F32),
        vmem((3 * chunks, 128), F32),
        vmem((heads, 64, 128), BF16),
        vmem((heads, 64, 128), BF16),
        vmem((queries, 128), BF16),
        vmem((queries, 128), BF16),
        vmem((keys // 8, 128), F32),
        vmem((64, queries), F32),
        vmem((keys // 2, 128), BF16),
        vmem((keys // 2, 128), BF16),
        vmem((keys // 2, 128), BF16),
        vmem((chips, ROWS, 128), BF16),
        vmem((queries // 2, 128), BF16),
        vmem((heads, 64, 128), BF16),
        vmem((PIECES, 2, chips, 16, piece_width), BF16),
        vmem((PIECES, chips, 16, piece_width), BF16),
        vmem((PIECES, chips, 16, piece_width), BF16),
        vmem((PIECES, chips, 16, piece_width), BF16),
        vmem((PIECES, 16, piece_width), BF16),
        vmem((PIECES, depth, 16, piece_width), BF16),
        pltpu.SemaphoreType.DMA((9,)),
        pltpu.SemaphoreType.DMA((25,)),
        pltpu.SemaphoreType.DMA((25,)),
        pltpu.SemaphoreType.DMA((heads + 2,)),
        pltpu.SemaphoreType.DMA((heads,)),
        pltpu.SemaphoreType.DMA((4,)),
        pltpu.SemaphoreType.DMA((4,)),
        pltpu.SemaphoreType.DMA,
        pltpu.SemaphoreType.DMA((5 * PIECES,)),
        pltpu.SemaphoreType.DMA((5 * PIECES,)),
        pltpu.SemaphoreType.DMA((5,)),
    ]
    in_vmem = pl.BlockSpec(memory_space=pltpu.VMEM)
    anywhere = pl.BlockSpec(memory_space=pl.ANY)
    plain = (
        jax.ShapeDtypeStruct((ROWS, channels), BF16),
        jax.ShapeDtypeStruct((ROWS, channels), BF16),
        jax.ShapeDtypeStruct((ROWS, width), BF16),
        jax.ShapeDtypeStruct((ROWS, width), BF16),
        jax.ShapeDtypeStruct((ROWS, width), BF16),
    )
    results = pl.pallas_call(
        functools.partial(kernel, heads, seq, depth),
        out_shape=plain
        + (
            jax.ShapeDtypeStruct((PIECES, 2, chips, 16, piece_width), BF16),
            jax.ShapeDtypeStruct((2 * chunks, 128), F32),
        ),
        in_specs=[pl.BlockSpec(memory_space=pltpu.SMEM)] + [anywhere] * 9,
        out_specs=(anywhere,) * 5 + (in_vmem,) * 2,
        scratch_shapes=scratch,
        compiler_params=pltpu.CompilerParams(
            collective_id=0, has_side_effects=True, vmem_limit_bytes=60 * 1024 * 1024
        ),
    )(
        lengths,
        query_rows[0],
        key_rows[0],
        value_rows[0],
        inputs[0],
        cotangent[0],
        out_weight,
        taps,
        norm_gain[None],
        norm_shift[None],
    )
    final = pl.pallas_call(
        functools.partial(finish, width, chunks),
        out_shape=plain
        + (
            jax.ShapeDtypeStruct((width, channels), F32),
            jax.ShapeDtypeStruct((KERNEL, channels), F32),
            jax.ShapeDtypeStruct((chunks, 128), F32),
            jax.ShapeDtypeStruct((chunks, 128), F32),
        ),
        in_specs=[anywhere] * 7,
        out_specs=(anywhere,) * 9,
        scratch_shapes=[vmem(array.shape, array.dtype) for array in results]
        + [
            vmem((width, channels), F32),
            vmem((KERNEL, channels), F32),
            pltpu.SemaphoreType.DMA((7,)),
            pltpu.SemaphoreType.DMA((9,)),
        ],
        compiler_params=pltpu.CompilerParams(vmem_limit_bytes=60 * 1024 * 1024),
    )(*results)
    return (
        *(array[None] for array in final[:5]),
        final[5],
        final[6],
        final[7].reshape(channels),
        final[8].reshape(channels),
    )


def solution(mesh):
    rows = P("dp", "seq", None)
    return jax.shard_map(
        functools.partial(shards, mesh.shape["dp"]),
        mesh=mesh,
        in_specs=(rows, rows, rows, rows, P("dp"), P(), P(), P(), P(), rows),
        out_specs=(rows, rows, rows, rows, rows, P(), P(), P(), P()),
        check_vma=False,
    )
```

```python
import functools

import jax
import jax.numpy as jnp
from jax import lax
from jax.experimental import pallas as pl
from jax.experimental.pallas import tpu as pltpu
from jax.sharding import PartitionSpec as P

KERNEL = 31
HALF = 15
HEAD_DIM = 64
ROWS = 128
HALO = 32
NEGATIVE = -1e30
EPSILON = 1e-05
PIECES = 3
MESH = pl.DeviceIdType.MESH
F32 = jnp.float32
BF16 = jnp.bfloat16


def roll64(x):
    return pltpu.roll(x, 64, 1)


def low_lanes(shape):
    return lax.broadcasted_iota(jnp.int32, shape, 1) < 64


def split_units(x):
    rows = x.shape[0]
    units = x.reshape(rows // 32, 2, 16, 128)
    return units[:, 0].reshape(rows // 2, 128), units[:, 1].reshape(rows // 2, 128)


def join_units(first, second):
    rows = first.shape[0]
    first = first.reshape(rows // 16, 1, 16, 128)
    second = second.reshape(rows // 16, 1, 16, 128)
    return jnp.concatenate([first, second], axis=1).reshape(2 * rows, 128)


def pack_pair(x):
    first, second = split_units(x)
    low = low_lanes(first.shape)
    even = jnp.where(low, first, roll64(second))
    odd = jnp.where(low, roll64(first), second)
    return even, odd


def unpack_pair(even, odd):
    low = low_lanes(even.shape)
    return join_units(jnp.where(low, even, roll64(odd)), jnp.where(low, roll64(even), odd))


def unpack_low(packed):
    low = low_lanes(packed.shape)
    return join_units(jnp.where(low, packed, 0.0), jnp.where(low, roll64(packed), 0.0))


def unpack_high(packed):
    low = low_lanes(packed.shape)
    return join_units(jnp.where(low, 0.0, roll64(packed)), jnp.where(low, 0.0, packed))


def pack_low(x):
    first, second = split_units(x)
    return jnp.where(low_lanes(first.shape), first, roll64(second))


def pack_high(x):
    first, second = split_units(x)
    return jnp.where(low_lanes(first.shape), roll64(first), second)


def dot(a, b, dims=((1,), (0,))):
    return lax.dot_general(a, b, (dims, ((), ())), preferred_element_type=F32)


def shifted(x, amount):
    return x if amount == 0 else pltpu.roll(x, x.shape[0] - amount, 0)


def kernel(
    heads,
    seq,
    depth,
    length_ref,
    q_hbm,
    k_hbm,
    v_hbm,
    x_hbm,
    cot_hbm,
    w_hbm,
    taps_hbm,
    gain_hbm,
    shift_hbm,
    out_hbm,
    ginp_hbm,
    gq_hbm,
    gk_hbm,
    gv_hbm,
    gfin_ref,
    sums_ref,
    q_ref,
    k_ref,
    v_ref,
    gain_ref,
    shift_ref,
    out_ref,
    ginp_ref,
    gq_ref,
    gk_ref,
    gv_ref,
    len_send,
    len_recv,
    cmask_ref,
    cgrad_ref,
    cnorm_ref,
    own_ctx,
    tmask_ref,
    tgrad_ref,
    tnorm_ref,
    count_a,
    count_b,
    kv_send,
    q_send,
    kvbuf,
    qpk,
    k1,
    v1,
    kt,
    v1t,
    qaug,
    qcl,
    sbuf,
    pt,
    ctxh,
    linv,
    ctx_send,
    ctx_recv,
    x_ext,
    cot_ext,
    w_ref,
    taps_ref,
    ctx_ref,
    hid_ref,
    conv_ref,
    ga_ref,
    stat_a,
    stat_b,
    recv_a,
    recv_b,
    stat_c,
    recv_c,
    stat_d,
    recv_d,
    tot_ref,
    do_send,
    do_recv,
    doaug,
    docl,
    rbuf,
    dqt,
    dsend,
    precv,
    osend,
    kvrecv,
    dq_send,
    dq_recv,
    wsend,
    g0,
    gs1,
    g1,
    gs2,
    g2,
    load_sem,
    send,
    recv,
    ctx_sem,
    dq_sem,
    part_send,
    part_recv,
    own_sem,
    piece_send,
    piece_recv,
    write_sem,
):
    chips = seq // 2
    width = q_ref.shape[1]
    channels = out_ref.shape[1]
    chunks = channels // 128
    queries = ROWS * heads
    half_keys = chips * ROWS
    forward_block = half_keys // 2
    backward_block = half_keys // 4
    query_block = min(queries, 512)
    query_blocks = queries // query_block
    padded = channels + 128
    piece_width = padded // PIECES
    ext = ROWS + 2 * HALO
    mid = ROWS + 32

    z = lax.axis_index("dp")
    me = lax.axis_index("seq")
    chip = me // 2
    core = me % 2
    other = 1 - core
    partner = (z, chip * 2 + other)
    group = (chip // heads) * 2 + core
    my_group = me // heads
    length = length_ref[0]

    def remote(src, dst, send_sem, recv_sem, device):
        return pltpu.make_async_remote_copy(
            src_ref=src, dst_ref=dst, send_sem=send_sem, recv_sem=recv_sem, device_id=device, device_id_type=MESH
        )

    def drain(ref, sem):
        pltpu.make_async_copy(ref, ref, sem).wait()

    pending = {}

    def later(name, ref, sem):
        pending[name] = lambda: drain(ref, sem)

    def settle(*names):
        for name in names or tuple(pending):
            pending.pop(name)()

    def around(count, act):
        act(count // 2)

        @pl.loop(1, count // 2)
        def _(k):
            act(count // 2 + k)
            act(count // 2 - k)

    barrier = pltpu.get_barrier_semaphore()

    def greet(device):
        pl.semaphore_signal(barrier, inc=1, device_id=device, device_id_type=MESH)

    around(depth, lambda d: greet(((z + d) % depth, me)))
    around(seq, lambda d: greet((z, (me + d) % seq)))


    loads = (
        ("k", k_hbm, k_ref),
        ("v", v_hbm, v_ref),
        ("q", q_hbm, q_ref),
        ("x", x_hbm, x_ext.at[pl.ds(HALO, ROWS)]),
        ("cot", cot_hbm, cot_ext.at[pl.ds(16, ROWS)]),
        ("w", w_hbm, w_ref),
        ("taps", taps_hbm, taps_ref),
        ("gain", gain_hbm, gain_ref),
        ("shift", shift_hbm, shift_ref),
    )
    for index, (name, source, target) in enumerate(loads):
        copy = pltpu.make_async_copy(source, target, load_sem.at[index])
        copy.start()
        pending[name] = copy.wait

    len_send[...] = jnp.full((8, 128), length.astype(F32), F32)
    settle("k", "v", "q")
    for pair in range(heads // 2):
        columns = slice(128 * pair, 128 * pair + 128)
        kp = k_ref[:, columns].astype(F32)
        vp = v_ref[:, columns].astype(F32)
        low = low_lanes(kp.shape)
        kv_send[2 * pair] = jnp.where(low, kp, roll64(vp)).astype(BF16)
        kv_send[2 * pair + 1] = jnp.where(low, roll64(kp), vp).astype(BF16)
        even, odd = pack_pair(q_ref[:, columns].astype(F32))
        q_send[2 * pair] = even.astype(BF16)
        q_send[2 * pair + 1] = odd.astype(BF16)

    pl.semaphore_wait(barrier, seq - 1 + depth - 1)

    def kv_slot(d):
        return kvbuf.at[pl.ds(pl.multiple_of(core * half_keys + d * ROWS, ROWS), ROWS)]

    def send_keys(first, last, index):
        @pl.loop(first, last)
        def _(d):
            peer = (chip + d) % chips
            remote(kv_send.at[peer % heads], kv_slot(d), send.at[index], recv.at[index], (z, peer * 2 + core)).start()

    def quarter(half, index):
        return kvbuf.at[
            pl.ds(pl.multiple_of(half * half_keys + index * forward_block, forward_block), forward_block)
        ]

    some = chips // 2
    pltpu.make_async_copy(kv_send.at[chip % heads], kv_slot(0), recv.at[0]).start()
    send_keys(1, some, 0)
    later("keys 0 in", quarter(core, 0), recv.at[0])
    later("keys 0 out", kvbuf.at[pl.ds(0, (some - 1) * ROWS)], send.at[0])

    def head_device(head):
        return ((my_group // 2) * heads + head) * 2 + my_group % 2

    def to_heads(source, target, index, self_index):
        head = chip % heads
        slot = me % heads
        mine = head_device(head) == me

        @pl.when(mine)
        def _():
            pltpu.make_async_copy(source.at[head], target.at[slot], recv.at[index]).start()

        @pl.when(jnp.logical_not(mine))
        def _():
            remote(
                source.at[head], target.at[slot], send.at[self_index], recv.at[index], (z, head_device(head))
            ).start()

        @pl.loop(1, heads)
        def _(d):
            to = (chip + d) % heads
            remote(
                source.at[to], target.at[slot], send.at[index], recv.at[index], (z, head_device(to))
            ).start()

        def own_done():
            @pl.when(jnp.logical_not(mine))
            def _():
                drain(target.at[0], send.at[self_index])

        later(f"heads {index} in", target, recv.at[index])
        later(f"heads {index} out", target.at[pl.ds(0, heads - 1)], send.at[index])
        pending[f"heads {index} own"] = own_done

    to_heads(q_send, qpk, 1, 2)

    send_keys(some, chips, 22)
    later("keys 1 in", quarter(core, 1), recv.at[22])
    later("keys 1 out", kvbuf.at[pl.ds(0, some * ROWS)], send.at[22])

    len_recv[z] = len_send[...]

    @pl.loop(1, depth)
    def _(d):
        remote(len_send, len_recv.at[z], send.at[23], recv.at[23], ((z + d) % depth, me)).start()

    later("lengths in", len_recv.at[pl.ds(0, depth - 1)], recv.at[23])
    later("lengths out", len_recv.at[pl.ds(0, depth - 1)], send.at[23])

    after = (z, (me + 1) % seq)
    before = (z, (me + seq - 1) % seq)
    settle("x", "cot")
    halo_copies = (
        remote(x_ext.at[pl.ds(ROWS, HALO)], x_ext.at[pl.ds(0, HALO)], send.at[3], recv.at[3], after),
        remote(x_ext.at[pl.ds(HALO, HALO)], x_ext.at[pl.ds(HALO + ROWS, HALO)], send.at[4], recv.at[4], before),
        remote(cot_ext.at[pl.ds(ROWS, 16)], cot_ext.at[pl.ds(0, 16)], send.at[5], recv.at[5], after),
        remote(cot_ext.at[pl.ds(16, 16)], cot_ext.at[pl.ds(16 + ROWS, 16)], send.at[6], recv.at[6], before),
    )
    for index, copy in enumerate(halo_copies):
        copy.start()
        pending[f"halo {index} in"] = copy.wait_recv
        pending[f"halo {index} out"] = copy.wait_send

    def prepare_keys(half, index):
        rows_at_once = min(forward_block, 512)

        @pl.loop(0, forward_block // rows_at_once)
        def _(part):
            first = index * forward_block + part * rows_at_once
            rows = pl.ds(pl.multiple_of(half * half_keys + first, rows_at_once), rows_at_once)
            kv = kvbuf[rows].astype(F32)
            lane = lax.broadcasted_iota(jnp.int32, kv.shape, 1)
            row = lax.broadcasted_iota(jnp.int32, kv.shape, 0) + first
            source = chip - (row >> 7)
            source = jnp.where(source < 0, source + chips, source)
            frame = (source * 2 + half) * ROWS + (row & 127)
            bias = jnp.where(jnp.logical_and(lane == 64, frame >= length), NEGATIVE, 0.0)
            keyed = jnp.where(lane < 64, kv, bias)
            valued = jnp.where(lane < 64, 1.0, kv)
            k1[rows] = keyed.astype(BF16)
            v1[rows] = valued.astype(BF16)
            kt[:, rows] = jnp.transpose(kv)[:64].astype(BF16) * BF16(0.125)
            v1t[:, rows] = jnp.transpose(valued).astype(BF16)

    factor = 0.125 * 1.4426950408889634

    def block_rows(block):
        return pl.ds(pl.multiple_of(block * forward_block, forward_block), forward_block)

    def scores_step(part, block, highest):
        scores = dot(
            k1[block_rows(block)], qaug[part * query_block : (part + 1) * query_block], ((1,), (1,))
        )
        sbuf[part % 2, block_rows(block)] = scores
        return jnp.maximum(highest, jnp.max(scores.reshape(forward_block // 8, 8, query_block), axis=0))

    def weights_step(part, block, highest, total):
        rows = block_rows(block)
        weights = jnp.exp2((sbuf[part % 2, rows] - highest) * factor).astype(BF16)
        pt[rows, part * query_block : (part + 1) * query_block] = weights
        return total + dot(v1t[:, rows], weights)

    def context_finish(part, total):
        turned = jnp.transpose(total)
        low = low_lanes(turned.shape)
        inverse = 1.0 / jnp.where(low, 1.0, roll64(turned))
        context = jnp.where(low, 0.0, turned * inverse).astype(BF16).astype(F32)
        rows = slice(part * query_block, (part + 1) * query_block)
        linv[rows] = inverse
        ctxh[rows] = context
        half_rows = slice(part * query_block // 2, (part + 1) * query_block // 2)
        ctx_send[half_rows] = pack_high(context).astype(BF16)

    high = jnp.full((8, query_block), NEGATIVE, F32)
    for index in range(2):
        settle(f"keys {index} in")
        forward = remote(
            quarter(core, index), quarter(core, index), send.at[7 + 17 * index], recv.at[7 + 17 * index], partner
        )
        forward.start()
        later(f"forward {index} in", quarter(other, index), recv.at[7 + 17 * index])
        pending[f"forward {index} out"] = forward.wait_send
        prepare_keys(core, index)
        if index == 0:
            settle("heads 1 in")
            for slot in range(heads):
                rows = slice(ROWS * slot, ROWS * slot + ROWS)
                part = unpack_low(qpk[slot].astype(F32))
                lane = lax.broadcasted_iota(jnp.int32, part.shape, 1)
                qcl[rows] = (part * 0.125).astype(BF16)
                qaug[rows] = jnp.where(lane == 64, 1.0, part).astype(BF16)
        high = scores_step(0, core * 2 + index, high)
    for index in range(2):
        settle(f"forward {index} in")
        prepare_keys(other, index)
        high = scores_step(0, other * 2 + index, high)

    start_high = jnp.full((8, query_block), NEGATIVE, F32)
    start_total = jnp.zeros((128, query_block), F32)
    for part in range(query_blocks):
        highest = jnp.max(high, axis=0, keepdims=True)
        if part + 1 < query_blocks:

            def both(b, carried, part=part, highest=highest):
                h, t = carried
                return scores_step(part + 1, b, h), weights_step(part, b, highest, t)

            high, total = lax.fori_loop(0, 4, both, (start_high, start_total))
        else:
            total = lax.fori_loop(
                0, 4, lambda b, t, part=part, highest=highest: weights_step(part, b, highest, t), start_total
            )
        context_finish(part, total)

    my_head = chip % heads
    moves = [(-1, 0, 16, 80), (0, 0, 80, 16)]
    moves += [(i, 64 * i - 16, 96, 0) for i in range(1, heads - 1)]
    moves += [(heads - 1, 64 * (heads - 1) - 16, 80, 0), (heads, 64 * heads - 16, 16, 0)]

    def owner_of(i):
        return (group * heads + i + seq) % seq

    for index, (i, start, count, to) in enumerate(moves):
        source = ctx_send.at[pl.ds(start, count)]
        target = ctx_recv.at[my_head, pl.ds(to, count)]

        @pl.when(owner_of(i) == me)
        def _(source=source, target=target):
            pltpu.make_async_copy(source, target, recv.at[8]).start()

        @pl.when(owner_of(i) != me)
        def _(source=source, target=target, i=i, index=index):
            remote(source, target, ctx_sem.at[index], recv.at[8], (z, owner_of(i))).start()

        def sent(source=source, i=i, index=index):
            @pl.when(owner_of(i) != me)
            def _():
                drain(source, ctx_sem.at[index])

        pending[f"context {index}"] = sent

    def live(rows, first):
        frame = me * ROWS + first + lax.broadcasted_iota(jnp.int32, (rows, 128), 0)
        return jnp.logical_and(frame >= 0, frame < length)

    def column(chunk):
        return pl.ds(pl.multiple_of(chunk * 128, 128), 128)

    def turned_convolution(rows, columns):
        total = jnp.zeros((ROWS, 128), F32)
        for low in range(8):
            moved = shifted(rows, low)
            for high_part in range(4):
                tap = 31 - (8 * high_part + low)
                if 0 <= tap < KERNEL:
                    total = total + taps_ref[tap : tap + 1, columns] * moved[8 * high_part : 8 * high_part + ROWS]
        return total

    settle("w", "taps", "gain", "shift")

    @pl.loop(0, chunks)
    def _(chunk):
        columns = column(chunk)
        cmask_ref[:, columns] = turned_convolution(jnp.where(live(mid, -16), 1.0, 0.0), columns)

    settle("lengths in")
    lengths = len_recv[:, :1]
    count_a[...] = jnp.clip(lengths - (me * ROWS).astype(F32), 0.0, float(ROWS))
    for i in range(seq):
        count_b[i] = jnp.sum(jnp.clip(lengths - float(i * ROWS), 0.0, float(ROWS)), axis=0)
    for target in (tmask_ref, tgrad_ref, tnorm_ref):
        target[KERNEL:] = jnp.zeros((1, channels), F32)

    settle(*(f"halo {index} in" for index in range(4)))
    drain(ctx_recv, recv.at[8])

    for pair in range(heads // 2):
        ctx_ref[:, 128 * pair : 128 * pair + 128] = unpack_pair(
            ctx_recv[2 * pair].astype(F32), ctx_recv[2 * pair + 1].astype(F32)
        ).astype(BF16)

    counted = jnp.clip(length - me * ROWS, 0, ROWS).astype(F32)

    @pl.loop(0, channels // 256)
    def _(chunk):
        columns = pl.ds(pl.multiple_of(chunk * 256, 256), 256)
        hidden = x_ext[:, columns].astype(F32) + dot(ctx_ref[...], w_ref[:, columns])
        mask = live(ext, -HALO)
        mask = jnp.concatenate([mask, mask], axis=1)
        hid_ref[:, columns] = jnp.where(mask, hidden, 0.0).astype(BF16).astype(F32)

    @pl.loop(0, chunks)
    def _(chunk):
        columns = column(chunk)
        hidden = hid_ref[:, columns]
        total = jnp.zeros((mid, 128), F32)
        for low in range(8):
            moved = shifted(hidden, low)
            for high_part in range(4):
                tap = 8 * high_part + low - 1
                if 0 <= tap < KERNEL:
                    total = total + taps_ref[tap : tap + 1, columns] * moved[8 * high_part : 8 * high_part + mid]
        conv_ref[:, columns] = total
        own = total[16 : 16 + ROWS]
        mask = live(ROWS, 0)
        summed = jnp.sum(jnp.where(mask, own, 0.0), axis=0, keepdims=True)
        mean = summed / jnp.maximum(counted, 1.0)
        spread = own - mean
        squares = jnp.sum(jnp.where(mask, spread * spread, 0.0), axis=0, keepdims=True)
        stat_a[pl.ds(chunk, 1)] = summed
        stat_a[pl.ds(chunks + chunk, 1)] = squares


    def write(source, target, index):
        copy = pltpu.make_async_copy(source, target, write_sem.at[index])
        copy.start()
        pending[f"write {index}"] = copy.wait

    def gather(source, target, index, slot, count, peer, beside):
        target[slot] = source[...]

        around(
            count,
            lambda d: remote(source, target.at[slot], send.at[index], recv.at[index], peer(d)).start(),
        )

        later(f"sums {index}", target.at[pl.ds(0, count - 1)], send.at[index])
        if beside is not None:
            beside()
        drain(target.at[pl.ds(0, count - 1)], recv.at[index])

    def gather_first(source, target, index, beside=None):
        gather(source, target, index, z, depth, lambda d: ((z + d) % depth, me), beside)

    def gather_second(source, target, index, beside=None):
        gather(source, target, index, me, seq, lambda d: (z, (me + d) % seq), beside)

    def correlate(target, rows, columns):
        hidden = hid_ref[16:, columns]
        for low in range(8):
            moved = shifted(hidden, low)
            for high_part in range(4):
                tap = 8 * high_part + low - 1
                if 0 <= tap < KERNEL:
                    terms = rows * moved[8 * high_part : 8 * high_part + ROWS]
                    target[tap : tap + 1, columns] = jnp.sum(terms, axis=0, keepdims=True)

    def correlate_mask():
        own_ctx[...] = jnp.transpose(ctx_ref[HALO : HALO + ROWS].astype(F32)).astype(BF16)

        @pl.loop(0, chunks)
        def _(chunk):
            correlate(tmask_ref, jnp.where(live(ROWS, 0), 1.0, 0.0), column(chunk))

    def correlate_rest():
        @pl.loop(0, chunks)
        def _(chunk):
            columns = column(chunk)
            own = slice(16, 16 + ROWS)
            correlate(tgrad_ref, ga_ref[own, columns], columns)
            correlate(tnorm_ref, jnp.where(live(ROWS, 0), conv_ref[own, columns], 0.0), columns)

    def merged(gathered, counts):
        sums = gathered[:, :chunks]
        squares = gathered[:, chunks:]
        count = jnp.sum(counts, axis=0)
        total = jnp.sum(sums, axis=0)
        mean = total / jnp.maximum(count, 1.0)
        shift = sums / jnp.maximum(counts, 1.0) - mean[None]
        return total, jnp.sum(squares, axis=0) + jnp.sum(counts * shift * shift, axis=0), count, mean

    gather_first(stat_a, recv_a, 9, correlate_mask)
    total, squares, count, mean = merged(recv_a[...], count_a[...])
    stat_b[:chunks] = total
    stat_b[chunks:] = squares
    gather_second(stat_b, recv_b, 10)
    total, squares, count, mean = merged(recv_b[...], count_b[...])
    tot_ref[:chunks] = mean
    tot_ref[chunks : 2 * chunks] = lax.rsqrt(squares / count + EPSILON)
    tot_ref[2 * chunks : 3 * chunks] = jnp.broadcast_to(1.0 / count, (chunks, 128))

    @pl.loop(0, chunks)
    def _(chunk):
        columns = column(chunk)
        mean = tot_ref[pl.ds(chunk, 1)]
        inverse = tot_ref[pl.ds(chunks + chunk, 1)]
        normed = (conv_ref[:, columns] - mean) * inverse
        conv_ref[:, columns] = normed
        act = normed * gain_ref[:, columns] + shift_ref[:, columns]
        gate = 1.0 / (1.0 + jnp.exp(-act))
        grad_out = jnp.where(live(mid, -16), cot_ext[:, columns].astype(F32), 0.0)
        grad_act = grad_out * gate * (1.0 + act * (1.0 - gate))
        ga_ref[:, columns] = grad_act
        own = grad_act[16 : 16 + ROWS]
        stat_c[pl.ds(chunk, 1)] = jnp.sum(own * normed[16 : 16 + ROWS], axis=0, keepdims=True)
        stat_c[pl.ds(chunks + chunk, 1)] = jnp.sum(own, axis=0, keepdims=True)
        gated = (act * gate)[16 : 16 + ROWS]
        hidden = hid_ref[HALO : HALO + ROWS, columns]
        out_ref[:, columns] = jnp.where(live(ROWS, 0), hidden + gated, 0.0).astype(BF16)

    def beside():
        write(out_ref, out_hbm, 0)

        @pl.loop(0, chunks)
        def _(chunk):
            columns = column(chunk)
            cgrad_ref[:, columns] = turned_convolution(ga_ref[:, columns], columns)
            cnorm_ref[:, columns] = turned_convolution(
                jnp.where(live(mid, -16), conv_ref[:, columns], 0.0), columns
            )

    gather_first(stat_c, recv_c, 11, beside)
    stat_d[...] = jnp.sum(recv_c[...], axis=0)
    gather_second(stat_d, recv_d, 12, correlate_rest)
    sums_ref[...] = jnp.sum(recv_d[...], axis=0)

    @pl.loop(0, chunks)
    def _(chunk):
        columns = column(chunk)
        inverse = tot_ref[pl.ds(chunks + chunk, 1)]
        per_count = tot_ref[pl.ds(2 * chunks + chunk, 1)]
        gain_sum = sums_ref[pl.ds(chunk, 1)] * per_count
        shift_sum = sums_ref[pl.ds(chunks + chunk, 1)] * per_count
        scale = inverse * gain_ref[:, columns]
        turned = cgrad_ref[:, columns] - shift_sum * cmask_ref[:, columns] - gain_sum * cnorm_ref[:, columns]
        total = cot_ext[16 : 16 + ROWS, columns].astype(F32) + scale * turned
        ginp_ref[:, columns] = jnp.where(live(ROWS, 0), total, 0.0).astype(BF16)

    write(ginp_ref, ginp_hbm, 1)

    def stage0(piece):
        copy = remote(
            wsend.at[piece].at[other], g0.at[piece], piece_send.at[5 * piece + 0], piece_recv.at[5 * piece + 0], partner
        )
        copy.start()
        pending[f"stage 0 in {piece}"] = copy.wait_recv
        pending[f"stage 0 out {piece}"] = copy.wait_send

    for piece in range(PIECES):
        first = piece * piece_width
        size = min(piece_width, channels - first)
        if size > 0:
            terms = dot(own_ctx[...], ginp_ref[:, first : first + size]).astype(BF16)
            wsend.at[piece][:, :, :, :size] = terms.reshape(2, chips, 16, size)
        if piece < PIECES - 1:
            stage0(piece)

    tap_lanes = slice(piece_width - 128, piece_width)
    wsend[PIECES - 1, :, :, :, tap_lanes] = jnp.zeros((2, chips, 16, 128), BF16)

    @pl.loop(0, chunks)
    def _(chunk):
        columns = column(chunk)
        per_count = tot_ref[pl.ds(2 * chunks + chunk, 1)]
        gain_sum = sums_ref[pl.ds(chunk, 1)] * per_count
        shift_sum = sums_ref[pl.ds(chunks + chunk, 1)] * per_count
        scale = tot_ref[pl.ds(chunks + chunk, 1)] * gain_ref[:, columns]
        stacked = tgrad_ref[:, columns] - shift_sum * tmask_ref[:, columns] - gain_sum * tnorm_ref[:, columns]
        stacked = (scale * stacked).astype(BF16)
        wsend.at[PIECES - 1].at[0][pl.ds(chunk, 1), :, tap_lanes] = stacked[:16].reshape(1, 16, 128)
        wsend.at[PIECES - 1].at[1][pl.ds(chunk, 1), :, tap_lanes] = stacked[16:].reshape(1, 16, 128)

    stage0(PIECES - 1)

    @pl.loop(0, heads // 2)
    def _(pair):
        rows = pl.ds(pl.multiple_of(pair * 128, 128), 128)
        grad_context = dot(ginp_ref[...], w_ref[rows], ((1,), (1,))).astype(BF16).astype(F32)
        even, odd = pack_pair(grad_context)
        do_send[2 * pair] = even.astype(BF16)
        do_send[2 * pair + 1] = odd.astype(BF16)

    to_heads(do_send, do_recv, 13, 14)

    def stage1(piece):
        settle(f"stage 0 in {piece}")

        total = wsend.at[piece].at[core][...].astype(F32) + g0[piece].astype(F32)
        gs1[piece] = total.astype(BF16)
        g1.at[piece].at[chip][...] = gs1.at[piece].at[chip][...]

        @pl.loop(1, chips)
        def _(d):
            peer = (chip + d) % chips
            remote(
                gs1.at[piece].at[peer],
                g1.at[piece].at[chip],
                piece_send.at[5 * piece + 1],
                piece_recv.at[5 * piece + 1],
                (z, peer * 2 + core),
            ).start()

        later(f"stage 1 in {piece}", g1.at[piece].at[pl.ds(0, chips - 1)], piece_recv.at[5 * piece + 1])
        later(f"stage 1 out {piece}", g1.at[piece].at[pl.ds(0, chips - 1)], piece_send.at[5 * piece + 1])

    def stage2(piece):
        settle(f"stage 1 in {piece}")
        total = g1.at[piece][0].astype(F32)
        for i in range(1, chips):
            total = total + g1.at[piece][i].astype(F32)
        total = total.astype(BF16)
        gs2[piece] = total
        g2.at[piece].at[z][...] = total

        @pl.loop(1, depth)
        def _(d):
            remote(
                gs2.at[piece],
                g2.at[piece].at[z],
                piece_send.at[5 * piece + 2],
                piece_recv.at[5 * piece + 2],
                ((z + d) % depth, me),
            ).start()

        pending[f"stage 2 in {piece}"] = lambda: drain(
            g2.at[piece].at[pl.ds(0, depth - 1)], piece_recv.at[5 * piece + 2]
        )
        pending[f"stage 2 out {piece}"] = lambda: drain(
            g2.at[piece].at[pl.ds(0, depth - 1)], piece_send.at[5 * piece + 2]
        )

    def stage3(piece):
        settle(f"stage 2 in {piece}")
        total = g2.at[piece][0].astype(F32)
        for i in range(1, depth):
            total = total + g2.at[piece][i].astype(F32)
        gfin_ref.at[piece].at[core, chip][...] = total.astype(BF16)
        final = gfin_ref.at[piece].at[core, chip]

        @pl.loop(1, chips)
        def _(d):
            peer = (chip + d) % chips
            remote(
                final, final, piece_send.at[5 * piece + 3], piece_recv.at[5 * piece + 3], (z, peer * 2 + core)
            ).start()

        size = gfin_ref.at[piece].at[core, pl.ds(0, chips - 1)]
        later(f"stage 3 in {piece}", size, piece_recv.at[5 * piece + 3])
        later(f"stage 3 out {piece}", size, piece_send.at[5 * piece + 3])

    def stage4(piece):
        settle(f"stage 3 in {piece}")
        finals = gfin_ref.at[piece].at[core]
        copy = remote(finals, finals, piece_send.at[5 * piece + 4], piece_recv.at[5 * piece + 4], partner)
        copy.start()
        later(f"stage 4 in {piece}", gfin_ref.at[piece].at[other], piece_recv.at[5 * piece + 4])
        pending[f"stage 4 out {piece}"] = copy.wait_send

    for piece in range(PIECES):
        stage1(piece)

    settle("heads 13 in")
    for index in range(heads):
        rows = slice(ROWS * index, ROWS * index + ROWS)
        scaled = (unpack_high(do_recv[index].astype(F32)) * linv[rows]).astype(BF16)
        docl[rows] = scaled
        scaled = scaled.astype(F32)
        delta = jnp.sum(ctxh[rows] * scaled, axis=1, keepdims=True)
        first = delta.astype(BF16).astype(F32)
        rest = delta - first
        lane = lax.broadcasted_iota(jnp.int32, scaled.shape, 1)
        doaug[rows] = jnp.where(lane == 0, -first, jnp.where(lane == 1, -rest, scaled)).astype(BF16)

    dqt[...] = jnp.zeros_like(dqt)

    def part_copy(turn):
        rows = pl.ds(pl.multiple_of(turn * backward_block, backward_block), backward_block)
        return remote(dsend.at[rows], precv.at[rows], part_send.at[turn], part_recv.at[turn], partner)

    turns = 4
    slots = backward_block // ROWS

    @pl.loop(0, 2 * turns)
    def _(step):
        half = jnp.where(step < turns, other, core)
        turn = step % turns
        rows = pl.ds(
            pl.multiple_of(half * half_keys + turn * backward_block, backward_block), backward_block
        )
        turn_rows = pl.ds(pl.multiple_of(turn * backward_block, backward_block), backward_block)
        weights = pt[rows]
        grads = dot(v1[rows], doaug[...], ((1,), (1,))).astype(BF16)
        scores = weights * grads
        dqt[...] += dot(kt[:, rows], scores)
        rbuf[...] = dot(scores, qcl[...]) + dot(weights, docl[...])

        @pl.when(step < turns)
        def _():
            dsend[turn_rows] = rbuf[...].astype(BF16)
            part_copy(turn).start()

        @pl.when(step >= turns)
        def _():
            part_copy(turn).wait_recv()
            osend[turn_rows] = (rbuf[...] + precv[turn_rows].astype(F32)).astype(BF16)
            for i in range(slots):
                slot = turn * slots + i
                owner = (chip + chips - slot) % chips
                source = osend.at[pl.ds(pl.multiple_of(slot * ROWS, ROWS), ROWS)]

                def give(source=source, owner=owner):
                    remote(source, kvrecv.at[chip], own_sem, recv.at[20], (z, owner * 2 + core)).start()

                if i == 0:

                    @pl.when(turn == 0)
                    def _(source=source):
                        pltpu.make_async_copy(source, kvrecv.at[chip], recv.at[20]).start()

                    pl.when(turn > 0)(give)
                else:
                    give()

        for piece in range(PIECES):

            @pl.when(step == 2 + piece)
            def _(piece=piece):
                stage2(piece)

    def parts_sent():
        @pl.loop(0, turns)
        def _(turn):
            part_copy(turn).wait_send()

    pending["parts"] = parts_sent
    later("owned in", kvrecv, recv.at[20])
    later("owned out", kvrecv.at[pl.ds(0, chips - 1)], own_sem)

    @pl.loop(0, query_blocks)
    def _(block):
        part = pl.ds(pl.multiple_of(block * query_block, query_block), query_block)
        turned = dqt[:, part]
        turned = jnp.transpose(jnp.concatenate([turned, jnp.zeros_like(turned)], axis=0))
        half_part = pl.ds(pl.multiple_of(block * query_block // 2, query_block // 2), query_block // 2)
        dq_send[half_part] = pack_low(turned).astype(BF16)

    for i in range(heads):
        source = dq_send.at[pl.ds(64 * i, 64)]
        target = dq_recv.at[my_head]

        @pl.when(owner_of(i) == me)
        def _(source=source, target=target):
            pltpu.make_async_copy(source, target, recv.at[21]).start()

        @pl.when(owner_of(i) != me)
        def _(source=source, target=target, i=i):
            remote(source, target, dq_sem.at[i], recv.at[21], (z, owner_of(i))).start()

        def sent(source=source, i=i):
            @pl.when(owner_of(i) != me)
            def _():
                drain(source, dq_sem.at[i])

        pending[f"grad query {i}"] = sent

    for piece in range(PIECES):
        stage3(piece)

    settle("owned in")
    for pair in range(heads // 2):
        columns = slice(128 * pair, 128 * pair + 128)
        even = kvrecv[2 * pair].astype(F32) + kvrecv[2 * pair + heads].astype(F32)
        odd = kvrecv[2 * pair + 1].astype(F32) + kvrecv[2 * pair + 1 + heads].astype(F32)
        low = low_lanes(even.shape)
        gk_ref[:, columns] = jnp.where(low, even, roll64(odd)).astype(BF16)
        gv_ref[:, columns] = jnp.where(low, roll64(even), odd).astype(BF16)
    write(gk_ref, gk_hbm, 3)
    write(gv_ref, gv_hbm, 4)

    drain(dq_recv, recv.at[21])
    for pair in range(heads // 2):
        gq_ref[:, 128 * pair : 128 * pair + 128] = unpack_pair(
            dq_recv[2 * pair].astype(F32), dq_recv[2 * pair + 1].astype(F32)
        ).astype(BF16)

    write(gq_ref, gq_hbm, 2)
    for piece in range(PIECES):
        stage4(piece)
    settle()


def finish(width, chunks, *refs):
    sources = refs[:7]
    outs = refs[7:16]
    out, ginp, gq, gk, gv, packed, sums = refs[16:23]
    weights, taps, load_sem, sem = refs[23:]
    channels = weights.shape[1]
    loads = [
        pltpu.make_async_copy(source, target, load_sem.at[index])
        for index, (source, target) in enumerate(zip(sources, refs[16:23]))
    ]
    for index in (5, 6, 0, 1, 2, 3, 4):
        loads[index].start()
    copies = [
        pltpu.make_async_copy(source, target, sem.at[index])
        for index, (source, target) in enumerate(
            (
                (out, outs[0]),
                (ginp, outs[1]),
                (gq, outs[2]),
                (gk, outs[3]),
                (gv, outs[4]),
                (weights, outs[5]),
                (taps, outs[6]),
                (sums.at[pl.ds(0, chunks)], outs[7]),
                (sums.at[pl.ds(chunks, chunks)], outs[8]),
            )
        )
    ]
    loads[5].wait()
    piece_width = packed.shape[-1]
    for piece in range(PIECES):
        first = piece * piece_width
        size = min(piece_width, channels - first)
        for half in range(2 if size > 0 else 0):
            rows = slice(half * width // 2, (half + 1) * width // 2)
            terms = packed[piece, half, :, :, :size].astype(F32)
            weights[rows, first : first + size] = terms.reshape(width // 2, size)
    for chunk in range(chunks):
        lanes = slice(piece_width - 128, piece_width)
        columns = slice(128 * chunk, 128 * chunk + 128)
        taps[:16, columns] = packed[PIECES - 1, 0, chunk, :, lanes].astype(F32)
        taps[16:, columns] = packed[PIECES - 1, 1, chunk, :15, lanes].astype(F32)
    copies[5].start()
    copies[6].start()
    loads[6].wait()
    copies[7].start()
    copies[8].start()
    for index in range(5):
        loads[index].wait()
        copies[index].start()
    for copy in copies:
        copy.wait()


def shards(
    depth,
    query_rows,
    key_rows,
    value_rows,
    inputs,
    lengths,
    out_weight,
    taps,
    norm_gain,
    norm_shift,
    cotangent,
):
    seq = lax.axis_size("seq")
    heads = seq // 4
    chips = seq // 2
    width = query_rows.shape[2]
    channels = inputs.shape[2]
    chunks = channels // 128
    queries = ROWS * heads
    keys = seq * ROWS
    ext = ROWS + 2 * HALO
    mid = ROWS + 32
    padded = channels + 128
    piece_width = padded // PIECES
    query_block = min(queries, 512)
    vmem = pltpu.VMEM
    scratch = [
        vmem((ROWS, width), BF16),
        vmem((ROWS, width), BF16),
        vmem((ROWS, width), BF16),
        vmem((1, channels), F32),
        vmem((1, channels), F32),
        vmem((ROWS, channels), BF16),
        vmem((ROWS, channels), BF16),
        vmem((ROWS, width), BF16),
        vmem((ROWS, width), BF16),
        vmem((ROWS, width), BF16),
        vmem((8, 128), F32),
        vmem((depth, 8, 128), F32),
        vmem((ROWS, channels), F32),
        vmem((ROWS, channels), F32),
        vmem((ROWS, channels), F32),
        vmem((width, ROWS), BF16),
        vmem((KERNEL + 1, channels), F32),
        vmem((KERNEL + 1, channels), F32),
        vmem((KERNEL + 1, channels), F32),
        vmem((depth, 1, 128), F32),
        vmem((seq, 1, 128), F32),
        vmem((heads, ROWS, 128), BF16),
        vmem((heads, 64, 128), BF16),
        vmem((keys, 128), BF16),
        vmem((heads, 64, 128), BF16),
        vmem((keys, 128), BF16),
        vmem((keys, 128), BF16),
        vmem((64, keys), BF16),
        vmem((128, keys), BF16),
        vmem((queries, 128), BF16),
        vmem((queries, 128), BF16),
        vmem((2, keys, query_block), F32),
        vmem((keys, queries), BF16),
        vmem((queries, 128), F32),
        vmem((queries, 128), F32),
        vmem((queries // 2, 128), BF16),
        vmem((heads, ext // 2, 128), BF16),
        vmem((ext, channels), BF16),
        vmem((mid, channels), BF16),
        vmem((width, channels), BF16),
        vmem((KERNEL, channels), F32),
        vmem((ext, width), BF16),
        vmem((ext, channels), F32),
        vmem((mid, channels), F32),
        vmem((mid, channels), F32),
        vmem((2 * chunks, 128), F32),
        vmem((2 * chunks, 128), F32),
        vmem((depth, 2 * chunks, 128), F32),
        vmem((seq, 2 * chunks, 128), F32),
        vmem((2 * chunks, 128), F32),
        vmem((depth, 2 * chunks, 128), F32),
        vmem((2 * chunks, 128), F32),
        vmem((seq, 2 * chunks, 128), F32),
        vmem((3 * chunks, 128), F32),
        vmem((heads, 64, 128), BF16),
        vmem((heads, 64, 128), BF16),
        vmem((queries, 128), BF16),
        vmem((queries, 128), BF16),
        vmem((keys // 8, 128), F32),
        vmem((64, queries), F32),
        vmem((keys // 2, 128), BF16),
        vmem((keys // 2, 128), BF16),
        vmem((keys // 2, 128), BF16),
        vmem((chips, ROWS, 128), BF16),
        vmem((queries // 2, 128), BF16),
        vmem((heads, 64, 128), BF16),
        vmem((PIECES, 2, chips, 16, piece_width), BF16),
        vmem((PIECES, chips, 16, piece_width), BF16),
        vmem((PIECES, chips, 16, piece_width), BF16),
        vmem((PIECES, chips, 16, piece_width), BF16),
        vmem((PIECES, 16, piece_width), BF16),
        vmem((PIECES, depth, 16, piece_width), BF16),
        pltpu.SemaphoreType.DMA((9,)),
        pltpu.SemaphoreType.DMA((25,)),
        pltpu.SemaphoreType.DMA((25,)),
        pltpu.SemaphoreType.DMA((heads + 2,)),
        pltpu.SemaphoreType.DMA((heads,)),
        pltpu.SemaphoreType.DMA((4,)),
        pltpu.SemaphoreType.DMA((4,)),
        pltpu.SemaphoreType.DMA,
        pltpu.SemaphoreType.DMA((5 * PIECES,)),
        pltpu.SemaphoreType.DMA((5 * PIECES,)),
        pltpu.SemaphoreType.DMA((5,)),
    ]
    in_vmem = pl.BlockSpec(memory_space=pltpu.VMEM)
    anywhere = pl.BlockSpec(memory_space=pl.ANY)
    plain = (
        jax.ShapeDtypeStruct((ROWS, channels), BF16),
        jax.ShapeDtypeStruct((ROWS, channels), BF16),
        jax.ShapeDtypeStruct((ROWS, width), BF16),
        jax.ShapeDtypeStruct((ROWS, width), BF16),
        jax.ShapeDtypeStruct((ROWS, width), BF16),
    )
    results = pl.pallas_call(
        functools.partial(kernel, heads, seq, depth),
        out_shape=plain
        + (
            jax.ShapeDtypeStruct((PIECES, 2, chips, 16, piece_width), BF16),
            jax.ShapeDtypeStruct((2 * chunks, 128), F32),
        ),
        in_specs=[pl.BlockSpec(memory_space=pltpu.SMEM)] + [anywhere] * 9,
        out_specs=(anywhere,) * 5 + (in_vmem,) * 2,
        scratch_shapes=scratch,
        compiler_params=pltpu.CompilerParams(
            collective_id=0, has_side_effects=True, vmem_limit_bytes=60 * 1024 * 1024
        ),
    )(
        lengths,
        query_rows[0],
        key_rows[0],
        value_rows[0],
        inputs[0],
        cotangent[0],
        out_weight,
        taps,
        norm_gain[None],
        norm_shift[None],
    )
    final = pl.pallas_call(
        functools.partial(finish, width, chunks),
        out_shape=plain
        + (
            jax.ShapeDtypeStruct((width, channels), F32),
            jax.ShapeDtypeStruct((KERNEL, channels), F32),
            jax.ShapeDtypeStruct((chunks, 128), F32),
            jax.ShapeDtypeStruct((chunks, 128), F32),
        ),
        in_specs=[anywhere] * 7,
        out_specs=(anywhere,) * 9,
        scratch_shapes=[vmem(array.shape, array.dtype) for array in results]
        + [
            vmem((width, channels), F32),
            vmem((KERNEL, channels), F32),
            pltpu.SemaphoreType.DMA((7,)),
            pltpu.SemaphoreType.DMA((9,)),
        ],
        compiler_params=pltpu.CompilerParams(vmem_limit_bytes=60 * 1024 * 1024),
    )(*results)
    return (
        *(array[None] for array in final[:5]),
        final[5],
        final[6],
        final[7].reshape(channels),
        final[8].reshape(channels),
    )


def solution(mesh):
    rows = P("dp", "seq", None)
    return jax.shard_map(
        functools.partial(shards, mesh.shape["dp"]),
        mesh=mesh,
        in_specs=(rows, rows, rows, rows, P("dp"), P(), P(), P(), P(), rows),
        out_specs=(rows, rows, rows, rows, rows, P(), P(), P(), P()),
        check_vma=False,
    )
```

```python
import functools

import jax
import jax.numpy as jnp
from jax import lax
from jax.experimental import pallas as pl
from jax.experimental.pallas import tpu as pltpu
from jax.sharding import PartitionSpec as P

KERNEL = 31
HALF = 15
HEAD_DIM = 64
ROWS = 128
HALO = 32
NEGATIVE = -1e30
EPSILON = 1e-05
PIECES = 3
MESH = pl.DeviceIdType.MESH
F32 = jnp.float32
BF16 = jnp.bfloat16


def roll64(x):
    return pltpu.roll(x, 64, 1)


def low_lanes(shape):
    return lax.broadcasted_iota(jnp.int32, shape, 1) < 64


def split_units(x):
    rows = x.shape[0]
    units = x.reshape(rows // 32, 2, 16, 128)
    return units[:, 0].reshape(rows // 2, 128), units[:, 1].reshape(rows // 2, 128)


def join_units(first, second):
    rows = first.shape[0]
    first = first.reshape(rows // 16, 1, 16, 128)
    second = second.reshape(rows // 16, 1, 16, 128)
    return jnp.concatenate([first, second], axis=1).reshape(2 * rows, 128)


def pack_pair(x):
    first, second = split_units(x)
    low = low_lanes(first.shape)
    even = jnp.where(low, first, roll64(second))
    odd = jnp.where(low, roll64(first), second)
    return even, odd


def unpack_pair(even, odd):
    low = low_lanes(even.shape)
    return join_units(jnp.where(low, even, roll64(odd)), jnp.where(low, roll64(even), odd))


def unpack_low(packed):
    low = low_lanes(packed.shape)
    return join_units(jnp.where(low, packed, 0.0), jnp.where(low, roll64(packed), 0.0))


def unpack_high(packed):
    low = low_lanes(packed.shape)
    return join_units(jnp.where(low, 0.0, roll64(packed)), jnp.where(low, 0.0, packed))


def pack_low(x):
    first, second = split_units(x)
    return jnp.where(low_lanes(first.shape), first, roll64(second))


def pack_high(x):
    first, second = split_units(x)
    return jnp.where(low_lanes(first.shape), roll64(first), second)


def dot(a, b, dims=((1,), (0,))):
    return lax.dot_general(a, b, (dims, ((), ())), preferred_element_type=F32)


def shifted(x, amount):
    return x if amount == 0 else pltpu.roll(x, x.shape[0] - amount, 0)


def kernel(
    heads,
    seq,
    depth,
    length_ref,
    q_hbm,
    k_hbm,
    v_hbm,
    x_hbm,
    cot_hbm,
    w_hbm,
    taps_hbm,
    gain_hbm,
    shift_hbm,
    out_hbm,
    ginp_hbm,
    gq_hbm,
    gk_hbm,
    gv_hbm,
    gfin_ref,
    sums_ref,
    q_ref,
    k_ref,
    v_ref,
    gain_ref,
    shift_ref,
    out_ref,
    ginp_ref,
    gq_ref,
    gk_ref,
    gv_ref,
    len_send,
    len_recv,
    cmask_ref,
    cgrad_ref,
    cnorm_ref,
    own_ctx,
    tmask_ref,
    tgrad_ref,
    tnorm_ref,
    count_a,
    count_b,
    kv_send,
    q_send,
    kvbuf,
    qpk,
    k1,
    v1,
    kt,
    v1t,
    qaug,
    qcl,
    sbuf,
    pt,
    ctxh,
    linv,
    ctx_send,
    ctx_recv,
    x_ext,
    cot_ext,
    w_ref,
    taps_ref,
    ctx_ref,
    hid_ref,
    conv_ref,
    ga_ref,
    stat_a,
    stat_b,
    recv_a,
    recv_b,
    stat_c,
    recv_c,
    stat_d,
    recv_d,
    tot_ref,
    do_send,
    do_recv,
    doaug,
    docl,
    rbuf,
    dqt,
    dsend,
    precv,
    osend,
    kvrecv,
    dq_send,
    dq_recv,
    wsend,
    g0,
    gs1,
    g1,
    gs2,
    g2,
    load_sem,
    send,
    recv,
    ctx_sem,
    dq_sem,
    part_send,
    part_recv,
    own_sem,
    piece_send,
    piece_recv,
    write_sem,
):
    chips = seq // 2
    width = q_ref.shape[1]
    channels = out_ref.shape[1]
    chunks = channels // 128
    queries = ROWS * heads
    half_keys = chips * ROWS
    forward_block = half_keys // 2
    backward_block = half_keys // 4
    query_block = min(queries, 512)
    query_blocks = queries // query_block
    padded = channels + 128
    piece_width = padded // PIECES
    ext = ROWS + 2 * HALO
    mid = ROWS + 32

    z = lax.axis_index("dp")
    me = lax.axis_index("seq")
    chip = me // 2
    core = me % 2
    other = 1 - core
    partner = (z, chip * 2 + other)
    group = (chip // heads) * 2 + core
    my_group = me // heads
    length = length_ref[0]

    def remote(src, dst, send_sem, recv_sem, device):
        return pltpu.make_async_remote_copy(
            src_ref=src, dst_ref=dst, send_sem=send_sem, recv_sem=recv_sem, device_id=device, device_id_type=MESH
        )

    def drain(ref, sem):
        pltpu.make_async_copy(ref, ref, sem).wait()

    pending = {}

    def later(name, ref, sem):
        pending[name] = lambda: drain(ref, sem)

    def settle(*names):
        for name in names or tuple(pending):
            pending.pop(name)()

    def around(count, act):
        act(count // 2)

        @pl.loop(1, count // 2)
        def _(k):
            act(count // 2 + k)
            act(count // 2 - k)

    barrier = pltpu.get_barrier_semaphore()

    def greet(device):
        pl.semaphore_signal(barrier, inc=1, device_id=device, device_id_type=MESH)

    around(depth, lambda d: greet(((z + d) % depth, me)))
    around(seq, lambda d: greet((z, (me + d) % seq)))


    loads = (
        ("k", k_hbm, k_ref),
        ("v", v_hbm, v_ref),
        ("q", q_hbm, q_ref),
        ("x", x_hbm, x_ext.at[pl.ds(HALO, ROWS)]),
        ("cot", cot_hbm, cot_ext.at[pl.ds(16, ROWS)]),
        ("w", w_hbm, w_ref),
        ("taps", taps_hbm, taps_ref),
        ("gain", gain_hbm, gain_ref),
        ("shift", shift_hbm, shift_ref),
    )
    for index, (name, source, target) in enumerate(loads):
        copy = pltpu.make_async_copy(source, target, load_sem.at[index])
        copy.start()
        pending[name] = copy.wait

    len_send[...] = jnp.full((8, 128), length.astype(F32), F32)
    settle("k", "v", "q")
    for pair in range(heads // 2):
        columns = slice(128 * pair, 128 * pair + 128)
        kp = k_ref[:, columns].astype(F32)
        vp = v_ref[:, columns].astype(F32)
        low = low_lanes(kp.shape)
        kv_send[2 * pair] = jnp.where(low, kp, roll64(vp)).astype(BF16)
        kv_send[2 * pair + 1] = jnp.where(low, roll64(kp), vp).astype(BF16)
        even, odd = pack_pair(q_ref[:, columns].astype(F32))
        q_send[2 * pair] = even.astype(BF16)
        q_send[2 * pair + 1] = odd.astype(BF16)

    pl.semaphore_wait(barrier, seq - 1 + depth - 1)

    def kv_slot(d):
        return kvbuf.at[pl.ds(pl.multiple_of(core * half_keys + d * ROWS, ROWS), ROWS)]

    def send_keys(first, last, index):
        @pl.loop(first, last)
        def _(d):
            peer = (chip + d) % chips
            remote(kv_send.at[peer % heads], kv_slot(d), send.at[index], recv.at[index], (z, peer * 2 + core)).start()

    def quarter(half, index):
        return kvbuf.at[
            pl.ds(pl.multiple_of(half * half_keys + index * forward_block, forward_block), forward_block)
        ]

    some = chips // 2
    pltpu.make_async_copy(kv_send.at[chip % heads], kv_slot(0), recv.at[0]).start()
    send_keys(1, some, 0)
    later("keys 0 in", quarter(core, 0), recv.at[0])
    later("keys 0 out", kvbuf.at[pl.ds(0, (some - 1) * ROWS)], send.at[0])

    def head_device(head):
        return ((my_group // 2) * heads + head) * 2 + my_group % 2

    def to_heads(source, target, index, self_index):
        head = chip % heads
        slot = me % heads
        mine = head_device(head) == me

        @pl.when(mine)
        def _():
            pltpu.make_async_copy(source.at[head], target.at[slot], recv.at[index]).start()

        @pl.when(jnp.logical_not(mine))
        def _():
            remote(
                source.at[head], target.at[slot], send.at[self_index], recv.at[index], (z, head_device(head))
            ).start()

        @pl.loop(1, heads)
        def _(d):
            to = (chip + d) % heads
            remote(
                source.at[to], target.at[slot], send.at[index], recv.at[index], (z, head_device(to))
            ).start()

        def own_done():
            @pl.when(jnp.logical_not(mine))
            def _():
                drain(target.at[0], send.at[self_index])

        later(f"heads {index} in", target, recv.at[index])
        later(f"heads {index} out", target.at[pl.ds(0, heads - 1)], send.at[index])
        pending[f"heads {index} own"] = own_done

    to_heads(q_send, qpk, 1, 2)

    send_keys(some, chips, 22)
    later("keys 1 in", quarter(core, 1), recv.at[22])
    later("keys 1 out", kvbuf.at[pl.ds(0, some * ROWS)], send.at[22])

    len_recv[z] = len_send[...]

    @pl.loop(1, depth)
    def _(d):
        remote(len_send, len_recv.at[z], send.at[23], recv.at[23], ((z + d) % depth, me)).start()

    later("lengths in", len_recv.at[pl.ds(0, depth - 1)], recv.at[23])
    later("lengths out", len_recv.at[pl.ds(0, depth - 1)], send.at[23])

    after = (z, (me + 1) % seq)
    before = (z, (me + seq - 1) % seq)
    settle("x", "cot")
    halo_copies = (
        remote(x_ext.at[pl.ds(ROWS, HALO)], x_ext.at[pl.ds(0, HALO)], send.at[3], recv.at[3], after),
        remote(x_ext.at[pl.ds(HALO, HALO)], x_ext.at[pl.ds(HALO + ROWS, HALO)], send.at[4], recv.at[4], before),
        remote(cot_ext.at[pl.ds(ROWS, 16)], cot_ext.at[pl.ds(0, 16)], send.at[5], recv.at[5], after),
        remote(cot_ext.at[pl.ds(16, 16)], cot_ext.at[pl.ds(16 + ROWS, 16)], send.at[6], recv.at[6], before),
    )
    for index, copy in enumerate(halo_copies):
        copy.start()
        pending[f"halo {index} in"] = copy.wait_recv
        pending[f"halo {index} out"] = copy.wait_send

    def prepare_keys(half, index):
        rows_at_once = min(forward_block, 512)

        @pl.loop(0, forward_block // rows_at_once)
        def _(part):
            first = index * forward_block + part * rows_at_once
            rows = pl.ds(pl.multiple_of(half * half_keys + first, rows_at_once), rows_at_once)
            kv = kvbuf[rows].astype(F32)
            lane = lax.broadcasted_iota(jnp.int32, kv.shape, 1)
            row = lax.broadcasted_iota(jnp.int32, kv.shape, 0) + first
            source = chip - (row >> 7)
            source = jnp.where(source < 0, source + chips, source)
            frame = (source * 2 + half) * ROWS + (row & 127)
            bias = jnp.where(jnp.logical_and(lane == 64, frame >= length), NEGATIVE, 0.0)
            keyed = jnp.where(lane < 64, kv, bias)
            valued = jnp.where(lane < 64, 1.0, kv)
            k1[rows] = keyed.astype(BF16)
            v1[rows] = valued.astype(BF16)
            kt[:, rows] = jnp.transpose(kv)[:64].astype(BF16) * BF16(0.125)
            v1t[:, rows] = jnp.transpose(valued).astype(BF16)

    factor = 0.125 * 1.4426950408889634

    def block_rows(block):
        return pl.ds(pl.multiple_of(block * forward_block, forward_block), forward_block)

    def scores_step(part, block, highest):
        scores = dot(
            k1[block_rows(block)], qaug[part * query_block : (part + 1) * query_block], ((1,), (1,))
        )
        sbuf[part % 2, block_rows(block)] = scores
        return jnp.maximum(highest, jnp.max(scores.reshape(forward_block // 8, 8, query_block), axis=0))

    def weights_step(part, block, highest, total):
        rows = block_rows(block)
        weights = jnp.exp2((sbuf[part % 2, rows] - highest) * factor).astype(BF16)
        pt[rows, part * query_block : (part + 1) * query_block] = weights
        return total + dot(v1t[:, rows], weights)

    def context_finish(part, total):
        turned = jnp.transpose(total)
        low = low_lanes(turned.shape)
        inverse = 1.0 / jnp.where(low, 1.0, roll64(turned))
        context = jnp.where(low, 0.0, turned * inverse).astype(BF16).astype(F32)
        rows = slice(part * query_block, (part + 1) * query_block)
        linv[rows] = inverse
        ctxh[rows] = context
        half_rows = slice(part * query_block // 2, (part + 1) * query_block // 2)
        ctx_send[half_rows] = pack_high(context).astype(BF16)

    high = jnp.full((8, query_block), NEGATIVE, F32)
    for index in range(2):
        settle(f"keys {index} in")
        forward = remote(
            quarter(core, index), quarter(core, index), send.at[7 + 17 * index], recv.at[7 + 17 * index], partner
        )
        forward.start()
        later(f"forward {index} in", quarter(other, index), recv.at[7 + 17 * index])
        pending[f"forward {index} out"] = forward.wait_send
        prepare_keys(core, index)
        if index == 0:
            settle("heads 1 in")
            for slot in range(heads):
                rows = slice(ROWS * slot, ROWS * slot + ROWS)
                part = unpack_low(qpk[slot].astype(F32))
                lane = lax.broadcasted_iota(jnp.int32, part.shape, 1)
                qcl[rows] = (part * 0.125).astype(BF16)
                qaug[rows] = jnp.where(lane == 64, 1.0, part).astype(BF16)
        high = scores_step(0, core * 2 + index, high)
    for index in range(2):
        settle(f"forward {index} in")
        prepare_keys(other, index)
        high = scores_step(0, other * 2 + index, high)

    start_high = jnp.full((8, query_block), NEGATIVE, F32)
    start_total = jnp.zeros((128, query_block), F32)
    for part in range(query_blocks):
        highest = jnp.max(high, axis=0, keepdims=True)
        if part + 1 < query_blocks:

            def both(b, carried, part=part, highest=highest):
                h, t = carried
                return scores_step(part + 1, b, h), weights_step(part, b, highest, t)

            high, total = lax.fori_loop(0, 4, both, (start_high, start_total))
        else:
            total = lax.fori_loop(
                0, 4, lambda b, t, part=part, highest=highest: weights_step(part, b, highest, t), start_total
            )
        context_finish(part, total)

    my_head = chip % heads
    moves = [(-1, 0, 16, 80), (0, 0, 80, 16)]
    moves += [(i, 64 * i - 16, 96, 0) for i in range(1, heads - 1)]
    moves += [(heads - 1, 64 * (heads - 1) - 16, 80, 0), (heads, 64 * heads - 16, 16, 0)]

    def owner_of(i):
        return (group * heads + i + seq) % seq

    for index, (i, start, count, to) in enumerate(moves):
        source = ctx_send.at[pl.ds(start, count)]
        target = ctx_recv.at[my_head, pl.ds(to, count)]

        @pl.when(owner_of(i) == me)
        def _(source=source, target=target):
            pltpu.make_async_copy(source, target, recv.at[8]).start()

        @pl.when(owner_of(i) != me)
        def _(source=source, target=target, i=i, index=index):
            remote(source, target, ctx_sem.at[index], recv.at[8], (z, owner_of(i))).start()

        def sent(source=source, i=i, index=index):
            @pl.when(owner_of(i) != me)
            def _():
                drain(source, ctx_sem.at[index])

        pending[f"context {index}"] = sent

    def live(rows, first):
        frame = me * ROWS + first + lax.broadcasted_iota(jnp.int32, (rows, 128), 0)
        return jnp.logical_and(frame >= 0, frame < length)

    def column(chunk):
        return pl.ds(pl.multiple_of(chunk * 128, 128), 128)

    def turned_convolution(rows, columns):
        total = jnp.zeros((ROWS, 128), F32)
        for low in range(8):
            moved = shifted(rows, low)
            for high_part in range(4):
                tap = 31 - (8 * high_part + low)
                if 0 <= tap < KERNEL:
                    total = total + taps_ref[tap : tap + 1, columns] * moved[8 * high_part : 8 * high_part + ROWS]
        return total

    settle("w", "taps", "gain", "shift")

    @pl.loop(0, chunks)
    def _(chunk):
        columns = column(chunk)
        cmask_ref[:, columns] = turned_convolution(jnp.where(live(mid, -16), 1.0, 0.0), columns)

    settle("lengths in")
    lengths = len_recv[:, :1]
    count_a[...] = jnp.clip(lengths - (me * ROWS).astype(F32), 0.0, float(ROWS))
    for i in range(seq):
        count_b[i] = jnp.sum(jnp.clip(lengths - float(i * ROWS), 0.0, float(ROWS)), axis=0)
    for target in (tmask_ref, tgrad_ref, tnorm_ref):
        target[KERNEL:] = jnp.zeros((1, channels), F32)

    settle(*(f"halo {index} in" for index in range(4)))
    drain(ctx_recv, recv.at[8])

    for pair in range(heads // 2):
        ctx_ref[:, 128 * pair : 128 * pair + 128] = unpack_pair(
            ctx_recv[2 * pair].astype(F32), ctx_recv[2 * pair + 1].astype(F32)
        ).astype(BF16)

    counted = jnp.clip(length - me * ROWS, 0, ROWS).astype(F32)

    @pl.loop(0, channels // 256)
    def _(chunk):
        columns = pl.ds(pl.multiple_of(chunk * 256, 256), 256)
        hidden = x_ext[:, columns].astype(F32) + dot(ctx_ref[...], w_ref[:, columns])
        mask = live(ext, -HALO)
        mask = jnp.concatenate([mask, mask], axis=1)
        hid_ref[:, columns] = jnp.where(mask, hidden, 0.0).astype(BF16).astype(F32)

    @pl.loop(0, chunks)
    def _(chunk):
        columns = column(chunk)
        hidden = hid_ref[:, columns]
        total = jnp.zeros((mid, 128), F32)
        for low in range(8):
            moved = shifted(hidden, low)
            for high_part in range(4):
                tap = 8 * high_part + low - 1
                if 0 <= tap < KERNEL:
                    total = total + taps_ref[tap : tap + 1, columns] * moved[8 * high_part : 8 * high_part + mid]
        conv_ref[:, columns] = total
        own = total[16 : 16 + ROWS]
        mask = live(ROWS, 0)
        summed = jnp.sum(jnp.where(mask, own, 0.0), axis=0, keepdims=True)
        mean = summed / jnp.maximum(counted, 1.0)
        spread = own - mean
        squares = jnp.sum(jnp.where(mask, spread * spread, 0.0), axis=0, keepdims=True)
        stat_a[pl.ds(chunk, 1)] = summed
        stat_a[pl.ds(chunks + chunk, 1)] = squares


    def write(source, target, index):
        copy = pltpu.make_async_copy(source, target, write_sem.at[index])
        copy.start()
        pending[f"write {index}"] = copy.wait

    def gather(source, target, index, slot, count, peer, beside):
        target[slot] = source[...]

        around(
            count,
            lambda d: remote(source, target.at[slot], send.at[index], recv.at[index], peer(d)).start(),
        )

        later(f"sums {index}", target.at[pl.ds(0, count - 1)], send.at[index])
        if beside is not None:
            beside()
        drain(target.at[pl.ds(0, count - 1)], recv.at[index])

    def gather_first(source, target, index, beside=None):
        gather(source, target, index, z, depth, lambda d: ((z + d) % depth, me), beside)

    def gather_second(source, target, index, beside=None):
        gather(source, target, index, me, seq, lambda d: (z, (me + d) % seq), beside)

    def correlate(target, rows, columns):
        hidden = hid_ref[16:, columns]
        for low in range(8):
            moved = shifted(hidden, low)
            for high_part in range(4):
                tap = 8 * high_part + low - 1
                if 0 <= tap < KERNEL:
                    terms = rows * moved[8 * high_part : 8 * high_part + ROWS]
                    target[tap : tap + 1, columns] = jnp.sum(terms, axis=0, keepdims=True)

    def correlate_mask():
        own_ctx[...] = jnp.transpose(ctx_ref[HALO : HALO + ROWS].astype(F32)).astype(BF16)

        @pl.loop(0, chunks)
        def _(chunk):
            correlate(tmask_ref, jnp.where(live(ROWS, 0), 1.0, 0.0), column(chunk))

    def correlate_rest():
        @pl.loop(0, chunks)
        def _(chunk):
            columns = column(chunk)
            own = slice(16, 16 + ROWS)
            correlate(tgrad_ref, ga_ref[own, columns], columns)
            correlate(tnorm_ref, jnp.where(live(ROWS, 0), conv_ref[own, columns], 0.0), columns)

    def merged(gathered, counts):
        sums = gathered[:, :chunks]
        squares = gathered[:, chunks:]
        count = jnp.sum(counts, axis=0)
        total = jnp.sum(sums, axis=0)
        mean = total / jnp.maximum(count, 1.0)
        shift = sums / jnp.maximum(counts, 1.0) - mean[None]
        return total, jnp.sum(squares, axis=0) + jnp.sum(counts * shift * shift, axis=0), count, mean

    gather_first(stat_a, recv_a, 9, correlate_mask)
    total, squares, count, mean = merged(recv_a[...], count_a[...])
    stat_b[:chunks] = total
    stat_b[chunks:] = squares
    gather_second(stat_b, recv_b, 10)
    total, squares, count, mean = merged(recv_b[...], count_b[...])
    tot_ref[:chunks] = mean
    tot_ref[chunks : 2 * chunks] = lax.rsqrt(squares / count + EPSILON)
    tot_ref[2 * chunks : 3 * chunks] = jnp.broadcast_to(1.0 / count, (chunks, 128))

    @pl.loop(0, chunks)
    def _(chunk):
        columns = column(chunk)
        mean = tot_ref[pl.ds(chunk, 1)]
        inverse = tot_ref[pl.ds(chunks + chunk, 1)]
        normed = (conv_ref[:, columns] - mean) * inverse
        conv_ref[:, columns] = normed
        act = normed * gain_ref[:, columns] + shift_ref[:, columns]
        gate = 1.0 / (1.0 + jnp.exp(-act))
        grad_out = jnp.where(live(mid, -16), cot_ext[:, columns].astype(F32), 0.0)
        grad_act = grad_out * gate * (1.0 + act * (1.0 - gate))
        ga_ref[:, columns] = grad_act
        own = grad_act[16 : 16 + ROWS]
        stat_c[pl.ds(chunk, 1)] = jnp.sum(own * normed[16 : 16 + ROWS], axis=0, keepdims=True)
        stat_c[pl.ds(chunks + chunk, 1)] = jnp.sum(own, axis=0, keepdims=True)
        gated = (act * gate)[16 : 16 + ROWS]
        hidden = hid_ref[HALO : HALO + ROWS, columns]
        out_ref[:, columns] = jnp.where(live(ROWS, 0), hidden + gated, 0.0).astype(BF16)

    def beside():
        write(out_ref, out_hbm, 0)

        @pl.loop(0, chunks)
        def _(chunk):
            columns = column(chunk)
            cgrad_ref[:, columns] = turned_convolution(ga_ref[:, columns], columns)
            cnorm_ref[:, columns] = turned_convolution(
                jnp.where(live(mid, -16), conv_ref[:, columns], 0.0), columns
            )

    gather_first(stat_c, recv_c, 11, beside)
    stat_d[...] = jnp.sum(recv_c[...], axis=0)
    gather_second(stat_d, recv_d, 12, correlate_rest)
    sums_ref[...] = jnp.sum(recv_d[...], axis=0)

    @pl.loop(0, chunks)
    def _(chunk):
        columns = column(chunk)
        inverse = tot_ref[pl.ds(chunks + chunk, 1)]
        per_count = tot_ref[pl.ds(2 * chunks + chunk, 1)]
        gain_sum = sums_ref[pl.ds(chunk, 1)] * per_count
        shift_sum = sums_ref[pl.ds(chunks + chunk, 1)] * per_count
        scale = inverse * gain_ref[:, columns]
        turned = cgrad_ref[:, columns] - shift_sum * cmask_ref[:, columns] - gain_sum * cnorm_ref[:, columns]
        total = cot_ext[16 : 16 + ROWS, columns].astype(F32) + scale * turned
        ginp_ref[:, columns] = jnp.where(live(ROWS, 0), total, 0.0).astype(BF16)

    write(ginp_ref, ginp_hbm, 1)

    def stage0(piece):
        copy = remote(
            wsend.at[piece].at[other], g0.at[piece], piece_send.at[5 * piece + 0], piece_recv.at[5 * piece + 0], partner
        )
        copy.start()
        pending[f"stage 0 in {piece}"] = copy.wait_recv
        pending[f"stage 0 out {piece}"] = copy.wait_send

    for piece in range(PIECES):
        first = piece * piece_width
        size = min(piece_width, channels - first)
        if size > 0:
            terms = dot(own_ctx[...], ginp_ref[:, first : first + size]).astype(BF16)
            wsend.at[piece][:, :, :, :size] = terms.reshape(2, chips, 16, size)
        if piece < PIECES - 1:
            stage0(piece)

    tap_lanes = slice(piece_width - 128, piece_width)
    wsend[PIECES - 1, :, :, :, tap_lanes] = jnp.zeros((2, chips, 16, 128), BF16)

    @pl.loop(0, chunks)
    def _(chunk):
        columns = column(chunk)
        per_count = tot_ref[pl.ds(2 * chunks + chunk, 1)]
        gain_sum = sums_ref[pl.ds(chunk, 1)] * per_count
        shift_sum = sums_ref[pl.ds(chunks + chunk, 1)] * per_count
        scale = tot_ref[pl.ds(chunks + chunk, 1)] * gain_ref[:, columns]
        stacked = tgrad_ref[:, columns] - shift_sum * tmask_ref[:, columns] - gain_sum * tnorm_ref[:, columns]
        stacked = (scale * stacked).astype(BF16)
        wsend.at[PIECES - 1].at[0][pl.ds(chunk, 1), :, tap_lanes] = stacked[:16].reshape(1, 16, 128)
        wsend.at[PIECES - 1].at[1][pl.ds(chunk, 1), :, tap_lanes] = stacked[16:].reshape(1, 16, 128)

    stage0(PIECES - 1)

    def stage1(piece):
        settle(f"stage 0 in {piece}")

        total = wsend.at[piece].at[core][...].astype(F32) + g0[piece].astype(F32)
        gs1[piece] = total.astype(BF16)
        g1.at[piece].at[chip][...] = gs1.at[piece].at[chip][...]

        @pl.loop(1, chips)
        def _(d):
            peer = (chip + d) % chips
            remote(
                gs1.at[piece].at[peer],
                g1.at[piece].at[chip],
                piece_send.at[5 * piece + 1],
                piece_recv.at[5 * piece + 1],
                (z, peer * 2 + core),
            ).start()

        later(f"stage 1 in {piece}", g1.at[piece].at[pl.ds(0, chips - 1)], piece_recv.at[5 * piece + 1])
        later(f"stage 1 out {piece}", g1.at[piece].at[pl.ds(0, chips - 1)], piece_send.at[5 * piece + 1])

    for piece in range(PIECES - 1):
        stage1(piece)

    @pl.loop(0, heads // 2)
    def _(pair):
        rows = pl.ds(pl.multiple_of(pair * 128, 128), 128)
        grad_context = dot(ginp_ref[...], w_ref[rows], ((1,), (1,))).astype(BF16).astype(F32)
        even, odd = pack_pair(grad_context)
        do_send[2 * pair] = even.astype(BF16)
        do_send[2 * pair + 1] = odd.astype(BF16)

    to_heads(do_send, do_recv, 13, 14)

    def stage2(piece):
        settle(f"stage 1 in {piece}")
        total = g1.at[piece][0].astype(F32)
        for i in range(1, chips):
            total = total + g1.at[piece][i].astype(F32)
        total = total.astype(BF16)
        gs2[piece] = total
        g2.at[piece].at[z][...] = total

        @pl.loop(1, depth)
        def _(d):
            remote(
                gs2.at[piece],
                g2.at[piece].at[z],
                piece_send.at[5 * piece + 2],
                piece_recv.at[5 * piece + 2],
                ((z + d) % depth, me),
            ).start()

        pending[f"stage 2 in {piece}"] = lambda: drain(
            g2.at[piece].at[pl.ds(0, depth - 1)], piece_recv.at[5 * piece + 2]
        )
        pending[f"stage 2 out {piece}"] = lambda: drain(
            g2.at[piece].at[pl.ds(0, depth - 1)], piece_send.at[5 * piece + 2]
        )

    def stage3(piece):
        settle(f"stage 2 in {piece}")
        total = g2.at[piece][0].astype(F32)
        for i in range(1, depth):
            total = total + g2.at[piece][i].astype(F32)
        gfin_ref.at[piece].at[core, chip][...] = total.astype(BF16)
        final = gfin_ref.at[piece].at[core, chip]

        @pl.loop(1, chips)
        def _(d):
            peer = (chip + d) % chips
            remote(
                final, final, piece_send.at[5 * piece + 3], piece_recv.at[5 * piece + 3], (z, peer * 2 + core)
            ).start()

        pending[f"stage 3 in {piece}"] = lambda: drain(
            gfin_ref.at[piece].at[core, pl.ds(0, chips - 1)], piece_recv.at[5 * piece + 3]
        )
        pending[f"stage 3 out {piece}"] = lambda: drain(
            gfin_ref.at[piece].at[core, pl.ds(0, chips - 1)], piece_send.at[5 * piece + 3]
        )

    def stage4(piece):
        settle(f"stage 3 in {piece}")
        finals = gfin_ref.at[piece].at[core]
        copy = remote(finals, finals, piece_send.at[5 * piece + 4], piece_recv.at[5 * piece + 4], partner)
        copy.start()
        later(f"stage 4 in {piece}", gfin_ref.at[piece].at[other], piece_recv.at[5 * piece + 4])
        pending[f"stage 4 out {piece}"] = copy.wait_send

    stage1(PIECES - 1)

    settle("heads 13 in")
    for index in range(heads):
        rows = slice(ROWS * index, ROWS * index + ROWS)
        scaled = (unpack_high(do_recv[index].astype(F32)) * linv[rows]).astype(BF16)
        docl[rows] = scaled
        scaled = scaled.astype(F32)
        delta = jnp.sum(ctxh[rows] * scaled, axis=1, keepdims=True)
        first = delta.astype(BF16).astype(F32)
        rest = delta - first
        lane = lax.broadcasted_iota(jnp.int32, scaled.shape, 1)
        doaug[rows] = jnp.where(lane == 0, -first, jnp.where(lane == 1, -rest, scaled)).astype(BF16)

    dqt[...] = jnp.zeros_like(dqt)

    def part_copy(turn):
        rows = pl.ds(pl.multiple_of(turn * backward_block, backward_block), backward_block)
        return remote(dsend.at[rows], precv.at[rows], part_send.at[turn], part_recv.at[turn], partner)

    turns = 4
    slots = backward_block // ROWS

    @pl.loop(0, 2 * turns)
    def _(step):
        half = jnp.where(step < turns, other, core)
        turn = step % turns
        rows = pl.ds(
            pl.multiple_of(half * half_keys + turn * backward_block, backward_block), backward_block
        )
        turn_rows = pl.ds(pl.multiple_of(turn * backward_block, backward_block), backward_block)
        weights = pt[rows]
        grads = dot(v1[rows], doaug[...], ((1,), (1,))).astype(BF16)
        scores = weights * grads
        dqt[...] += dot(kt[:, rows], scores)
        rbuf[...] = dot(scores, qcl[...]) + dot(weights, docl[...])

        @pl.when(step < turns)
        def _():
            dsend[turn_rows] = rbuf[...].astype(BF16)
            part_copy(turn).start()

        @pl.when(step >= turns)
        def _():
            part_copy(turn).wait_recv()
            osend[turn_rows] = (rbuf[...] + precv[turn_rows].astype(F32)).astype(BF16)
            for i in range(slots):
                slot = turn * slots + i
                owner = (chip + chips - slot) % chips
                source = osend.at[pl.ds(pl.multiple_of(slot * ROWS, ROWS), ROWS)]

                def give(source=source, owner=owner):
                    remote(source, kvrecv.at[chip], own_sem, recv.at[20], (z, owner * 2 + core)).start()

                if i == 0:

                    @pl.when(turn == 0)
                    def _(source=source):
                        pltpu.make_async_copy(source, kvrecv.at[chip], recv.at[20]).start()

                    pl.when(turn > 0)(give)
                else:
                    give()

        for piece in range(PIECES):

            @pl.when(step == 2 + piece)
            def _(piece=piece):
                stage2(piece)

        for piece in range(PIECES - 1):

            @pl.when(step == 6 + piece)
            def _(piece=piece):
                stage3(piece)

    stage3(PIECES - 1)

    def parts_sent():
        @pl.loop(0, turns)
        def _(turn):
            part_copy(turn).wait_send()

    pending["parts"] = parts_sent
    later("owned in", kvrecv, recv.at[20])
    later("owned out", kvrecv.at[pl.ds(0, chips - 1)], own_sem)

    @pl.loop(0, query_blocks)
    def _(block):
        part = pl.ds(pl.multiple_of(block * query_block, query_block), query_block)
        turned = dqt[:, part]
        turned = jnp.transpose(jnp.concatenate([turned, jnp.zeros_like(turned)], axis=0))
        half_part = pl.ds(pl.multiple_of(block * query_block // 2, query_block // 2), query_block // 2)
        dq_send[half_part] = pack_low(turned).astype(BF16)

    for i in range(heads):
        source = dq_send.at[pl.ds(64 * i, 64)]
        target = dq_recv.at[my_head]

        @pl.when(owner_of(i) == me)
        def _(source=source, target=target):
            pltpu.make_async_copy(source, target, recv.at[21]).start()

        @pl.when(owner_of(i) != me)
        def _(source=source, target=target, i=i):
            remote(source, target, dq_sem.at[i], recv.at[21], (z, owner_of(i))).start()

        def sent(source=source, i=i):
            @pl.when(owner_of(i) != me)
            def _():
                drain(source, dq_sem.at[i])

        pending[f"grad query {i}"] = sent

    settle("owned in")
    for pair in range(heads // 2):
        columns = slice(128 * pair, 128 * pair + 128)
        even = kvrecv[2 * pair].astype(F32) + kvrecv[2 * pair + heads].astype(F32)
        odd = kvrecv[2 * pair + 1].astype(F32) + kvrecv[2 * pair + 1 + heads].astype(F32)
        low = low_lanes(even.shape)
        gk_ref[:, columns] = jnp.where(low, even, roll64(odd)).astype(BF16)
        gv_ref[:, columns] = jnp.where(low, roll64(even), odd).astype(BF16)
    write(gk_ref, gk_hbm, 3)
    write(gv_ref, gv_hbm, 4)

    drain(dq_recv, recv.at[21])
    for pair in range(heads // 2):
        gq_ref[:, 128 * pair : 128 * pair + 128] = unpack_pair(
            dq_recv[2 * pair].astype(F32), dq_recv[2 * pair + 1].astype(F32)
        ).astype(BF16)

    write(gq_ref, gq_hbm, 2)
    for piece in range(PIECES):
        stage4(piece)
    settle()


def finish(width, chunks, *refs):
    sources = refs[:7]
    outs = refs[7:16]
    out, ginp, gq, gk, gv, packed, sums = refs[16:23]
    weights, taps, load_sem, sem = refs[23:]
    channels = weights.shape[1]
    loads = [
        pltpu.make_async_copy(source, target, load_sem.at[index])
        for index, (source, target) in enumerate(zip(sources, refs[16:23]))
    ]
    for index in (5, 6, 0, 1, 2, 3, 4):
        loads[index].start()
    copies = [
        pltpu.make_async_copy(source, target, sem.at[index])
        for index, (source, target) in enumerate(
            (
                (out, outs[0]),
                (ginp, outs[1]),
                (gq, outs[2]),
                (gk, outs[3]),
                (gv, outs[4]),
                (weights, outs[5]),
                (taps, outs[6]),
                (sums.at[pl.ds(0, chunks)], outs[7]),
                (sums.at[pl.ds(chunks, chunks)], outs[8]),
            )
        )
    ]
    loads[5].wait()
    piece_width = packed.shape[-1]
    for piece in range(PIECES):
        first = piece * piece_width
        size = min(piece_width, channels - first)
        for half in range(2 if size > 0 else 0):
            rows = slice(half * width // 2, (half + 1) * width // 2)
            terms = packed[piece, half, :, :, :size].astype(F32)
            weights[rows, first : first + size] = terms.reshape(width // 2, size)
    for chunk in range(chunks):
        lanes = slice(piece_width - 128, piece_width)
        columns = slice(128 * chunk, 128 * chunk + 128)
        taps[:16, columns] = packed[PIECES - 1, 0, chunk, :, lanes].astype(F32)
        taps[16:, columns] = packed[PIECES - 1, 1, chunk, :15, lanes].astype(F32)
    copies[5].start()
    copies[6].start()
    loads[6].wait()
    copies[7].start()
    copies[8].start()
    for index in range(5):
        loads[index].wait()
        copies[index].start()
    for copy in copies:
        copy.wait()


def shards(
    depth,
    query_rows,
    key_rows,
    value_rows,
    inputs,
    lengths,
    out_weight,
    taps,
    norm_gain,
    norm_shift,
    cotangent,
):
    seq = lax.axis_size("seq")
    heads = seq // 4
    chips = seq // 2
    width = query_rows.shape[2]
    channels = inputs.shape[2]
    chunks = channels // 128
    queries = ROWS * heads
    keys = seq * ROWS
    ext = ROWS + 2 * HALO
    mid = ROWS + 32
    padded = channels + 128
    piece_width = padded // PIECES
    query_block = min(queries, 512)
    vmem = pltpu.VMEM
    scratch = [
        vmem((ROWS, width), BF16),
        vmem((ROWS, width), BF16),
        vmem((ROWS, width), BF16),
        vmem((1, channels), F32),
        vmem((1, channels), F32),
        vmem((ROWS, channels), BF16),
        vmem((ROWS, channels), BF16),
        vmem((ROWS, width), BF16),
        vmem((ROWS, width), BF16),
        vmem((ROWS, width), BF16),
        vmem((8, 128), F32),
        vmem((depth, 8, 128), F32),
        vmem((ROWS, channels), F32),
        vmem((ROWS, channels), F32),
        vmem((ROWS, channels), F32),
        vmem((width, ROWS), BF16),
        vmem((KERNEL + 1, channels), F32),
        vmem((KERNEL + 1, channels), F32),
        vmem((KERNEL + 1, channels), F32),
        vmem((depth, 1, 128), F32),
        vmem((seq, 1, 128), F32),
        vmem((heads, ROWS, 128), BF16),
        vmem((heads, 64, 128), BF16),
        vmem((keys, 128), BF16),
        vmem((heads, 64, 128), BF16),
        vmem((keys, 128), BF16),
        vmem((keys, 128), BF16),
        vmem((64, keys), BF16),
        vmem((128, keys), BF16),
        vmem((queries, 128), BF16),
        vmem((queries, 128), BF16),
        vmem((2, keys, query_block), F32),
        vmem((keys, queries), BF16),
        vmem((queries, 128), F32),
        vmem((queries, 128), F32),
        vmem((queries // 2, 128), BF16),
        vmem((heads, ext // 2, 128), BF16),
        vmem((ext, channels), BF16),
        vmem((mid, channels), BF16),
        vmem((width, channels), BF16),
        vmem((KERNEL, channels), F32),
        vmem((ext, width), BF16),
        vmem((ext, channels), F32),
        vmem((mid, channels), F32),
        vmem((mid, channels), F32),
        vmem((2 * chunks, 128), F32),
        vmem((2 * chunks, 128), F32),
        vmem((depth, 2 * chunks, 128), F32),
        vmem((seq, 2 * chunks, 128), F32),
        vmem((2 * chunks, 128), F32),
        vmem((depth, 2 * chunks, 128), F32),
        vmem((2 * chunks, 128), F32),
        vmem((seq, 2 * chunks, 128), F32),
        vmem((3 * chunks, 128), F32),
        vmem((heads, 64, 128), BF16),
        vmem((heads, 64, 128), BF16),
        vmem((queries, 128), BF16),
        vmem((queries, 128), BF16),
        vmem((keys // 8, 128), F32),
        vmem((64, queries), F32),
        vmem((keys // 2, 128), BF16),
        vmem((keys // 2, 128), BF16),
        vmem((keys // 2, 128), BF16),
        vmem((chips, ROWS, 128), BF16),
        vmem((queries // 2, 128), BF16),
        vmem((heads, 64, 128), BF16),
        vmem((PIECES, 2, chips, 16, piece_width), BF16),
        vmem((PIECES, chips, 16, piece_width), BF16),
        vmem((PIECES, chips, 16, piece_width), BF16),
        vmem((PIECES, chips, 16, piece_width), BF16),
        vmem((PIECES, 16, piece_width), BF16),
        vmem((PIECES, depth, 16, piece_width), BF16),
        pltpu.SemaphoreType.DMA((9,)),
        pltpu.SemaphoreType.DMA((25,)),
        pltpu.SemaphoreType.DMA((25,)),
        pltpu.SemaphoreType.DMA((heads + 2,)),
        pltpu.SemaphoreType.DMA((heads,)),
        pltpu.SemaphoreType.DMA((4,)),
        pltpu.SemaphoreType.DMA((4,)),
        pltpu.SemaphoreType.DMA,
        pltpu.SemaphoreType.DMA((5 * PIECES,)),
        pltpu.SemaphoreType.DMA((5 * PIECES,)),
        pltpu.SemaphoreType.DMA((5,)),
    ]
    in_vmem = pl.BlockSpec(memory_space=pltpu.VMEM)
    anywhere = pl.BlockSpec(memory_space=pl.ANY)
    plain = (
        jax.ShapeDtypeStruct((ROWS, channels), BF16),
        jax.ShapeDtypeStruct((ROWS, channels), BF16),
        jax.ShapeDtypeStruct((ROWS, width), BF16),
        jax.ShapeDtypeStruct((ROWS, width), BF16),
        jax.ShapeDtypeStruct((ROWS, width), BF16),
    )
    results = pl.pallas_call(
        functools.partial(kernel, heads, seq, depth),
        out_shape=plain
        + (
            jax.ShapeDtypeStruct((PIECES, 2, chips, 16, piece_width), BF16),
            jax.ShapeDtypeStruct((2 * chunks, 128), F32),
        ),
        in_specs=[pl.BlockSpec(memory_space=pltpu.SMEM)] + [anywhere] * 9,
        out_specs=(anywhere,) * 5 + (in_vmem,) * 2,
        scratch_shapes=scratch,
        compiler_params=pltpu.CompilerParams(
            collective_id=0, has_side_effects=True, vmem_limit_bytes=60 * 1024 * 1024
        ),
    )(
        lengths,
        query_rows[0],
        key_rows[0],
        value_rows[0],
        inputs[0],
        cotangent[0],
        out_weight,
        taps,
        norm_gain[None],
        norm_shift[None],
    )
    final = pl.pallas_call(
        functools.partial(finish, width, chunks),
        out_shape=plain
        + (
            jax.ShapeDtypeStruct((width, channels), F32),
            jax.ShapeDtypeStruct((KERNEL, channels), F32),
            jax.ShapeDtypeStruct((chunks, 128), F32),
            jax.ShapeDtypeStruct((chunks, 128), F32),
        ),
        in_specs=[anywhere] * 7,
        out_specs=(anywhere,) * 9,
        scratch_shapes=[vmem(array.shape, array.dtype) for array in results]
        + [
            vmem((width, channels), F32),
            vmem((KERNEL, channels), F32),
            pltpu.SemaphoreType.DMA((7,)),
            pltpu.SemaphoreType.DMA((9,)),
        ],
        compiler_params=pltpu.CompilerParams(vmem_limit_bytes=60 * 1024 * 1024),
    )(*results)
    return (
        *(array[None] for array in final[:5]),
        final[5],
        final[6],
        final[7].reshape(channels),
        final[8].reshape(channels),
    )


def solution(mesh):
    rows = P("dp", "seq", None)
    return jax.shard_map(
        functools.partial(shards, mesh.shape["dp"]),
        mesh=mesh,
        in_specs=(rows, rows, rows, rows, P("dp"), P(), P(), P(), P(), rows),
        out_specs=(rows, rows, rows, rows, rows, P(), P(), P(), P()),
        check_vma=False,
    )
```

```python
import functools

import jax
import jax.numpy as jnp
from jax import lax
from jax.experimental import pallas as pl
from jax.experimental.pallas import tpu as pltpu
from jax.sharding import PartitionSpec as P

KERNEL = 31
HALF = 15
HEAD_DIM = 64
ROWS = 128
HALO = 32
NEGATIVE = -1e30
EPSILON = 1e-05
PIECES = 3
MESH = pl.DeviceIdType.MESH
F32 = jnp.float32
BF16 = jnp.bfloat16


def roll64(x):
    return pltpu.roll(x, 64, 1)


def low_lanes(shape):
    return lax.broadcasted_iota(jnp.int32, shape, 1) < 64


def split_units(x):
    rows = x.shape[0]
    units = x.reshape(rows // 32, 2, 16, 128)
    return units[:, 0].reshape(rows // 2, 128), units[:, 1].reshape(rows // 2, 128)


def join_units(first, second):
    rows = first.shape[0]
    first = first.reshape(rows // 16, 1, 16, 128)
    second = second.reshape(rows // 16, 1, 16, 128)
    return jnp.concatenate([first, second], axis=1).reshape(2 * rows, 128)


def pack_pair(x):
    first, second = split_units(x)
    low = low_lanes(first.shape)
    even = jnp.where(low, first, roll64(second))
    odd = jnp.where(low, roll64(first), second)
    return even, odd


def unpack_pair(even, odd):
    low = low_lanes(even.shape)
    return join_units(jnp.where(low, even, roll64(odd)), jnp.where(low, roll64(even), odd))


def unpack_low(packed):
    low = low_lanes(packed.shape)
    return join_units(jnp.where(low, packed, 0.0), jnp.where(low, roll64(packed), 0.0))


def unpack_high(packed):
    low = low_lanes(packed.shape)
    return join_units(jnp.where(low, 0.0, roll64(packed)), jnp.where(low, 0.0, packed))


def pack_low(x):
    first, second = split_units(x)
    return jnp.where(low_lanes(first.shape), first, roll64(second))


def pack_high(x):
    first, second = split_units(x)
    return jnp.where(low_lanes(first.shape), roll64(first), second)


def dot(a, b, dims=((1,), (0,))):
    return lax.dot_general(a, b, (dims, ((), ())), preferred_element_type=F32)


def shifted(x, amount):
    return x if amount == 0 else pltpu.roll(x, x.shape[0] - amount, 0)


def kernel(
    heads,
    seq,
    depth,
    length_ref,
    q_hbm,
    k_hbm,
    v_hbm,
    x_hbm,
    cot_hbm,
    w_hbm,
    taps_hbm,
    gain_hbm,
    shift_hbm,
    out_hbm,
    ginp_hbm,
    gq_hbm,
    gk_hbm,
    gv_hbm,
    gfin_ref,
    sums_ref,
    q_ref,
    k_ref,
    v_ref,
    gain_ref,
    shift_ref,
    out_ref,
    ginp_ref,
    gq_ref,
    gk_ref,
    gv_ref,
    len_send,
    len_recv,
    cmask_ref,
    cgrad_ref,
    cnorm_ref,
    own_ctx,
    tmask_ref,
    tgrad_ref,
    tnorm_ref,
    count_a,
    count_b,
    kv_send,
    q_send,
    kvbuf,
    qpk,
    k1,
    v1,
    kt,
    v1t,
    qaug,
    qcl,
    sbuf,
    pt,
    ctxh,
    linv,
    ctx_send,
    ctx_recv,
    x_ext,
    cot_ext,
    w_ref,
    taps_ref,
    ctx_ref,
    hid_ref,
    conv_ref,
    ga_ref,
    stat_a,
    stat_b,
    recv_a,
    recv_b,
    stat_c,
    recv_c,
    stat_d,
    recv_d,
    tot_ref,
    do_send,
    do_recv,
    doaug,
    docl,
    rbuf,
    dqt,
    dsend,
    precv,
    osend,
    kvrecv,
    dq_send,
    dq_recv,
    wsend,
    g0,
    gs1,
    g1,
    gs2,
    g2,
    load_sem,
    send,
    recv,
    ctx_sem,
    dq_sem,
    part_send,
    part_recv,
    own_sem,
    piece_send,
    piece_recv,
    write_sem,
):
    chips = seq // 2
    width = q_ref.shape[1]
    channels = out_ref.shape[1]
    chunks = channels // 128
    queries = ROWS * heads
    half_keys = chips * ROWS
    forward_block = half_keys // 2
    backward_block = half_keys // 4
    query_block = min(queries, 512)
    query_blocks = queries // query_block
    padded = channels + 128
    piece_width = padded // PIECES
    ext = ROWS + 2 * HALO
    mid = ROWS + 32

    z = lax.axis_index("dp")
    me = lax.axis_index("seq")
    chip = me // 2
    core = me % 2
    other = 1 - core
    partner = (z, chip * 2 + other)
    group = (chip // heads) * 2 + core
    my_group = me // heads
    length = length_ref[0]

    def remote(src, dst, send_sem, recv_sem, device):
        return pltpu.make_async_remote_copy(
            src_ref=src, dst_ref=dst, send_sem=send_sem, recv_sem=recv_sem, device_id=device, device_id_type=MESH
        )

    def drain(ref, sem):
        pltpu.make_async_copy(ref, ref, sem).wait()

    pending = {}

    def later(name, ref, sem):
        pending[name] = lambda: drain(ref, sem)

    def settle(*names):
        for name in names or tuple(pending):
            pending.pop(name)()

    def around(count, act):
        act(count // 2)

        @pl.loop(1, count // 2)
        def _(k):
            act(count // 2 + k)
            act(count // 2 - k)

    barrier = pltpu.get_barrier_semaphore()

    def greet(device):
        pl.semaphore_signal(barrier, inc=1, device_id=device, device_id_type=MESH)

    around(depth, lambda d: greet(((z + d) % depth, me)))
    around(seq, lambda d: greet((z, (me + d) % seq)))


    loads = (
        ("k", k_hbm, k_ref),
        ("v", v_hbm, v_ref),
        ("q", q_hbm, q_ref),
        ("x", x_hbm, x_ext.at[pl.ds(HALO, ROWS)]),
        ("cot", cot_hbm, cot_ext.at[pl.ds(16, ROWS)]),
        ("w", w_hbm, w_ref),
        ("taps", taps_hbm, taps_ref),
        ("gain", gain_hbm, gain_ref),
        ("shift", shift_hbm, shift_ref),
    )
    for index, (name, source, target) in enumerate(loads):
        copy = pltpu.make_async_copy(source, target, load_sem.at[index])
        copy.start()
        pending[name] = copy.wait

    len_send[...] = jnp.full((8, 128), length.astype(F32), F32)
    settle("k", "v", "q")
    for pair in range(heads // 2):
        columns = slice(128 * pair, 128 * pair + 128)
        kp = k_ref[:, columns].astype(F32)
        vp = v_ref[:, columns].astype(F32)
        low = low_lanes(kp.shape)
        kv_send[2 * pair] = jnp.where(low, kp, roll64(vp)).astype(BF16)
        kv_send[2 * pair + 1] = jnp.where(low, roll64(kp), vp).astype(BF16)
        even, odd = pack_pair(q_ref[:, columns].astype(F32))
        q_send[2 * pair] = even.astype(BF16)
        q_send[2 * pair + 1] = odd.astype(BF16)

    pl.semaphore_wait(barrier, seq - 1 + depth - 1)

    def kv_slot(d):
        return kvbuf.at[pl.ds(pl.multiple_of(core * half_keys + d * ROWS, ROWS), ROWS)]

    def send_keys(first, last, index):
        @pl.loop(first, last)
        def _(d):
            peer = (chip + d) % chips
            remote(kv_send.at[peer % heads], kv_slot(d), send.at[index], recv.at[index], (z, peer * 2 + core)).start()

    def quarter(half, index):
        return kvbuf.at[
            pl.ds(pl.multiple_of(half * half_keys + index * forward_block, forward_block), forward_block)
        ]

    some = chips // 2
    pltpu.make_async_copy(kv_send.at[chip % heads], kv_slot(0), recv.at[0]).start()
    send_keys(1, some, 0)
    later("keys 0 in", quarter(core, 0), recv.at[0])
    later("keys 0 out", kvbuf.at[pl.ds(0, (some - 1) * ROWS)], send.at[0])

    def head_device(head):
        return ((my_group // 2) * heads + head) * 2 + my_group % 2

    def to_heads(source, target, index, self_index):
        head = chip % heads
        slot = me % heads
        mine = head_device(head) == me

        @pl.when(mine)
        def _():
            pltpu.make_async_copy(source.at[head], target.at[slot], recv.at[index]).start()

        @pl.when(jnp.logical_not(mine))
        def _():
            remote(
                source.at[head], target.at[slot], send.at[self_index], recv.at[index], (z, head_device(head))
            ).start()

        @pl.loop(1, heads)
        def _(d):
            to = (chip + d) % heads
            remote(
                source.at[to], target.at[slot], send.at[index], recv.at[index], (z, head_device(to))
            ).start()

        def own_done():
            @pl.when(jnp.logical_not(mine))
            def _():
                drain(target.at[0], send.at[self_index])

        later(f"heads {index} in", target, recv.at[index])
        later(f"heads {index} out", target.at[pl.ds(0, heads - 1)], send.at[index])
        pending[f"heads {index} own"] = own_done

    to_heads(q_send, qpk, 1, 2)

    send_keys(some, chips, 22)
    later("keys 1 in", quarter(core, 1), recv.at[22])
    later("keys 1 out", kvbuf.at[pl.ds(0, some * ROWS)], send.at[22])

    len_recv[z] = len_send[...]

    @pl.loop(1, depth)
    def _(d):
        remote(len_send, len_recv.at[z], send.at[23], recv.at[23], ((z + d) % depth, me)).start()

    later("lengths in", len_recv.at[pl.ds(0, depth - 1)], recv.at[23])
    later("lengths out", len_recv.at[pl.ds(0, depth - 1)], send.at[23])

    after = (z, (me + 1) % seq)
    before = (z, (me + seq - 1) % seq)
    settle("x", "cot")
    halo_copies = (
        remote(x_ext.at[pl.ds(ROWS, HALO)], x_ext.at[pl.ds(0, HALO)], send.at[3], recv.at[3], after),
        remote(x_ext.at[pl.ds(HALO, HALO)], x_ext.at[pl.ds(HALO + ROWS, HALO)], send.at[4], recv.at[4], before),
        remote(cot_ext.at[pl.ds(ROWS, 16)], cot_ext.at[pl.ds(0, 16)], send.at[5], recv.at[5], after),
        remote(cot_ext.at[pl.ds(16, 16)], cot_ext.at[pl.ds(16 + ROWS, 16)], send.at[6], recv.at[6], before),
    )
    for index, copy in enumerate(halo_copies):
        copy.start()
        pending[f"halo {index} in"] = copy.wait_recv
        pending[f"halo {index} out"] = copy.wait_send

    def prepare_keys(half, index):
        rows_at_once = min(forward_block, 512)

        @pl.loop(0, forward_block // rows_at_once)
        def _(part):
            first = index * forward_block + part * rows_at_once
            rows = pl.ds(pl.multiple_of(half * half_keys + first, rows_at_once), rows_at_once)
            kv = kvbuf[rows].astype(F32)
            lane = lax.broadcasted_iota(jnp.int32, kv.shape, 1)
            row = lax.broadcasted_iota(jnp.int32, kv.shape, 0) + first
            source = chip - (row >> 7)
            source = jnp.where(source < 0, source + chips, source)
            frame = (source * 2 + half) * ROWS + (row & 127)
            bias = jnp.where(jnp.logical_and(lane == 64, frame >= length), NEGATIVE, 0.0)
            keyed = jnp.where(lane < 64, kv, bias)
            valued = jnp.where(lane < 64, 1.0, kv)
            k1[rows] = keyed.astype(BF16)
            v1[rows] = valued.astype(BF16)
            kt[:, rows] = jnp.transpose(kv)[:64].astype(BF16) * BF16(0.125)
            v1t[:, rows] = jnp.transpose(valued).astype(BF16)

    factor = 0.125 * 1.4426950408889634

    def block_rows(block):
        return pl.ds(pl.multiple_of(block * forward_block, forward_block), forward_block)

    def scores_step(part, block, highest):
        scores = dot(
            k1[block_rows(block)], qaug[part * query_block : (part + 1) * query_block], ((1,), (1,))
        )
        sbuf[part % 2, block_rows(block)] = scores
        return jnp.maximum(highest, jnp.max(scores.reshape(forward_block // 8, 8, query_block), axis=0))

    def weights_step(part, block, highest, total):
        rows = block_rows(block)
        weights = jnp.exp2((sbuf[part % 2, rows] - highest) * factor).astype(BF16)
        pt[rows, part * query_block : (part + 1) * query_block] = weights
        return total + dot(v1t[:, rows], weights)

    def context_finish(part, total):
        turned = jnp.transpose(total)
        low = low_lanes(turned.shape)
        inverse = 1.0 / jnp.where(low, 1.0, roll64(turned))
        context = jnp.where(low, 0.0, turned * inverse).astype(BF16).astype(F32)
        rows = slice(part * query_block, (part + 1) * query_block)
        linv[rows] = inverse
        ctxh[rows] = context
        half_rows = slice(part * query_block // 2, (part + 1) * query_block // 2)
        ctx_send[half_rows] = pack_high(context).astype(BF16)

    high = jnp.full((8, query_block), NEGATIVE, F32)
    for index in range(2):
        settle(f"keys {index} in")
        forward = remote(
            quarter(core, index), quarter(core, index), send.at[7 + 17 * index], recv.at[7 + 17 * index], partner
        )
        forward.start()
        later(f"forward {index} in", quarter(other, index), recv.at[7 + 17 * index])
        pending[f"forward {index} out"] = forward.wait_send
        prepare_keys(core, index)
        if index == 0:
            settle("heads 1 in")
            for slot in range(heads):
                rows = slice(ROWS * slot, ROWS * slot + ROWS)
                part = unpack_low(qpk[slot].astype(F32))
                lane = lax.broadcasted_iota(jnp.int32, part.shape, 1)
                qcl[rows] = (part * 0.125).astype(BF16)
                qaug[rows] = jnp.where(lane == 64, 1.0, part).astype(BF16)
        high = scores_step(0, core * 2 + index, high)
    for index in range(2):
        settle(f"forward {index} in")
        prepare_keys(other, index)
        high = scores_step(0, other * 2 + index, high)

    start_high = jnp.full((8, query_block), NEGATIVE, F32)
    start_total = jnp.zeros((128, query_block), F32)
    for part in range(query_blocks):
        highest = jnp.max(high, axis=0, keepdims=True)
        if part + 1 < query_blocks:

            def both(b, carried, part=part, highest=highest):
                h, t = carried
                return scores_step(part + 1, b, h), weights_step(part, b, highest, t)

            high, total = lax.fori_loop(0, 4, both, (start_high, start_total))
        else:
            total = lax.fori_loop(
                0, 4, lambda b, t, part=part, highest=highest: weights_step(part, b, highest, t), start_total
            )
        context_finish(part, total)

    my_head = chip % heads
    moves = [(-1, 0, 16, 80), (0, 0, 80, 16)]
    moves += [(i, 64 * i - 16, 96, 0) for i in range(1, heads - 1)]
    moves += [(heads - 1, 64 * (heads - 1) - 16, 80, 0), (heads, 64 * heads - 16, 16, 0)]

    def owner_of(i):
        return (group * heads + i + seq) % seq

    for index, (i, start, count, to) in enumerate(moves):
        source = ctx_send.at[pl.ds(start, count)]
        target = ctx_recv.at[my_head, pl.ds(to, count)]

        @pl.when(owner_of(i) == me)
        def _(source=source, target=target):
            pltpu.make_async_copy(source, target, recv.at[8]).start()

        @pl.when(owner_of(i) != me)
        def _(source=source, target=target, i=i, index=index):
            remote(source, target, ctx_sem.at[index], recv.at[8], (z, owner_of(i))).start()

        def sent(source=source, i=i, index=index):
            @pl.when(owner_of(i) != me)
            def _():
                drain(source, ctx_sem.at[index])

        pending[f"context {index}"] = sent

    def live(rows, first):
        frame = me * ROWS + first + lax.broadcasted_iota(jnp.int32, (rows, 128), 0)
        return jnp.logical_and(frame >= 0, frame < length)

    def column(chunk):
        return pl.ds(pl.multiple_of(chunk * 128, 128), 128)

    def turned_convolution(rows, columns):
        total = jnp.zeros((ROWS, 128), F32)
        for low in range(8):
            moved = shifted(rows, low)
            for high_part in range(4):
                tap = 31 - (8 * high_part + low)
                if 0 <= tap < KERNEL:
                    total = total + taps_ref[tap : tap + 1, columns] * moved[8 * high_part : 8 * high_part + ROWS]
        return total

    settle("w", "taps", "gain", "shift")

    @pl.loop(0, chunks)
    def _(chunk):
        columns = column(chunk)
        cmask_ref[:, columns] = turned_convolution(jnp.where(live(mid, -16), 1.0, 0.0), columns)

    settle("lengths in")
    lengths = len_recv[:, :1]
    count_a[...] = jnp.clip(lengths - (me * ROWS).astype(F32), 0.0, float(ROWS))
    for i in range(seq):
        count_b[i] = jnp.sum(jnp.clip(lengths - float(i * ROWS), 0.0, float(ROWS)), axis=0)
    for target in (tmask_ref, tgrad_ref, tnorm_ref):
        target[KERNEL:] = jnp.zeros((1, channels), F32)

    settle(*(f"halo {index} in" for index in range(4)))
    drain(ctx_recv, recv.at[8])

    for pair in range(heads // 2):
        ctx_ref[:, 128 * pair : 128 * pair + 128] = unpack_pair(
            ctx_recv[2 * pair].astype(F32), ctx_recv[2 * pair + 1].astype(F32)
        ).astype(BF16)

    counted = jnp.clip(length - me * ROWS, 0, ROWS).astype(F32)

    @pl.loop(0, channels // 256)
    def _(chunk):
        columns = pl.ds(pl.multiple_of(chunk * 256, 256), 256)
        hidden = x_ext[:, columns].astype(F32) + dot(ctx_ref[...], w_ref[:, columns])
        mask = live(ext, -HALO)
        mask = jnp.concatenate([mask, mask], axis=1)
        hid_ref[:, columns] = jnp.where(mask, hidden, 0.0).astype(BF16).astype(F32)

    @pl.loop(0, chunks)
    def _(chunk):
        columns = column(chunk)
        hidden = hid_ref[:, columns]
        total = jnp.zeros((mid, 128), F32)
        for low in range(8):
            moved = shifted(hidden, low)
            for high_part in range(4):
                tap = 8 * high_part + low - 1
                if 0 <= tap < KERNEL:
                    total = total + taps_ref[tap : tap + 1, columns] * moved[8 * high_part : 8 * high_part + mid]
        conv_ref[:, columns] = total
        own = total[16 : 16 + ROWS]
        mask = live(ROWS, 0)
        summed = jnp.sum(jnp.where(mask, own, 0.0), axis=0, keepdims=True)
        mean = summed / jnp.maximum(counted, 1.0)
        spread = own - mean
        squares = jnp.sum(jnp.where(mask, spread * spread, 0.0), axis=0, keepdims=True)
        stat_a[pl.ds(chunk, 1)] = summed
        stat_a[pl.ds(chunks + chunk, 1)] = squares


    def write(source, target, index):
        copy = pltpu.make_async_copy(source, target, write_sem.at[index])
        copy.start()
        pending[f"write {index}"] = copy.wait

    def gather(source, target, index, slot, count, peer, beside):
        target[slot] = source[...]

        around(
            count,
            lambda d: remote(source, target.at[slot], send.at[index], recv.at[index], peer(d)).start(),
        )

        later(f"sums {index}", target.at[pl.ds(0, count - 1)], send.at[index])
        if beside is not None:
            beside()
        drain(target.at[pl.ds(0, count - 1)], recv.at[index])

    def gather_first(source, target, index, beside=None):
        gather(source, target, index, z, depth, lambda d: ((z + d) % depth, me), beside)

    def gather_second(source, target, index, beside=None):
        gather(source, target, index, me, seq, lambda d: (z, (me + d) % seq), beside)

    def correlate(target, rows, columns):
        hidden = hid_ref[16:, columns]
        for low in range(8):
            moved = shifted(hidden, low)
            for high_part in range(4):
                tap = 8 * high_part + low - 1
                if 0 <= tap < KERNEL:
                    terms = rows * moved[8 * high_part : 8 * high_part + ROWS]
                    target[tap : tap + 1, columns] = jnp.sum(terms, axis=0, keepdims=True)

    def correlate_mask():
        own_ctx[...] = jnp.transpose(ctx_ref[HALO : HALO + ROWS].astype(F32)).astype(BF16)

        @pl.loop(0, chunks)
        def _(chunk):
            correlate(tmask_ref, jnp.where(live(ROWS, 0), 1.0, 0.0), column(chunk))

    def correlate_rest():
        @pl.loop(0, chunks)
        def _(chunk):
            columns = column(chunk)
            own = slice(16, 16 + ROWS)
            correlate(tgrad_ref, ga_ref[own, columns], columns)
            correlate(tnorm_ref, jnp.where(live(ROWS, 0), conv_ref[own, columns], 0.0), columns)

    def merged(gathered, counts):
        sums = gathered[:, :chunks]
        squares = gathered[:, chunks:]
        count = jnp.sum(counts, axis=0)
        total = jnp.sum(sums, axis=0)
        mean = total / jnp.maximum(count, 1.0)
        shift = sums / jnp.maximum(counts, 1.0) - mean[None]
        return total, jnp.sum(squares, axis=0) + jnp.sum(counts * shift * shift, axis=0), count, mean

    gather_first(stat_a, recv_a, 9, correlate_mask)
    total, squares, count, mean = merged(recv_a[...], count_a[...])
    stat_b[:chunks] = total
    stat_b[chunks:] = squares
    gather_second(stat_b, recv_b, 10)
    total, squares, count, mean = merged(recv_b[...], count_b[...])
    tot_ref[:chunks] = mean
    tot_ref[chunks : 2 * chunks] = lax.rsqrt(squares / count + EPSILON)
    tot_ref[2 * chunks : 3 * chunks] = jnp.broadcast_to(1.0 / count, (chunks, 128))

    @pl.loop(0, chunks)
    def _(chunk):
        columns = column(chunk)
        mean = tot_ref[pl.ds(chunk, 1)]
        inverse = tot_ref[pl.ds(chunks + chunk, 1)]
        normed = (conv_ref[:, columns] - mean) * inverse
        conv_ref[:, columns] = normed
        act = normed * gain_ref[:, columns] + shift_ref[:, columns]
        gate = 1.0 / (1.0 + jnp.exp(-act))
        grad_out = jnp.where(live(mid, -16), cot_ext[:, columns].astype(F32), 0.0)
        grad_act = grad_out * gate * (1.0 + act * (1.0 - gate))
        ga_ref[:, columns] = grad_act
        own = grad_act[16 : 16 + ROWS]
        stat_c[pl.ds(chunk, 1)] = jnp.sum(own * normed[16 : 16 + ROWS], axis=0, keepdims=True)
        stat_c[pl.ds(chunks + chunk, 1)] = jnp.sum(own, axis=0, keepdims=True)
        gated = (act * gate)[16 : 16 + ROWS]
        hidden = hid_ref[HALO : HALO + ROWS, columns]
        out_ref[:, columns] = jnp.where(live(ROWS, 0), hidden + gated, 0.0).astype(BF16)

    def beside():
        write(out_ref, out_hbm, 0)

        @pl.loop(0, chunks)
        def _(chunk):
            columns = column(chunk)
            cgrad_ref[:, columns] = turned_convolution(ga_ref[:, columns], columns)
            cnorm_ref[:, columns] = turned_convolution(
                jnp.where(live(mid, -16), conv_ref[:, columns], 0.0), columns
            )

    gather_first(stat_c, recv_c, 11, beside)
    stat_d[...] = jnp.sum(recv_c[...], axis=0)
    gather_second(stat_d, recv_d, 12, correlate_rest)
    sums_ref[...] = jnp.sum(recv_d[...], axis=0)

    @pl.loop(0, chunks)
    def _(chunk):
        columns = column(chunk)
        inverse = tot_ref[pl.ds(chunks + chunk, 1)]
        per_count = tot_ref[pl.ds(2 * chunks + chunk, 1)]
        gain_sum = sums_ref[pl.ds(chunk, 1)] * per_count
        shift_sum = sums_ref[pl.ds(chunks + chunk, 1)] * per_count
        scale = inverse * gain_ref[:, columns]
        turned = cgrad_ref[:, columns] - shift_sum * cmask_ref[:, columns] - gain_sum * cnorm_ref[:, columns]
        total = cot_ext[16 : 16 + ROWS, columns].astype(F32) + scale * turned
        ginp_ref[:, columns] = jnp.where(live(ROWS, 0), total, 0.0).astype(BF16)

    write(ginp_ref, ginp_hbm, 1)

    def stage0(piece):
        copy = remote(
            wsend.at[piece].at[other], g0.at[piece], piece_send.at[5 * piece + 0], piece_recv.at[5 * piece + 0], partner
        )
        copy.start()
        pending[f"stage 0 in {piece}"] = copy.wait_recv
        pending[f"stage 0 out {piece}"] = copy.wait_send

    for piece in range(PIECES):
        first = piece * piece_width
        size = min(piece_width, channels - first)
        if size > 0:
            terms = dot(own_ctx[...], ginp_ref[:, first : first + size]).astype(BF16)
            wsend.at[piece][:, :, :, :size] = terms.reshape(2, chips, 16, size)
        if piece < PIECES - 1:
            stage0(piece)

    tap_lanes = slice(piece_width - 128, piece_width)
    wsend[PIECES - 1, :, :, :, tap_lanes] = jnp.zeros((2, chips, 16, 128), BF16)

    @pl.loop(0, chunks)
    def _(chunk):
        columns = column(chunk)
        per_count = tot_ref[pl.ds(2 * chunks + chunk, 1)]
        gain_sum = sums_ref[pl.ds(chunk, 1)] * per_count
        shift_sum = sums_ref[pl.ds(chunks + chunk, 1)] * per_count
        scale = tot_ref[pl.ds(chunks + chunk, 1)] * gain_ref[:, columns]
        stacked = tgrad_ref[:, columns] - shift_sum * tmask_ref[:, columns] - gain_sum * tnorm_ref[:, columns]
        stacked = (scale * stacked).astype(BF16)
        wsend.at[PIECES - 1].at[0][pl.ds(chunk, 1), :, tap_lanes] = stacked[:16].reshape(1, 16, 128)
        wsend.at[PIECES - 1].at[1][pl.ds(chunk, 1), :, tap_lanes] = stacked[16:].reshape(1, 16, 128)

    stage0(PIECES - 1)

    @pl.loop(0, heads // 2)
    def _(pair):
        rows = pl.ds(pl.multiple_of(pair * 128, 128), 128)
        grad_context = dot(ginp_ref[...], w_ref[rows], ((1,), (1,))).astype(BF16).astype(F32)
        even, odd = pack_pair(grad_context)
        do_send[2 * pair] = even.astype(BF16)
        do_send[2 * pair + 1] = odd.astype(BF16)

    to_heads(do_send, do_recv, 13, 14)

    def stage1(piece):
        settle(f"stage 0 in {piece}")

        total = wsend.at[piece].at[core][...].astype(F32) + g0[piece].astype(F32)
        gs1[piece] = total.astype(BF16)
        g1.at[piece].at[chip][...] = gs1.at[piece].at[chip][...]

        @pl.loop(1, chips)
        def _(d):
            peer = (chip + d) % chips
            remote(
                gs1.at[piece].at[peer],
                g1.at[piece].at[chip],
                piece_send.at[5 * piece + 1],
                piece_recv.at[5 * piece + 1],
                (z, peer * 2 + core),
            ).start()

        later(f"stage 1 in {piece}", g1.at[piece].at[pl.ds(0, chips - 1)], piece_recv.at[5 * piece + 1])
        later(f"stage 1 out {piece}", g1.at[piece].at[pl.ds(0, chips - 1)], piece_send.at[5 * piece + 1])

    def stage2(piece):
        settle(f"stage 1 in {piece}")
        total = g1.at[piece][0].astype(F32)
        for i in range(1, chips):
            total = total + g1.at[piece][i].astype(F32)
        total = total.astype(BF16)
        gs2[piece] = total
        g2.at[piece].at[z][...] = total

        @pl.loop(1, depth)
        def _(d):
            remote(
                gs2.at[piece],
                g2.at[piece].at[z],
                piece_send.at[5 * piece + 2],
                piece_recv.at[5 * piece + 2],
                ((z + d) % depth, me),
            ).start()

        pending[f"stage 2 in {piece}"] = lambda: drain(
            g2.at[piece].at[pl.ds(0, depth - 1)], piece_recv.at[5 * piece + 2]
        )
        pending[f"stage 2 out {piece}"] = lambda: drain(
            g2.at[piece].at[pl.ds(0, depth - 1)], piece_send.at[5 * piece + 2]
        )

    def stage3(piece):
        settle(f"stage 2 in {piece}")
        total = g2.at[piece][0].astype(F32)
        for i in range(1, depth):
            total = total + g2.at[piece][i].astype(F32)
        gfin_ref.at[piece].at[core, chip][...] = total.astype(BF16)
        final = gfin_ref.at[piece].at[core, chip]

        @pl.loop(1, chips)
        def _(d):
            peer = (chip + d) % chips
            remote(
                final, final, piece_send.at[5 * piece + 3], piece_recv.at[5 * piece + 3], (z, peer * 2 + core)
            ).start()

        size = gfin_ref.at[piece].at[core, pl.ds(0, chips - 1)]
        later(f"stage 3 in {piece}", size, piece_recv.at[5 * piece + 3])
        later(f"stage 3 out {piece}", size, piece_send.at[5 * piece + 3])

    def stage4(piece):
        settle(f"stage 3 in {piece}")
        finals = gfin_ref.at[piece].at[core]
        copy = remote(finals, finals, piece_send.at[5 * piece + 4], piece_recv.at[5 * piece + 4], partner)
        copy.start()
        later(f"stage 4 in {piece}", gfin_ref.at[piece].at[other], piece_recv.at[5 * piece + 4])
        pending[f"stage 4 out {piece}"] = copy.wait_send

    for piece in range(PIECES):
        stage1(piece)

    settle("heads 13 in")
    for index in range(heads):
        rows = slice(ROWS * index, ROWS * index + ROWS)
        scaled = (unpack_high(do_recv[index].astype(F32)) * linv[rows]).astype(BF16)
        docl[rows] = scaled
        scaled = scaled.astype(F32)
        delta = jnp.sum(ctxh[rows] * scaled, axis=1, keepdims=True)
        first = delta.astype(BF16).astype(F32)
        rest = delta - first
        lane = lax.broadcasted_iota(jnp.int32, scaled.shape, 1)
        doaug[rows] = jnp.where(lane == 0, -first, jnp.where(lane == 1, -rest, scaled)).astype(BF16)

    dqt[...] = jnp.zeros_like(dqt)

    def part_copy(turn):
        rows = pl.ds(pl.multiple_of(turn * backward_block, backward_block), backward_block)
        return remote(dsend.at[rows], precv.at[rows], part_send.at[turn], part_recv.at[turn], partner)

    turns = 4
    slots = backward_block // ROWS

    @pl.loop(0, 2 * turns)
    def _(step):
        half = jnp.where(step < turns, other, core)
        turn = step % turns
        rows = pl.ds(
            pl.multiple_of(half * half_keys + turn * backward_block, backward_block), backward_block
        )
        turn_rows = pl.ds(pl.multiple_of(turn * backward_block, backward_block), backward_block)
        weights = pt[rows]
        grads = dot(v1[rows], doaug[...], ((1,), (1,))).astype(BF16)
        scores = weights * grads
        dqt[...] += dot(kt[:, rows], scores)
        rbuf[...] = dot(scores, qcl[...]) + dot(weights, docl[...])

        @pl.when(step < turns)
        def _():
            dsend[turn_rows] = rbuf[...].astype(BF16)
            part_copy(turn).start()

        @pl.when(step >= turns)
        def _():
            part_copy(turn).wait_recv()
            osend[turn_rows] = (rbuf[...] + precv[turn_rows].astype(F32)).astype(BF16)
            for i in range(slots):
                slot = turn * slots + i
                owner = (chip + chips - slot) % chips
                source = osend.at[pl.ds(pl.multiple_of(slot * ROWS, ROWS), ROWS)]

                def give(source=source, owner=owner):
                    remote(source, kvrecv.at[chip], own_sem, recv.at[20], (z, owner * 2 + core)).start()

                if i == 0:

                    @pl.when(turn == 0)
                    def _(source=source):
                        pltpu.make_async_copy(source, kvrecv.at[chip], recv.at[20]).start()

                    pl.when(turn > 0)(give)
                else:
                    give()

        for piece in range(PIECES):

            @pl.when(step == 3 + piece)
            def _(piece=piece):
                stage2(piece)

    def parts_sent():
        @pl.loop(0, turns)
        def _(turn):
            part_copy(turn).wait_send()

    pending["parts"] = parts_sent
    later("owned in", kvrecv, recv.at[20])
    later("owned out", kvrecv.at[pl.ds(0, chips - 1)], own_sem)

    @pl.loop(0, query_blocks)
    def _(block):
        part = pl.ds(pl.multiple_of(block * query_block, query_block), query_block)
        turned = dqt[:, part]
        turned = jnp.transpose(jnp.concatenate([turned, jnp.zeros_like(turned)], axis=0))
        half_part = pl.ds(pl.multiple_of(block * query_block // 2, query_block // 2), query_block // 2)
        dq_send[half_part] = pack_low(turned).astype(BF16)

    for i in range(heads):
        source = dq_send.at[pl.ds(64 * i, 64)]
        target = dq_recv.at[my_head]

        @pl.when(owner_of(i) == me)
        def _(source=source, target=target):
            pltpu.make_async_copy(source, target, recv.at[21]).start()

        @pl.when(owner_of(i) != me)
        def _(source=source, target=target, i=i):
            remote(source, target, dq_sem.at[i], recv.at[21], (z, owner_of(i))).start()

        def sent(source=source, i=i):
            @pl.when(owner_of(i) != me)
            def _():
                drain(source, dq_sem.at[i])

        pending[f"grad query {i}"] = sent

    for piece in range(PIECES):
        stage3(piece)

    settle("owned in")
    for pair in range(heads // 2):
        columns = slice(128 * pair, 128 * pair + 128)
        even = kvrecv[2 * pair].astype(F32) + kvrecv[2 * pair + heads].astype(F32)
        odd = kvrecv[2 * pair + 1].astype(F32) + kvrecv[2 * pair + 1 + heads].astype(F32)
        low = low_lanes(even.shape)
        gk_ref[:, columns] = jnp.where(low, even, roll64(odd)).astype(BF16)
        gv_ref[:, columns] = jnp.where(low, roll64(even), odd).astype(BF16)
    write(gk_ref, gk_hbm, 3)
    write(gv_ref, gv_hbm, 4)

    drain(dq_recv, recv.at[21])
    for pair in range(heads // 2):
        gq_ref[:, 128 * pair : 128 * pair + 128] = unpack_pair(
            dq_recv[2 * pair].astype(F32), dq_recv[2 * pair + 1].astype(F32)
        ).astype(BF16)

    write(gq_ref, gq_hbm, 2)
    for piece in range(PIECES):
        stage4(piece)
    settle()


def finish(width, chunks, *refs):
    sources = refs[:7]
    outs = refs[7:16]
    out, ginp, gq, gk, gv, packed, sums = refs[16:23]
    weights, taps, load_sem, sem = refs[23:]
    channels = weights.shape[1]
    loads = [
        pltpu.make_async_copy(source, target, load_sem.at[index])
        for index, (source, target) in enumerate(zip(sources, refs[16:23]))
    ]
    for index in (5, 6, 0, 1, 2, 3, 4):
        loads[index].start()
    copies = [
        pltpu.make_async_copy(source, target, sem.at[index])
        for index, (source, target) in enumerate(
            (
                (out, outs[0]),
                (ginp, outs[1]),
                (gq, outs[2]),
                (gk, outs[3]),
                (gv, outs[4]),
                (weights, outs[5]),
                (taps, outs[6]),
                (sums.at[pl.ds(0, chunks)], outs[7]),
                (sums.at[pl.ds(chunks, chunks)], outs[8]),
            )
        )
    ]
    loads[5].wait()
    piece_width = packed.shape[-1]
    for piece in range(PIECES):
        first = piece * piece_width
        size = min(piece_width, channels - first)
        for half in range(2 if size > 0 else 0):
            rows = slice(half * width // 2, (half + 1) * width // 2)
            terms = packed[piece, half, :, :, :size].astype(F32)
            weights[rows, first : first + size] = terms.reshape(width // 2, size)
    for chunk in range(chunks):
        lanes = slice(piece_width - 128, piece_width)
        columns = slice(128 * chunk, 128 * chunk + 128)
        taps[:16, columns] = packed[PIECES - 1, 0, chunk, :, lanes].astype(F32)
        taps[16:, columns] = packed[PIECES - 1, 1, chunk, :15, lanes].astype(F32)
    copies[5].start()
    copies[6].start()
    loads[6].wait()
    copies[7].start()
    copies[8].start()
    for index in range(5):
        loads[index].wait()
        copies[index].start()
    for copy in copies:
        copy.wait()


def shards(
    depth,
    query_rows,
    key_rows,
    value_rows,
    inputs,
    lengths,
    out_weight,
    taps,
    norm_gain,
    norm_shift,
    cotangent,
):
    seq = lax.axis_size("seq")
    heads = seq // 4
    chips = seq // 2
    width = query_rows.shape[2]
    channels = inputs.shape[2]
    chunks = channels // 128
    queries = ROWS * heads
    keys = seq * ROWS
    ext = ROWS + 2 * HALO
    mid = ROWS + 32
    padded = channels + 128
    piece_width = padded // PIECES
    query_block = min(queries, 512)
    vmem = pltpu.VMEM
    scratch = [
        vmem((ROWS, width), BF16),
        vmem((ROWS, width), BF16),
        vmem((ROWS, width), BF16),
        vmem((1, channels), F32),
        vmem((1, channels), F32),
        vmem((ROWS, channels), BF16),
        vmem((ROWS, channels), BF16),
        vmem((ROWS, width), BF16),
        vmem((ROWS, width), BF16),
        vmem((ROWS, width), BF16),
        vmem((8, 128), F32),
        vmem((depth, 8, 128), F32),
        vmem((ROWS, channels), F32),
        vmem((ROWS, channels), F32),
        vmem((ROWS, channels), F32),
        vmem((width, ROWS), BF16),
        vmem((KERNEL + 1, channels), F32),
        vmem((KERNEL + 1, channels), F32),
        vmem((KERNEL + 1, channels), F32),
        vmem((depth, 1, 128), F32),
        vmem((seq, 1, 128), F32),
        vmem((heads, ROWS, 128), BF16),
        vmem((heads, 64, 128), BF16),
        vmem((keys, 128), BF16),
        vmem((heads, 64, 128), BF16),
        vmem((keys, 128), BF16),
        vmem((keys, 128), BF16),
        vmem((64, keys), BF16),
        vmem((128, keys), BF16),
        vmem((queries, 128), BF16),
        vmem((queries, 128), BF16),
        vmem((2, keys, query_block), F32),
        vmem((keys, queries), BF16),
        vmem((queries, 128), F32),
        vmem((queries, 128), F32),
        vmem((queries // 2, 128), BF16),
        vmem((heads, ext // 2, 128), BF16),
        vmem((ext, channels), BF16),
        vmem((mid, channels), BF16),
        vmem((width, channels), BF16),
        vmem((KERNEL, channels), F32),
        vmem((ext, width), BF16),
        vmem((ext, channels), F32),
        vmem((mid, channels), F32),
        vmem((mid, channels), F32),
        vmem((2 * chunks, 128), F32),
        vmem((2 * chunks, 128), F32),
        vmem((depth, 2 * chunks, 128), F32),
        vmem((seq, 2 * chunks, 128), F32),
        vmem((2 * chunks, 128), F32),
        vmem((depth, 2 * chunks, 128), F32),
        vmem((2 * chunks, 128), F32),
        vmem((seq, 2 * chunks, 128), F32),
        vmem((3 * chunks, 128), F32),
        vmem((heads, 64, 128), BF16),
        vmem((heads, 64, 128), BF16),
        vmem((queries, 128), BF16),
        vmem((queries, 128), BF16),
        vmem((keys // 8, 128), F32),
        vmem((64, queries), F32),
        vmem((keys // 2, 128), BF16),
        vmem((keys // 2, 128), BF16),
        vmem((keys // 2, 128), BF16),
        vmem((chips, ROWS, 128), BF16),
        vmem((queries // 2, 128), BF16),
        vmem((heads, 64, 128), BF16),
        vmem((PIECES, 2, chips, 16, piece_width), BF16),
        vmem((PIECES, chips, 16, piece_width), BF16),
        vmem((PIECES, chips, 16, piece_width), BF16),
        vmem((PIECES, chips, 16, piece_width), BF16),
        vmem((PIECES, 16, piece_width), BF16),
        vmem((PIECES, depth, 16, piece_width), BF16),
        pltpu.SemaphoreType.DMA((9,)),
        pltpu.SemaphoreType.DMA((25,)),
        pltpu.SemaphoreType.DMA((25,)),
        pltpu.SemaphoreType.DMA((heads + 2,)),
        pltpu.SemaphoreType.DMA((heads,)),
        pltpu.SemaphoreType.DMA((4,)),
        pltpu.SemaphoreType.DMA((4,)),
        pltpu.SemaphoreType.DMA,
        pltpu.SemaphoreType.DMA((5 * PIECES,)),
        pltpu.SemaphoreType.DMA((5 * PIECES,)),
        pltpu.SemaphoreType.DMA((5,)),
    ]
    in_vmem = pl.BlockSpec(memory_space=pltpu.VMEM)
    anywhere = pl.BlockSpec(memory_space=pl.ANY)
    plain = (
        jax.ShapeDtypeStruct((ROWS, channels), BF16),
        jax.ShapeDtypeStruct((ROWS, channels), BF16),
        jax.ShapeDtypeStruct((ROWS, width), BF16),
        jax.ShapeDtypeStruct((ROWS, width), BF16),
        jax.ShapeDtypeStruct((ROWS, width), BF16),
    )
    results = pl.pallas_call(
        functools.partial(kernel, heads, seq, depth),
        out_shape=plain
        + (
            jax.ShapeDtypeStruct((PIECES, 2, chips, 16, piece_width), BF16),
            jax.ShapeDtypeStruct((2 * chunks, 128), F32),
        ),
        in_specs=[pl.BlockSpec(memory_space=pltpu.SMEM)] + [anywhere] * 9,
        out_specs=(anywhere,) * 5 + (in_vmem,) * 2,
        scratch_shapes=scratch,
        compiler_params=pltpu.CompilerParams(
            collective_id=0, has_side_effects=True, vmem_limit_bytes=60 * 1024 * 1024
        ),
    )(
        lengths,
        query_rows[0],
        key_rows[0],
        value_rows[0],
        inputs[0],
        cotangent[0],
        out_weight,
        taps,
        norm_gain[None],
        norm_shift[None],
    )
    final = pl.pallas_call(
        functools.partial(finish, width, chunks),
        out_shape=plain
        + (
            jax.ShapeDtypeStruct((width, channels), F32),
            jax.ShapeDtypeStruct((KERNEL, channels), F32),
            jax.ShapeDtypeStruct((chunks, 128), F32),
            jax.ShapeDtypeStruct((chunks, 128), F32),
        ),
        in_specs=[anywhere] * 7,
        out_specs=(anywhere,) * 9,
        scratch_shapes=[vmem(array.shape, array.dtype) for array in results]
        + [
            vmem((width, channels), F32),
            vmem((KERNEL, channels), F32),
            pltpu.SemaphoreType.DMA((7,)),
            pltpu.SemaphoreType.DMA((9,)),
        ],
        compiler_params=pltpu.CompilerParams(vmem_limit_bytes=60 * 1024 * 1024),
    )(*results)
    return (
        *(array[None] for array in final[:5]),
        final[5],
        final[6],
        final[7].reshape(channels),
        final[8].reshape(channels),
    )


def solution(mesh):
    rows = P("dp", "seq", None)
    return jax.shard_map(
        functools.partial(shards, mesh.shape["dp"]),
        mesh=mesh,
        in_specs=(rows, rows, rows, rows, P("dp"), P(), P(), P(), P(), rows),
        out_specs=(rows, rows, rows, rows, rows, P(), P(), P(), P()),
        check_vma=False,
    )
```
